128 devices in a mesh: seq: 8 (over z, core), head: 8 (over x_hi, y), batch: 2 (over x_lo).
Axes of the slice: x: 4 (x_hi: 2, x_lo: 2; x = x_hi * 2 + x_lo), y: 4, z: 4, core: 2. Of those that a mesh axis runs over, the one named last changes fastest.
Arguments:
- tokens: bfloat16 [16384, 2048], P(('batch', 'seq')), parts along dimension 0, may hold values from -256 to 256
- w_shared: bfloat16 [2048, 2048], P(None, 'head'), may hold values from -0.125 to 0.125
- w_value: bfloat16 [2048, 2048], P(None, 'head'), may hold values from -0.125 to 0.125
- w_output: bfloat16 [2048, 2048], P('head'), may hold values from -0.125 to 0.125
- doc_length: int32 [2], P('batch'), parts along dimension 0, may hold values from 2048 to 8192
Outputs:
- attended: bfloat16 [16384, 2048], P(('batch', 'seq'), 'head'), parts along dimension 0
The draws below stay inside these ranges and needn't reach their ends.
There are 2 independent parts, one for each index of `batch`. The reference program is written for one: setup_inputs(seed, part) draws one part's arguments, and reference() takes and returns one part's arrays. A program takes and returns all parts, laid end to end along the dimension named above; an argument that names none is the same for every part. Nothing has to cross between parts.
All inputs are finite; a program needn't handle non-finite values.
Results may differ from the reference program's by a relative error of at most 0.018.
Values may be sent and summed in bfloat16 or wider, within the bound.
No kernel may reach another device: no remote copies, remote signals or barrier semaphores. Data moves between devices by JAX's collectives and lax.ppermute only.
A program may use at most 192 MiB of HBM per device.

```python
import math
import jax
import jax.numpy as jnp
from jax import lax

D = 2048
HEADS = 16
HEAD_DIM = 128
SEQ = 8192
N_SEQ = 8


def draw_tokens(key, part):
    key = jax.random.fold_in(key, 7)
    key_rows = jax.random.fold_in(key, 0)
    key_center = jax.random.fold_in(key, 2)
    key_member = jax.random.fold_in(key, 3)
    groups = max(SEQ // 32, 2)
    centers = jnp.clip(jax.random.normal(key_center, (groups, D), jnp.float32), -6.0, 6.0)
    member = jax.random.randint(key_member, (SEQ,), 0, groups)
    noise_rows = jnp.clip(jax.random.normal(key_rows, (SEQ, D), jnp.float32), -6.0, 6.0)
    base = 0.75 * centers[member] + 0.65 * noise_rows
    return base.astype(jnp.bfloat16)


def level_of(stream_key, shape, cuts, least, high):
    def one(axis_at, parts):
        steps = jax.random.uniform(jax.random.fold_in(jax.random.fold_in(stream_key, 6), axis_at), (parts,), jnp.float32, least / len(cuts), high / len(cuts))
        return jnp.repeat(jnp.exp(steps), shape[axis_at] // parts).reshape((-1,) + (1,) * (len(shape) - axis_at - 1))

    factor_of = one(*cuts[0])
    for cut in cuts[1:]:
        factor_of = factor_of * one(*cut)
    return factor_of


def scatter_about(key, extent, scale, limit, cuts=(), held_as=jnp.bfloat16):
    values = jax.random.normal(key, extent, jnp.float32) * scale
    if len(cuts) > 0:
        values = level_of(key, extent, cuts, -0.22, 0.18) * values
    return jnp.clip(values, min=-limit, max=limit).astype(held_as)


def setup_inputs(seed: int = 0, part: int = 0) -> dict:
    key_list = jax.random.split(jax.random.key(seed), 6)
    part_keys = jax.random.split(jax.random.fold_in(key_list[5], part), 6)
    tokens = draw_tokens(jax.random.fold_in(jax.random.fold_in(key_list[5], part), 71), part)
    w_shared = scatter_about(key_list[1], (D, HEADS * HEAD_DIM), D ** -0.5, 0.125, ((1, 8),))
    w_value = scatter_about(key_list[2], (D, HEADS * HEAD_DIM), D ** -0.5, 0.125, ((1, 8),))
    w_output = scatter_about(key_list[3], (HEADS * HEAD_DIM, D), (HEADS * HEAD_DIM) ** -0.5, 0.125, ((0, 8),))
    doc_length = jax.random.randint(part_keys[4], (1,), SEQ // 4, SEQ + 1).astype(jnp.int32)
    return {"tokens": tokens, "w_shared": w_shared, "w_value": w_value, "w_output": w_output, "doc_length": doc_length}


def reference(tokens, w_shared, w_value, w_output, doc_length):
    full_rows = tokens.shape[0]
    shared = jnp.dot(tokens, w_shared, preferred_element_type=jnp.float32).astype(jnp.bfloat16)
    values = jnp.dot(tokens, w_value, preferred_element_type=jnp.float32).astype(jnp.bfloat16)
    shared3 = shared.reshape(full_rows, HEADS, HEAD_DIM)
    values3 = values.reshape(full_rows, HEADS, HEAD_DIM)
    wide = shared3.astype(jnp.float32)
    factor = lax.rsqrt(lax.optimization_barrier(jnp.mean(wide * wide, axis=-1)) + 1e-06) / math.sqrt(HEAD_DIM)
    positions = jnp.arange(full_rows, dtype=jnp.int32)
    key_valid = positions < doc_length[0]
    block_rows = full_rows // N_SEQ

    def head_fn(head_index):
        head_keys = lax.dynamic_index_in_dim(shared3, head_index, 1, keepdims=False)
        head_vals = lax.dynamic_index_in_dim(values3, head_index, 1, keepdims=False)
        head_fac = lax.dynamic_index_in_dim(factor, head_index, 1, keepdims=False)

        def query_fn(block_index):
            query_first = (block_index * block_rows).astype(jnp.int32)
            queries = lax.dynamic_slice_in_dim(head_keys, query_first, block_rows, 0)
            query_pos = query_first + jnp.arange(block_rows, dtype=jnp.int32)
            allowed = key_valid[None, :] & (positions[None, :] != query_pos[:, None])
            scores = jnp.dot(queries, head_keys.T, preferred_element_type=jnp.float32) * head_fac[None, :]
            scores = jnp.where(allowed, scores, -1e+30)
            peak = lax.optimization_barrier(jnp.max(scores, axis=-1, keepdims=True))
            unnorm = jnp.where(allowed, jnp.exp(scores - peak), 0.0)
            weight_sum = lax.optimization_barrier(jnp.sum(unnorm, axis=-1, keepdims=True))
            mixed = jnp.dot(unnorm.astype(jnp.bfloat16), head_vals, preferred_element_type=jnp.float32)
            return mixed / weight_sum
        return lax.map(query_fn, jnp.arange(N_SEQ, dtype=jnp.int32)).reshape(full_rows, HEAD_DIM)
    per_head = lax.map(head_fn, jnp.arange(HEADS, dtype=jnp.int32))
    context = jnp.transpose(per_head, (1, 0, 2)).reshape(full_rows, HEADS * HEAD_DIM)
    context = jnp.where(key_valid[:, None], context, 0.0).astype(jnp.bfloat16)
    return jnp.dot(context, w_output, preferred_element_type=jnp.float32).astype(jnp.bfloat16)
```

```python
import functools
import math

import jax
import jax.numpy as jnp
from jax import lax
from jax.experimental import pallas as pl
from jax.experimental.pallas import tpu as pltpu
from jax.sharding import PartitionSpec as P

HEAD_DIM = 128
LOG2E = 1.4426950408889634
NORM_LIMIT = 60.0
NT = (((1,), (1,)), ((), ()))
VMEM = 56 * 2**20


def project_kernel(head_ref, x_ref, ws_ref, wv_ref, out_ref, w_scr):
    @pl.when(pl.program_id(0) == 0)
    def _():
        w_scr[:, :HEAD_DIM] = ws_ref[...]
        w_scr[:, HEAD_DIM:] = wv_ref[...]

    out_ref[...] = jnp.dot(
        x_ref[...], w_scr[...], preferred_element_type=jnp.float32
    ).astype(out_ref.dtype)


def project(tokens, w_shared, w_value, head, name):
    rows, width = tokens.shape
    step = 256
    weight = pl.BlockSpec((width, HEAD_DIM), lambda i, h: (0, h[0]))
    return pl.pallas_call(
        project_kernel,
        grid_spec=pltpu.PrefetchScalarGridSpec(
            num_scalar_prefetch=1,
            grid=(rows // step,),
            in_specs=[pl.BlockSpec((step, width), lambda i, h: (i, 0)), weight, weight],
            out_specs=pl.BlockSpec((step, 2 * HEAD_DIM), lambda i, h: (i, 0)),
            scratch_shapes=[pltpu.VMEM((width, 2 * HEAD_DIM), jnp.bfloat16)],
        ),
        out_shape=jax.ShapeDtypeStruct((rows, 2 * HEAD_DIM), jnp.bfloat16),
        compiler_params=pltpu.CompilerParams(vmem_limit_bytes=VMEM),
        cost_estimate=pl.CostEstimate(
            flops=2 * rows * width * 256, bytes_accessed=6 * 2**20, transcendentals=0
        ),
        name=name,
    )(head.reshape(1), tokens, w_shared, w_value)


def attend_kernel(count, first, last, scal_ref, *refs):
    own_ref, peer_ref = refs[:2]
    kv_refs = refs[2 : 2 + count]
    refs = refs[2 + count :]
    acc_in = None
    if not first:
        acc_in, refs = refs[0], refs[1:]
    if first:
        out_ref, norm_ref, q_scr, f_scr, v_scr = refs
        acc = out_ref
    elif last:
        out_ref, q_scr, f_scr, v_scr, acc = refs
    else:
        out_ref, q_scr, f_scr, v_scr = refs
        acc = out_ref
    step = pl.program_id(0)
    doc_len = scal_ref[0]
    rows = own_ref.shape[0]
    tile = 512

    @pl.when(step == 0)
    def _():
        q_scr[...] = own_ref[:, :HEAD_DIM]
        largest = None
        for at, kv_ref in enumerate(kv_refs):
            wide = kv_ref[:, :HEAD_DIM].astype(jnp.float32)
            square = wide * wide
            high = square.astype(jnp.bfloat16)
            low = (square - high.astype(jnp.float32)).astype(jnp.bfloat16)
            ones = jnp.ones((8, HEAD_DIM), jnp.bfloat16)
            total = lax.dot_general(ones, high, NT, preferred_element_type=jnp.float32)
            total += lax.dot_general(ones, low, NT, preferred_element_type=jnp.float32)
            f_scr[at] = lax.rsqrt(total / HEAD_DIM + 1e-06) * (LOG2E / math.sqrt(HEAD_DIM))
            if first:
                top = jnp.max(total)
                largest = top if largest is None else jnp.maximum(largest, top)
            place = lax.broadcasted_iota(jnp.int32, (rows, HEAD_DIM), 0) + scal_ref[4 + at]
            valid = place < doc_len
            v_scr[at, :, :HEAD_DIM] = jnp.where(
                valid, kv_ref[:, HEAD_DIM:].astype(jnp.float32), 0.0
            ).astype(jnp.bfloat16)
            v_scr[at, :, HEAD_DIM:] = jnp.where(valid, 1.0, 0.0).astype(jnp.bfloat16)
        if first:
            norm_ref[0, 0] = largest

    @pl.when(step == 1)
    def _():
        q_scr[...] = peer_ref[:, :HEAD_DIM]

    query_start = scal_ref[2 + step]
    if first:
        acc[...] = jnp.zeros_like(acc)
    else:
        acc[...] = acc_in[...]
    for at, kv_ref in enumerate(kv_refs):

        @pl.when((query_start < doc_len) & (scal_ref[4 + at] < doc_len))
        def _(at=at, kv_ref=kv_ref):
            queries = q_scr[...]
            total = acc[...]
            for cut in range(rows // tile):
                keys = slice(cut * tile, (cut + 1) * tile)
                scores = lax.dot_general(
                    queries, kv_ref[keys, :HEAD_DIM], NT, preferred_element_type=jnp.float32
                )
                weights = jnp.exp2(scores * f_scr[at, 0:1, keys])
                if first:
                    apart = jnp.where(step == at, cut * tile, 4 * rows)
                    weights = jnp.where(
                        lax.broadcasted_iota(jnp.int32, weights.shape, 0)
                        == lax.broadcasted_iota(jnp.int32, weights.shape, 1) + apart,
                        0.0,
                        weights,
                    )
                total += jnp.dot(
                    weights.astype(jnp.bfloat16),
                    v_scr[at, keys, :],
                    preferred_element_type=jnp.float32,
                )
            acc[...] = total

    if last:
        total = acc[...]
        inside = (
            lax.broadcasted_iota(jnp.int32, (rows, HEAD_DIM), 0) + query_start < doc_len
        )
        mixed = jnp.where(inside, total[:, :HEAD_DIM] / total[:, HEAD_DIM:], 0.0)
        out_ref[...] = mixed.astype(out_ref.dtype).reshape(out_ref.shape)


def attend(scalars, own, peer, blocks, state, last, name):
    rows = own.shape[0]
    count = len(blocks)
    first = state is None
    whole = pl.BlockSpec((rows, 2 * HEAD_DIM), lambda i, s: (0, 0))
    sums = pl.BlockSpec((rows, 2 * HEAD_DIM), lambda i, s: (i, 0))
    out_shape = jax.ShapeDtypeStruct((2 * rows, 2 * HEAD_DIM), jnp.float32)
    out_specs = sums
    scratch = [
        pltpu.VMEM((rows, HEAD_DIM), jnp.bfloat16),
        pltpu.VMEM((count, 8, rows), jnp.float32),
        pltpu.VMEM((count, rows, 2 * HEAD_DIM), jnp.bfloat16),
    ]
    if first:
        out_shape = (out_shape, jax.ShapeDtypeStruct((1, 1), jnp.float32))
        out_specs = (sums, pl.BlockSpec(memory_space=pltpu.SMEM))
    if last:
        out_shape = jax.ShapeDtypeStruct((8, 2, rows // 8, HEAD_DIM), jnp.bfloat16)
        out_specs = pl.BlockSpec(
            (8, 1, rows // 8, HEAD_DIM),
            lambda i, s: (0, jnp.where(i == 0, s[1], 1 - s[1]), 0, 0),
        )
        scratch.append(pltpu.VMEM((rows, 2 * HEAD_DIM), jnp.float32))
    return pl.pallas_call(
        functools.partial(attend_kernel, count, first, last),
        grid_spec=pltpu.PrefetchScalarGridSpec(
            num_scalar_prefetch=1,
            grid=(2,),
            in_specs=[whole] * (2 + count) + ([] if first else [sums]),
            out_specs=out_specs,
            scratch_shapes=scratch,
        ),
        out_shape=out_shape,
        compiler_params=pltpu.CompilerParams(vmem_limit_bytes=VMEM),
        cost_estimate=pl.CostEstimate(
            flops=8 * 2 * rows * rows * count * HEAD_DIM,
            bytes_accessed=8 * 2**20,
            transcendentals=0,
        ),
        name=name,
    )(scalars, own, peer, *blocks, *([] if first else [state]))


def attend_with_peak(doc_len, core, own_starts, own, peer, blocks, starts):
    rows = own.shape[0]
    queries = jnp.concatenate([own[:, :HEAD_DIM], peer[:, :HEAD_DIM]])
    here = jnp.arange(rows, dtype=jnp.int32)
    query_pos = jnp.concatenate([own_starts[0] + here, own_starts[1] + here])

    def absorb(running, block):
        key_values, start = block
        peak, weight_sum, total = running
        keys, values = key_values[:, :HEAD_DIM], key_values[:, HEAD_DIM:]
        wide = keys.astype(jnp.float32)
        factor = lax.rsqrt(jnp.mean(wide * wide, axis=-1) + 1e-06) / math.sqrt(HEAD_DIM)
        key_pos = start + here
        allowed = (key_pos[None, :] < doc_len) & (key_pos[None, :] != query_pos[:, None])
        scores = jnp.dot(queries, keys.T, preferred_element_type=jnp.float32) * factor[None, :]
        scores = jnp.where(allowed, scores, -1e30)
        new_peak = jnp.maximum(peak, jnp.max(scores, axis=-1))
        weights = jnp.where(allowed, jnp.exp(scores - new_peak[:, None]), 0.0)
        rescale = jnp.exp(peak - new_peak)
        mixed = jnp.dot(weights.astype(jnp.bfloat16), values, preferred_element_type=jnp.float32)
        return (
            new_peak,
            weight_sum * rescale + jnp.sum(weights, axis=-1),
            total * rescale[:, None] + mixed,
        ), None

    empty = (
        jnp.full((2 * rows,), -1e30, jnp.float32),
        jnp.zeros((2 * rows,), jnp.float32),
        jnp.zeros((2 * rows, HEAD_DIM), jnp.float32),
    )
    (_, weight_sum, total), _ = lax.scan(absorb, empty, (jnp.stack(blocks), jnp.stack(starts)))
    denom = jnp.where(weight_sum > 0.0, weight_sum, 1.0)
    mixed = jnp.where((query_pos < doc_len)[:, None], total / denom[:, None], 0.0)
    mixed = mixed.astype(jnp.bfloat16).reshape(2, 8, rows // 8, HEAD_DIM)
    mixed = jnp.where(core == 0, mixed, mixed[::-1])
    return mixed.transpose(1, 0, 2, 3)


def output_kernel(scal_ref, near_ref, far_ref, w_near_ref, w_far_ref, out_ref):
    def side(ctx_ref, w_ref):
        left = jnp.concatenate([ctx_ref[g, 0] for g in range(4)], axis=1)
        return jnp.dot(left, w_ref[...], preferred_element_type=jnp.float32)

    total = side(near_ref, w_near_ref) + side(far_ref, w_far_ref)
    out_ref[0] = total.astype(out_ref.dtype)


def output_part(scalars, context, w_near, w_far, dtype, name):
    rows = context.shape[2]
    width = w_near.shape[1]
    ctx = (4, 1, rows, HEAD_DIM)
    return pl.pallas_call(
        output_kernel,
        grid_spec=pltpu.PrefetchScalarGridSpec(
            num_scalar_prefetch=1,
            grid=(width // 256,),
            in_specs=[
                pl.BlockSpec(ctx, lambda i, s: (s[0], s[1], 0, 0)),
                pl.BlockSpec(ctx, lambda i, s: (1 - s[0], s[1], 0, 0)),
                pl.BlockSpec((4 * HEAD_DIM, 256), lambda i, s: (0, i)),
                pl.BlockSpec((4 * HEAD_DIM, 256), lambda i, s: (0, i)),
            ],
            out_specs=pl.BlockSpec((1, rows, 256), lambda i, s: (i, 0, 0)),
        ),
        out_shape=jax.ShapeDtypeStruct((width // 256, rows, 256), dtype),
        compiler_params=pltpu.CompilerParams(vmem_limit_bytes=VMEM),
        cost_estimate=pl.CostEstimate(
            flops=2 * rows * width * 1024, bytes_accessed=5 * 2**20, transcendentals=0
        ),
        name=name,
    )(scalars, context, context, w_near, w_far)


def body(tokens, w_shared, w_value, w_output, doc_length):
    rows = tokens.shape[0]
    doc_len = doc_length[0]
    seq = lax.axis_index("seq")
    core = lax.rem(seq, 2)
    z = lax.div(seq, 2)
    x_hi = lax.div(lax.axis_index("head"), 4)

    def swap(array):
        return lax.ppermute(array, "seq", [(i, i ^ 1) for i in range(8)])

    def along_z(array, by):
        return lax.ppermute(array, "seq", [(i, (i + 2 * by) % 8) for i in range(8)])

    y_groups = [[0, 1, 2, 3], [4, 5, 6, 7]]
    w_own = lax.dynamic_slice_in_dim(w_output, core * HEAD_DIM, HEAD_DIM, 0)
    w_other = lax.ppermute(
        w_own,
        ("head", "batch"),
        [(h * 2 + b, (h ^ 4) * 2 + (1 - b)) for h in range(8) for b in range(2)],
    )
    w_near = lax.all_gather(w_own, "head", axis=0, axis_index_groups=y_groups, tiled=True)
    w_far = lax.all_gather(w_other, "head", axis=0, axis_index_groups=y_groups, tiled=True)

    given = project(tokens, w_shared, w_value, 1 - core, "project_given")
    peer = swap(given)
    own = project(tokens, w_shared, w_value, core, "project_own")

    own_left, peer_right = along_z(own, 1), along_z(peer, -1)
    peer_left, own_right = along_z(peer, 1), along_z(own, -1)
    own_far, peer_far = along_z(own_left, 1), along_z(peer_right, -1)

    def start_of(by, other):
        place = lax.rem(z + by, 4) * 2
        return (place + (1 - core if other else core)) * rows

    def scalars(*starts):
        return jnp.stack([doc_len, core, start_of(0, False), start_of(0, True), *starts])

    here = (start_of(0, False), start_of(0, True))
    near = (start_of(3, False), start_of(1, True), start_of(3, True), start_of(1, False))
    far = (start_of(2, False), start_of(2, True))
    state, norm = attend(scalars(*here), own, peer, (own, peer), None, False, "attend_here")
    near_blocks = (own_left, peer_right, peer_left, own_right)
    state = attend(scalars(*near), own, peer, near_blocks, state, False, "attend_near")
    context = attend(scalars(*far), own, peer, (own_far, peer_far), state, True, "attend_far")
    context = lax.cond(
        norm[0, 0] <= NORM_LIMIT**2,
        lambda: context,
        lambda: attend_with_peak(
            doc_len,
            core,
            here,
            own,
            peer,
            (own, peer, *near_blocks, own_far, peer_far),
            (*here, *near, *far),
        ),
    )
    context = lax.all_to_all(context, "head", 0, 0, tiled=True)
    given_part = output_part(
        jnp.stack([x_hi, 1 - core]), context, w_near, w_far, jnp.bfloat16, "output_given"
    )
    swapped = swap(given_part)
    own_part = output_part(
        jnp.stack([x_hi, core]), context, w_near, w_far, jnp.float32, "output_own"
    )
    result = (own_part + swapped.astype(jnp.float32)).astype(jnp.bfloat16)
    result = lax.all_to_all(result, "head", 0, 0, tiled=True)
    return result.reshape(rows, result.shape[-1])


def solution(mesh):
    placed = (
        P(("batch", "seq"), None),
        P(None, "head"),
        P(None, "head"),
        P("head", None),
        P("batch"),
    )
    return jax.shard_map(
        body, mesh=mesh, in_specs=placed, out_specs=P(("batch", "seq"), "head"), check_vma=False
    )
```

```python
import functools
import math

import jax
import jax.numpy as jnp
from jax import lax
from jax.experimental import pallas as pl
from jax.experimental.pallas import tpu as pltpu
from jax.sharding import PartitionSpec as P

HEAD_DIM = 128
LOG2E = 1.4426950408889634
NORM_LIMIT = 60.0
EXTRA = 16
NT = (((1,), (1,)), ((), ()))
VMEM = 56 * 2**20
HBM = pl.BlockSpec(memory_space=pl.ANY)
SMEM = pl.BlockSpec(memory_space=pltpu.SMEM)
F32 = jnp.float32
BF16 = jnp.bfloat16


def own_core():
    return lax.rem(lax.axis_index("seq"), 2)


def block_start(by, other, rows):
    seq = lax.axis_index("seq")
    place = lax.rem(lax.div(seq, 2) + by, 4) * 2
    core = lax.rem(seq, 2)
    return (place + (1 - core if other else core)) * rows


def start_all(copies):
    for copy in copies:
        copy.start()
    return copies


def project_kernel(x_ref, ws_ref, wv_ref, own_ref, given_ref, x_scr, ws_scr, wv_scr, out_scr, sem):
    rows, _ = x_ref.shape
    cuts = x_scr.shape[0]
    step = rows // cuts
    weights = start_all(
        [
            pltpu.make_async_copy(ws_ref, ws_scr, sem.at[0]),
            pltpu.make_async_copy(wv_ref, wv_scr, sem.at[1]),
        ]
    )
    tokens = start_all(
        [
            pltpu.make_async_copy(x_ref.at[pl.ds(i * step, step)], x_scr.at[i], sem.at[2 + i])
            for i in range(cuts)
        ]
    )
    wide = 2 * HEAD_DIM
    row = lax.broadcasted_iota(jnp.int32, (EXTRA, wide), 0)
    extra = [jnp.zeros((EXTRA, wide), F32) for _ in range(2)]
    largest = [jnp.zeros((8, wide), F32) for _ in range(2)]
    ones = jnp.ones((8, HEAD_DIM), BF16)
    for copy in weights:
        copy.wait()
    for i in range(cuts):
        tokens[i].wait()
        x = x_scr[i]
        shared = jnp.dot(x, ws_scr[...], preferred_element_type=F32).astype(BF16)
        values = jnp.dot(x, wv_scr[...], preferred_element_type=F32).astype(BF16)
        for h in range(2):
            cols = slice(h * HEAD_DIM, (h + 1) * HEAD_DIM)
            keys = shared[:, cols]
            out_scr[h, i * step : (i + 1) * step, :HEAD_DIM] = keys
            out_scr[h, i * step : (i + 1) * step, HEAD_DIM:] = values[:, cols]
            square = keys.astype(F32) * keys.astype(F32)
            high = square.astype(BF16)
            low = (square - high.astype(F32)).astype(BF16)
            total = lax.dot_general(ones, high, NT, preferred_element_type=F32)
            total += lax.dot_general(ones, low, NT, preferred_element_type=F32)
            for j in range(step // wide):
                part = total[:, j * wide : (j + 1) * wide]
                largest[h] = jnp.maximum(largest[h], part)
                factor = lax.rsqrt(part / HEAD_DIM + 1e-06) * (LOG2E / math.sqrt(HEAD_DIM))
                first = factor.astype(BF16).astype(F32)
                at = i * (step // wide) + j
                first16 = jnp.concatenate([first, first])
                second16 = jnp.concatenate([factor - first, factor - first])
                extra[h] = jnp.where(row == at, first16, extra[h])
                extra[h] = jnp.where(row == 4 + at, second16, extra[h])
    for h in range(2):
        top = jnp.broadcast_to(jnp.max(largest[h]), (EXTRA, wide))
        out_scr[h, rows:, :] = jnp.where(row >= 8, top, extra[h]).astype(BF16)
    core = own_core()
    for copy in start_all(
        [
            pltpu.make_async_copy(out_scr.at[core], own_ref, sem.at[0]),
            pltpu.make_async_copy(out_scr.at[1 - core], given_ref, sem.at[1]),
        ]
    ):
        copy.wait()


def project(tokens, w_shared, w_value):
    rows, width = tokens.shape
    cuts = 2
    out = jax.ShapeDtypeStruct((rows + EXTRA, 2 * HEAD_DIM), BF16)
    return pl.pallas_call(
        project_kernel,
        in_specs=[HBM] * 3,
        out_specs=(HBM, HBM),
        out_shape=(out, out),
        scratch_shapes=[
            pltpu.VMEM((cuts, rows // cuts, width), BF16),
            pltpu.VMEM(w_shared.shape, BF16),
            pltpu.VMEM(w_value.shape, BF16),
            pltpu.VMEM((2, rows + EXTRA, 2 * HEAD_DIM), BF16),
            pltpu.SemaphoreType.DMA((2 + cuts,)),
        ],
        compiler_params=pltpu.CompilerParams(vmem_limit_bytes=VMEM),
        cost_estimate=pl.CostEstimate(
            flops=2 * rows * width * 512, bytes_accessed=7 * 2**20, transcendentals=0
        ),
        name="project",
    )(tokens, w_shared, w_value)


def spread_kernel(w_ref, after_ref, out_ref, sem):
    del after_ref
    mine = w_ref.at[pl.ds(pl.multiple_of(own_core() * HEAD_DIM, HEAD_DIM), HEAD_DIM)]
    for copy in start_all(
        [pltpu.make_async_copy(mine, out_ref.at[i], sem.at[i]) for i in range(4)]
    ):
        copy.wait()


def spread(w_output, after):
    return pl.pallas_call(
        spread_kernel,
        in_specs=[HBM] * 2,
        out_specs=HBM,
        out_shape=jax.ShapeDtypeStruct((4, HEAD_DIM, w_output.shape[1]), BF16),
        scratch_shapes=[pltpu.SemaphoreType.DMA((4,))],
        name="spread",
    )(w_output, after)


def attend_kernel(places, first, last, doc_ref, *refs):
    count = len(places)
    if first:
        kv_refs, refs = refs[:count], refs[count:]
        out_ref, kv_scr, acc, sem, acc_sem = refs
        q_of = lambda q: kv_scr[q, :-EXTRA, :HEAD_DIM]
        copies = []
    else:
        q_refs, kv_refs, refs = refs[:2], refs[2 : 2 + count], refs[2 + count :]
        state_ref, refs = refs[0], refs[1:]
        if last:
            rest, refs = refs[:4], refs[4:]
            out_ref, kv_scr, acc, sem, acc_sem, q_scr, ctx_scr, peak, weight_sum = refs
        else:
            out_ref, kv_scr, acc, sem, acc_sem, q_scr = refs
        q_of = lambda q: q_scr[q, :-EXTRA, :]
        copies = start_all(
            [
                pltpu.make_async_copy(q_refs[q].at[:, pl.ds(0, HEAD_DIM)], q_scr.at[q], acc_sem.at[2 + q])
                for q in range(2)
            ]
        )
    rows = kv_scr.shape[1] - EXTRA
    tile = 512
    blocks = start_all(
        [pltpu.make_async_copy(kv_refs[i], kv_scr.at[i], sem.at[i]) for i in range(count)]
    )
    if not first:
        copies += start_all(
            [pltpu.make_async_copy(state_ref.at[q], acc.at[q], acc_sem.at[q]) for q in range(2)]
        )
    else:
        acc[...] = jnp.zeros_like(acc)
    for copy in copies:
        copy.wait()
    doc_len = doc_ref[0]
    q_starts = [block_start(0, other, rows) for other in (False, True)]
    active = jnp.minimum(q_starts[0], q_starts[1]) < doc_len
    if first:
        for copy in blocks:
            copy.wait()
    for i in range(count):
        if not first:
            blocks[i].wait()
        start = block_start(*places[i], rows)

        @pl.when(active & (start < doc_len))
        def _(i=i, start=start):
            extra = kv_scr[i, rows : rows + 8, :].astype(F32)
            factor = extra[0:4] + extra[4:8]
            for q in range(2):
                queries = q_of(q)
                total = acc[q]
                for cut in range(rows // tile):
                    keys = slice(cut * tile, (cut + 1) * tile)
                    each = tile // 256
                    scale = jnp.concatenate(
                        [factor[cut * each + j : cut * each + j + 1] for j in range(each)], axis=1
                    )
                    place = lax.broadcasted_iota(jnp.int32, (1, tile), 1) + (start + cut * tile)
                    bias = jnp.where(place < doc_len, 0.0, -1e30)
                    scores = lax.dot_general(
                        queries, kv_scr[i, keys, :HEAD_DIM], NT, preferred_element_type=F32
                    )
                    weights = jnp.exp2(scores * scale + bias)
                    if first and i == q:
                        weights = jnp.where(
                            lax.broadcasted_iota(jnp.int32, weights.shape, 0)
                            == lax.broadcasted_iota(jnp.int32, weights.shape, 1) + cut * tile,
                            0.0,
                            weights,
                        )
                    values = jnp.concatenate(
                        [kv_scr[i, keys, HEAD_DIM:], jnp.ones((tile, HEAD_DIM), BF16)], axis=1
                    )
                    total += jnp.dot(weights.astype(BF16), values, preferred_element_type=F32)
                acc[q] = total

    if not last:
        for copy in start_all(
            [pltpu.make_async_copy(acc.at[q], out_ref.at[q], acc_sem.at[q]) for q in range(2)]
        ):
            copy.wait()
        return

    norm = jnp.maximum(
        jnp.max(q_scr[0, rows + 8 :, :].astype(F32)), jnp.max(q_scr[1, rows + 8 :, :].astype(F32))
    )

    @pl.when(norm > NORM_LIMIT**2)
    def _():
        peak[...] = jnp.full_like(peak, -1e30)
        weight_sum[...] = jnp.zeros_like(weight_sum)
        acc[...] = jnp.zeros_like(acc)
        near = ((3, False), (3, True), (1, False), (1, True))
        everything = [
            (q_refs[0], (0, False)),
            (q_refs[1], (0, True)),
            *zip(rest, near),
            *zip(kv_refs, places),
        ]
        small = 256
        for block_ref, place in everything:
            pltpu.sync_copy(block_ref, kv_scr.at[0])
            key_start = block_start(*place, rows)
            extra = kv_scr[0, rows : rows + 8, :].astype(F32)
            factor = extra[0:4] + extra[4:8]

            def absorb(at, carry, key_start=key_start, factor=factor):
                q = lax.div(at, rows // small)
                low = pl.multiple_of(lax.rem(at, rows // small) * small, small)
                here = pl.ds(low, small)
                query_start = jnp.where(q == 0, q_starts[0], q_starts[1]) + low
                for cut in range(rows // small):
                    keys = slice(cut * small, (cut + 1) * small)
                    scores = lax.dot_general(
                        q_scr[q, here, :], kv_scr[0, keys, :HEAD_DIM], NT, preferred_element_type=F32
                    )
                    key_pos = lax.broadcasted_iota(jnp.int32, scores.shape, 1) + (
                        key_start + cut * small
                    )
                    query_pos = lax.broadcasted_iota(jnp.int32, scores.shape, 0) + query_start
                    allowed = (key_pos < doc_len) & (key_pos != query_pos)
                    scores = jnp.where(allowed, scores * factor[cut : cut + 1], -1e30)
                    old = peak[q, here, :]
                    new = jnp.maximum(old, jnp.max(scores, axis=1, keepdims=True))
                    weights = jnp.where(allowed, jnp.exp2(scores - new[:, :1]), 0.0)
                    rescale = jnp.exp2(old - new)
                    peak[q, here, :] = new
                    weight_sum[q, here, :] = weight_sum[q, here, :] * rescale + jnp.sum(
                        weights, axis=1, keepdims=True
                    )
                    acc[q, here, :HEAD_DIM] = acc[q, here, :HEAD_DIM] * rescale + jnp.dot(
                        weights.astype(BF16), kv_scr[0, keys, HEAD_DIM:], preferred_element_type=F32
                    )
                return carry

            lax.fori_loop(0, 2 * rows // small, absorb, 0)
        for q in range(2):
            acc[q, :, HEAD_DIM:] = weight_sum[q]

    core = own_core()
    outs = []
    for q in range(2):
        total = acc[q]
        inside = lax.broadcasted_iota(jnp.int32, (rows, HEAD_DIM), 0) + q_starts[q] < doc_len
        mixed = jnp.where(inside, total[:, :HEAD_DIM] / total[:, HEAD_DIM:], 0.0)
        ctx_scr[q] = mixed.astype(BF16).reshape(ctx_scr.shape[1:])
        block = core if q == 0 else 1 - core
        outs += start_all(
            [pltpu.make_async_copy(ctx_scr.at[q], out_ref.at[:, block], acc_sem.at[q])]
        )
    for copy in outs:
        copy.wait()


def attend(doc_length, queries, blocks, places, state, rest, name):
    rows = blocks[0].shape[0] - EXTRA
    count = len(blocks)
    first, last = state is None, rest is not None
    out_shape = jax.ShapeDtypeStruct((2, rows, 2 * HEAD_DIM), F32)
    scratch = [
        pltpu.VMEM((count, rows + EXTRA, 2 * HEAD_DIM), BF16),
        pltpu.VMEM(out_shape.shape, F32),
        pltpu.SemaphoreType.DMA((count,)),
        pltpu.SemaphoreType.DMA((4,)),
    ]
    args = list(blocks)
    if not first:
        args = [*queries, *blocks, state]
        scratch.append(pltpu.VMEM((2, rows + EXTRA, HEAD_DIM), BF16))
    if last:
        args += rest
        out_shape = jax.ShapeDtypeStruct((4, 2, rows // 4, HEAD_DIM), BF16)
        scratch += [
            pltpu.VMEM((2, 4, rows // 4, HEAD_DIM), BF16),
            pltpu.VMEM((2, rows, HEAD_DIM), F32),
            pltpu.VMEM((2, rows, HEAD_DIM), F32),
        ]
    return pl.pallas_call(
        functools.partial(attend_kernel, places, first, last),
        in_specs=[SMEM] + [HBM] * len(args),
        out_specs=HBM,
        out_shape=out_shape,
        scratch_shapes=scratch,
        compiler_params=pltpu.CompilerParams(vmem_limit_bytes=VMEM),
        cost_estimate=pl.CostEstimate(
            flops=16 * rows * rows * count * HEAD_DIM,
            bytes_accessed=4 * 2**20,
            transcendentals=0,
        ),
        name=name,
    )(doc_length, *args)


def output_kernel(ctx_ref, got_ref, w_ref, w_got_ref, out_ref, left_scr, w_scr, out_scr, sem, out_sem):
    core = own_core()
    width = w_ref.shape[2]
    cuts = out_sem.shape[0]
    step = width // cuts
    lefts = start_all(
        [
            pltpu.make_async_copy(ctx_ref.at[:, core], left_scr.at[0], sem.at[2 * cuts]),
            pltpu.make_async_copy(got_ref.at[:, core], left_scr.at[1], sem.at[2 * cuts + 1]),
        ]
    )
    weights = []
    for i in range(cuts):
        cols = pl.ds(i * step, step)
        weights.append(
            start_all(
                [
                    pltpu.make_async_copy(ref.at[:, :, cols], w_scr.at[at, :, :, cols], sem.at[2 * i + at])
                    for at, ref in enumerate((w_ref, w_got_ref))
                ]
            )
        )
    for copy in lefts:
        copy.wait()
    left = jnp.concatenate([left_scr[at, y] for at in range(2) for y in range(4)], axis=1)
    outs = []
    for i in range(cuts):
        for copy in weights[i]:
            copy.wait()
        cols = slice(i * step, (i + 1) * step)
        right = w_scr[:, :, :, cols].reshape(8 * HEAD_DIM, step)
        part = jnp.dot(left, right, preferred_element_type=F32).astype(BF16)
        for j in range(step // 256):
            out_scr[i * (step // 256) + j] = part[:, j * 256 : (j + 1) * 256]
        mine = pl.ds(i * (step // 256), step // 256)
        outs += start_all(
            [pltpu.make_async_copy(out_scr.at[mine], out_ref.at[mine], out_sem.at[i])]
        )
    for copy in outs:
        copy.wait()


def output(context, got, weights, weights_got):
    rows = context.shape[2]
    width = weights.shape[2]
    cuts = 4
    out_shape = jax.ShapeDtypeStruct((8, rows, width // 8), BF16)
    return pl.pallas_call(
        output_kernel,
        in_specs=[HBM] * 4,
        out_specs=HBM,
        out_shape=out_shape,
        scratch_shapes=[
            pltpu.VMEM((2, 4, rows, HEAD_DIM), BF16),
            pltpu.VMEM((2, *weights.shape), BF16),
            pltpu.VMEM(out_shape.shape, BF16),
            pltpu.SemaphoreType.DMA((2 * cuts + 2,)),
            pltpu.SemaphoreType.DMA((cuts,)),
        ],
        compiler_params=pltpu.CompilerParams(vmem_limit_bytes=VMEM),
        cost_estimate=pl.CostEstimate(
            flops=2 * rows * width * 1024, bytes_accessed=6 * 2**20, transcendentals=0
        ),
        name="output",
    )(context, got, weights, weights_got)


def body(tokens, w_shared, w_value, w_output, doc_length):
    def move(array, by, cross):
        return lax.ppermute(
            array, "seq", [(i, (i // 2 + by) % 4 * 2 + (i % 2 ^ cross)) for i in range(8)]
        )

    own, given = project(tokens, w_shared, w_value)
    peer = move(given, 0, 1)
    own_left, peer_right = move(own, 1, 0), move(given, -1, 1)
    peer_left, own_right = move(given, 1, 1), move(own, -1, 0)
    own_far, peer_far = move(own_left, 1, 0), move(peer_right, -1, 0)

    y_groups = [[0, 1, 2, 3], [4, 5, 6, 7]]
    weights = lax.all_to_all(
        spread(w_output, given), "head", 0, 0, axis_index_groups=y_groups, tiled=True
    )
    weights_got = move(weights, 0, 1)

    queries = (own, peer)
    near = (own_left, peer_left, own_right, peer_right)
    state = attend(doc_length, None, queries, ((0, False), (0, True)), None, None, "attend_here")
    state = attend(
        doc_length,
        queries,
        near,
        ((3, False), (3, True), (1, False), (1, True)),
        state,
        None,
        "attend_near",
    )
    context = attend(
        doc_length,
        queries,
        (own_far, peer_far),
        ((2, False), (2, True)),
        state,
        near,
        "attend_far",
    )
    context = lax.all_to_all(context, "head", 0, 0, axis_index_groups=y_groups, tiled=True)
    terms = output(context, move(context, 0, 1), weights, weights_got)
    terms = lax.all_to_all(terms, "head", 0, 0, tiled=True).astype(F32)
    result = (terms[:4] + terms[4:]).astype(BF16)
    return result.reshape(tokens.shape[0], result.shape[-1])


def solution(mesh):
    placed = (
        P(("batch", "seq"), None),
        P(None, "head"),
        P(None, "head"),
        P("head", None),
        P("batch"),
    )
    return jax.shard_map(
        body, mesh=mesh, in_specs=placed, out_specs=P(("batch", "seq"), "head"), check_vma=False
    )
```

```python
import functools
import math

import jax
import jax.numpy as jnp
from jax import lax
from jax.experimental import pallas as pl
from jax.experimental.pallas import tpu as pltpu
from jax.sharding import PartitionSpec as P

HEAD_DIM = 128
LOG2E = 1.4426950408889634
NORM_LIMIT = 60.0
EXTRA = 16
NT = (((1,), (1,)), ((), ()))
VMEM = 56 * 2**20
HBM = pl.BlockSpec(memory_space=pltpu.HBM)
SMEM = pl.BlockSpec(memory_space=pltpu.SMEM)
F32 = jnp.float32
BF16 = jnp.bfloat16


def own_core():
    return lax.rem(lax.axis_index("seq"), 2)


def block_start(by, other, rows):
    seq = lax.axis_index("seq")
    place = lax.rem(lax.div(seq, 2) + by, 4) * 2
    core = lax.rem(seq, 2)
    return (place + (1 - core if other else core)) * rows


def start_all(copies):
    for copy in copies:
        copy.start()
    return copies


def project_kernel(x_ref, ws_ref, wv_ref, own_ref, given_ref, x_scr, ws_scr, wv_scr, out_scr, sem, out_sem):
    rows, _ = x_ref.shape
    cuts = x_scr.shape[0]
    step = rows // cuts
    weights = start_all(
        [
            pltpu.make_async_copy(ws_ref, ws_scr, sem.at[0]),
            pltpu.make_async_copy(wv_ref, wv_scr, sem.at[1]),
        ]
    )
    tokens = start_all(
        [
            pltpu.make_async_copy(x_ref.at[pl.ds(i * step, step)], x_scr.at[i], sem.at[2 + i])
            for i in range(cuts)
        ]
    )
    wide = 2 * HEAD_DIM
    row = lax.broadcasted_iota(jnp.int32, (EXTRA, wide), 0)
    extra = [jnp.zeros((EXTRA, wide), F32) for _ in range(2)]
    largest = [jnp.zeros((8, wide), F32) for _ in range(2)]
    ones = jnp.ones((8, HEAD_DIM), BF16)
    core = own_core()
    outs = []

    def send(low, size):
        here = pl.ds(low, size)
        for h, ref in ((core, own_ref), (1 - core, given_ref)):
            copy = pltpu.make_async_copy(
                out_scr.at[h, here], ref.at[here], out_sem.at[len(outs)]
            )
            copy.start()
            outs.append(copy)

    for copy in weights:
        copy.wait()
    for i in range(cuts):
        tokens[i].wait()
        x = x_scr[i]
        shared = jnp.dot(x, ws_scr[...], preferred_element_type=F32).astype(BF16)
        values = jnp.dot(x, wv_scr[...], preferred_element_type=F32).astype(BF16)
        for h in range(2):
            cols = slice(h * HEAD_DIM, (h + 1) * HEAD_DIM)
            out_scr[h, i * step : (i + 1) * step, :HEAD_DIM] = shared[:, cols]
            out_scr[h, i * step : (i + 1) * step, HEAD_DIM:] = values[:, cols]
        send(i * step, step)
        for h in range(2):
            keys = shared[:, h * HEAD_DIM : (h + 1) * HEAD_DIM].astype(F32)
            square = keys * keys
            high = square.astype(BF16)
            low = (square - high.astype(F32)).astype(BF16)
            total = lax.dot_general(ones, high, NT, preferred_element_type=F32)
            total += lax.dot_general(ones, low, NT, preferred_element_type=F32)
            largest[h] = jnp.maximum(largest[h], total)
            factor = lax.rsqrt(total / HEAD_DIM + 1e-06) * (LOG2E / math.sqrt(HEAD_DIM))
            first = factor.astype(BF16).astype(F32)
            extra[h] = jnp.where(row == i, jnp.concatenate([first] * 2), extra[h])
            extra[h] = jnp.where(row == 4 + i, jnp.concatenate([factor - first] * 2), extra[h])
    for h in range(2):
        top = jnp.broadcast_to(jnp.max(largest[h]), (EXTRA, wide))
        out_scr[h, rows:, :] = jnp.where(row >= 8, top, extra[h]).astype(BF16)
    send(rows, EXTRA)
    for copy in outs:
        copy.wait()


def project(tokens, w_shared, w_value):
    rows, width = tokens.shape
    cuts = 4
    out = jax.ShapeDtypeStruct((rows + EXTRA, 2 * HEAD_DIM), BF16)
    return pl.pallas_call(
        project_kernel,
        in_specs=[HBM] * 3,
        out_specs=(HBM, HBM),
        out_shape=(out, out),
        scratch_shapes=[
            pltpu.VMEM((cuts, rows // cuts, width), BF16),
            pltpu.VMEM(w_shared.shape, BF16),
            pltpu.VMEM(w_value.shape, BF16),
            pltpu.VMEM((2, rows + EXTRA, 2 * HEAD_DIM), BF16),
            pltpu.SemaphoreType.DMA((2 + cuts,)),
            pltpu.SemaphoreType.DMA((2 * cuts + 2,)),
        ],
        compiler_params=pltpu.CompilerParams(vmem_limit_bytes=VMEM),
        cost_estimate=pl.CostEstimate(
            flops=2 * rows * width * 512, bytes_accessed=7 * 2**20, transcendentals=0
        ),
        name="project",
    )(tokens, w_shared, w_value)


def spread_kernel(w_ref, after_ref, out_ref, scr, sem):
    del after_ref
    mine = w_ref.at[pl.ds(pl.multiple_of(own_core() * HEAD_DIM, HEAD_DIM), HEAD_DIM)]
    pltpu.sync_copy(mine, scr)
    for copy in start_all(
        [pltpu.make_async_copy(scr, out_ref.at[i], sem.at[i]) for i in range(4)]
    ):
        copy.wait()


def spread(w_output, after):
    piece = (HEAD_DIM, w_output.shape[1])
    return pl.pallas_call(
        spread_kernel,
        in_specs=[HBM] * 2,
        out_specs=HBM,
        out_shape=jax.ShapeDtypeStruct((4, *piece), BF16),
        scratch_shapes=[pltpu.VMEM(piece, BF16), pltpu.SemaphoreType.DMA((4,))],
        name="spread",
    )(w_output, after)


def attend_kernel(places, first, last, doc_ref, *refs):
    count = len(places)
    if first:
        kv_refs, refs = refs[:count], refs[count:]
        out_ref, kv_scr, acc, sem, acc_sem = refs
        q_of = lambda q: kv_scr[q, :-EXTRA, :HEAD_DIM]
        copies = []
    else:
        q_refs, kv_refs, refs = refs[:2], refs[2 : 2 + count], refs[2 + count :]
        if last:
            states, rest, refs = refs[:2], refs[2:6], refs[6:]
            out_ref, kv_scr, acc, sem, acc_sem, q_scr, sums, sums_sem, ctx_scr, peak, weight_sum = refs
        else:
            out_ref, kv_scr, acc, sem, acc_sem, q_scr = refs
        q_of = lambda q: q_scr[q, :-EXTRA, :]
        copies = start_all(
            [
                pltpu.make_async_copy(q_refs[q].at[:, pl.ds(0, HEAD_DIM)], q_scr.at[q], acc_sem.at[2 + q])
                for q in range(2)
            ]
        )
    rows = kv_scr.shape[1] - EXTRA
    tile = 512
    blocks = start_all(
        [pltpu.make_async_copy(kv_refs[i], kv_scr.at[i], sem.at[i]) for i in range(count)]
    )
    if last:
        added = start_all(
            [pltpu.make_async_copy(states[i], sums.at[i], sums_sem.at[i]) for i in range(2)]
        )
    acc[...] = jnp.zeros_like(acc)
    for copy in copies:
        copy.wait()
    doc_len = doc_ref[0]
    q_starts = [block_start(0, other, rows) for other in (False, True)]
    active = jnp.minimum(q_starts[0], q_starts[1]) < doc_len
    if first:
        for copy in blocks:
            copy.wait()
    for i in range(count):
        if not first:
            blocks[i].wait()
        start = block_start(*places[i], rows)

        @pl.when(active & (start < doc_len))
        def _(i=i, start=start):
            extra = kv_scr[i, rows : rows + 8, :].astype(F32)
            factor = extra[0:4] + extra[4:8]
            for q in range(2):
                queries = q_of(q)
                total = acc[q]
                for cut in range(rows // tile):
                    keys = slice(cut * tile, (cut + 1) * tile)
                    each = tile // 256
                    scale = jnp.concatenate(
                        [factor[cut * each + j : cut * each + j + 1] for j in range(each)], axis=1
                    )
                    place = lax.broadcasted_iota(jnp.int32, (1, tile), 1) + (start + cut * tile)
                    bias = jnp.where(place < doc_len, 0.0, -1e30)
                    scores = lax.dot_general(
                        queries, kv_scr[i, keys, :HEAD_DIM], NT, preferred_element_type=F32
                    )
                    weights = jnp.exp2(scores * scale + bias)
                    if first and i == q:
                        weights = jnp.where(
                            lax.broadcasted_iota(jnp.int32, weights.shape, 0)
                            == lax.broadcasted_iota(jnp.int32, weights.shape, 1) + cut * tile,
                            0.0,
                            weights,
                        )
                    values = jnp.concatenate(
                        [kv_scr[i, keys, HEAD_DIM:], jnp.ones((tile, HEAD_DIM), BF16)], axis=1
                    )
                    total += jnp.dot(weights.astype(BF16), values, preferred_element_type=F32)
                acc[q] = total

    if not last:
        for copy in start_all(
            [pltpu.make_async_copy(acc.at[q], out_ref.at[q], acc_sem.at[q]) for q in range(2)]
        ):
            copy.wait()
        return

    for copy in added:
        copy.wait()
    norm = jnp.maximum(
        jnp.max(q_scr[0, rows + 8 :, :].astype(F32)), jnp.max(q_scr[1, rows + 8 :, :].astype(F32))
    )

    @pl.when(norm > NORM_LIMIT**2)
    def _():
        peak[...] = jnp.full_like(peak, -1e30)
        weight_sum[...] = jnp.zeros_like(weight_sum)
        acc[...] = jnp.zeros_like(acc)
        sums[...] = jnp.zeros_like(sums)
        near = ((3, False), (3, True), (1, False), (1, True))
        everything = [
            (q_refs[0], (0, False)),
            (q_refs[1], (0, True)),
            *zip(rest, near),
            *zip(kv_refs, places),
        ]
        small = 256
        for block_ref, place in everything:
            pltpu.sync_copy(block_ref, kv_scr.at[0])
            key_start = block_start(*place, rows)
            extra = kv_scr[0, rows : rows + 8, :].astype(F32)
            factor = extra[0:4] + extra[4:8]

            def absorb(at, carry, key_start=key_start, factor=factor):
                q = lax.div(at, rows // small)
                low = pl.multiple_of(lax.rem(at, rows // small) * small, small)
                here = pl.ds(low, small)
                query_start = jnp.where(q == 0, q_starts[0], q_starts[1]) + low
                for cut in range(rows // small):
                    keys = slice(cut * small, (cut + 1) * small)
                    scores = lax.dot_general(
                        q_scr[q, here, :], kv_scr[0, keys, :HEAD_DIM], NT, preferred_element_type=F32
                    )
                    key_pos = lax.broadcasted_iota(jnp.int32, scores.shape, 1) + (
                        key_start + cut * small
                    )
                    query_pos = lax.broadcasted_iota(jnp.int32, scores.shape, 0) + query_start
                    allowed = (key_pos < doc_len) & (key_pos != query_pos)
                    scores = jnp.where(allowed, scores * factor[cut : cut + 1], -1e30)
                    old = peak[q, here, :]
                    new = jnp.maximum(old, jnp.max(scores, axis=1, keepdims=True))
                    weights = jnp.where(allowed, jnp.exp2(scores - new[:, :1]), 0.0)
                    rescale = jnp.exp2(old - new)
                    peak[q, here, :] = new
                    weight_sum[q, here, :] = weight_sum[q, here, :] * rescale + jnp.sum(
                        weights, axis=1, keepdims=True
                    )
                    acc[q, here, :HEAD_DIM] = acc[q, here, :HEAD_DIM] * rescale + jnp.dot(
                        weights.astype(BF16), kv_scr[0, keys, HEAD_DIM:], preferred_element_type=F32
                    )
                return carry

            lax.fori_loop(0, 2 * rows // small, absorb, 0)
        for q in range(2):
            acc[q, :, HEAD_DIM:] = weight_sum[q]

    core = own_core()
    outs = []
    for q in range(2):
        total = acc[q] + (sums[0, q] + sums[1, q])
        inside = lax.broadcasted_iota(jnp.int32, (rows, HEAD_DIM), 0) + q_starts[q] < doc_len
        mixed = jnp.where(inside, total[:, :HEAD_DIM] / total[:, HEAD_DIM:], 0.0)
        ctx_scr[q] = mixed.astype(BF16).reshape(ctx_scr.shape[1:])
        block = core if q == 0 else 1 - core
        outs += start_all(
            [pltpu.make_async_copy(ctx_scr.at[q], out_ref.at[:, block], acc_sem.at[q])]
        )
    for copy in outs:
        copy.wait()


def attend(doc_length, queries, blocks, places, states, rest, name):
    rows = blocks[0].shape[0] - EXTRA
    count = len(blocks)
    first, last = queries is None, rest is not None
    out_shape = jax.ShapeDtypeStruct((2, rows, 2 * HEAD_DIM), F32)
    scratch = [
        pltpu.VMEM((count, rows + EXTRA, 2 * HEAD_DIM), BF16),
        pltpu.VMEM(out_shape.shape, F32),
        pltpu.SemaphoreType.DMA((count,)),
        pltpu.SemaphoreType.DMA((4,)),
    ]
    args = list(blocks)
    if not first:
        args = [*queries, *blocks]
        scratch.append(pltpu.VMEM((2, rows + EXTRA, HEAD_DIM), BF16))
    if last:
        args += [*states, *rest]
        scratch += [
            pltpu.VMEM((2, *out_shape.shape), F32),
            pltpu.SemaphoreType.DMA((2,)),
        ]
        out_shape = jax.ShapeDtypeStruct((4, 2, rows // 4, HEAD_DIM), BF16)
        scratch += [
            pltpu.VMEM((2, 4, rows // 4, HEAD_DIM), BF16),
            pltpu.VMEM((2, rows, HEAD_DIM), F32),
            pltpu.VMEM((2, rows, HEAD_DIM), F32),
        ]
    return pl.pallas_call(
        functools.partial(attend_kernel, places, first, last),
        in_specs=[SMEM] + [HBM] * len(args),
        out_specs=HBM,
        out_shape=out_shape,
        scratch_shapes=scratch,
        compiler_params=pltpu.CompilerParams(vmem_limit_bytes=VMEM),
        cost_estimate=pl.CostEstimate(
            flops=16 * rows * rows * count * HEAD_DIM,
            bytes_accessed=4 * 2**20,
            transcendentals=0,
        ),
        name=name,
    )(doc_length, *args)


def output_kernel(ctx_ref, got_ref, w_ref, w_got_ref, out_ref, left_scr, w_scr, out_scr, sem, out_sem):
    core = own_core()
    width = w_ref.shape[2]
    cuts = out_sem.shape[0]
    step = width // cuts
    lefts = start_all(
        [
            pltpu.make_async_copy(ctx_ref.at[:, core], left_scr.at[0], sem.at[2 * cuts]),
            pltpu.make_async_copy(got_ref.at[:, core], left_scr.at[1], sem.at[2 * cuts + 1]),
        ]
    )
    weights = []
    for i in range(cuts):
        cols = pl.ds(i * step, step)
        weights.append(
            start_all(
                [
                    pltpu.make_async_copy(ref.at[:, :, cols], w_scr.at[at, :, :, cols], sem.at[2 * i + at])
                    for at, ref in enumerate((w_ref, w_got_ref))
                ]
            )
        )
    for copy in lefts:
        copy.wait()
    left = jnp.concatenate([left_scr[at, y] for at in range(2) for y in range(4)], axis=1)
    outs = []
    for i in range(cuts):
        for copy in weights[i]:
            copy.wait()
        cols = slice(i * step, (i + 1) * step)
        right = w_scr[:, :, :, cols].reshape(8 * HEAD_DIM, step)
        part = jnp.dot(left, right, preferred_element_type=F32).astype(BF16)
        for j in range(step // 256):
            out_scr[i * (step // 256) + j] = part[:, j * 256 : (j + 1) * 256]
        mine = pl.ds(i * (step // 256), step // 256)
        outs += start_all(
            [pltpu.make_async_copy(out_scr.at[mine], out_ref.at[mine], out_sem.at[i])]
        )
    for copy in outs:
        copy.wait()


def output(context, got, weights, weights_got):
    rows = context.shape[2]
    width = weights.shape[2]
    cuts = 4
    out_shape = jax.ShapeDtypeStruct((8, rows, width // 8), BF16)
    return pl.pallas_call(
        output_kernel,
        in_specs=[HBM] * 4,
        out_specs=HBM,
        out_shape=out_shape,
        scratch_shapes=[
            pltpu.VMEM((2, 4, rows, HEAD_DIM), BF16),
            pltpu.VMEM((2, *weights.shape), BF16),
            pltpu.VMEM(out_shape.shape, BF16),
            pltpu.SemaphoreType.DMA((2 * cuts + 2,)),
            pltpu.SemaphoreType.DMA((cuts,)),
        ],
        compiler_params=pltpu.CompilerParams(vmem_limit_bytes=VMEM),
        cost_estimate=pl.CostEstimate(
            flops=2 * rows * width * 1024, bytes_accessed=6 * 2**20, transcendentals=0
        ),
        name="output",
    )(context, got, weights, weights_got)


def body(tokens, w_shared, w_value, w_output, doc_length):
    def move(array, by, cross):
        return lax.ppermute(
            array, "seq", [(i, (i // 2 + by) % 4 * 2 + (i % 2 ^ cross)) for i in range(8)]
        )

    own, given = project(tokens, w_shared, w_value)
    peer = move(given, 0, 1)
    own_left, peer_right = move(own, 1, 0), move(given, -1, 1)
    peer_left, own_right = move(given, 1, 1), move(own, -1, 0)

    y_groups = [[0, 1, 2, 3], [4, 5, 6, 7]]
    weights = lax.all_to_all(
        spread(w_output, peer), "head", 0, 0, axis_index_groups=y_groups, tiled=True
    )

    queries = (own, peer)
    here = attend(doc_length, None, queries, ((0, False), (0, True)), None, None, "attend_here")
    own_left, peer_right, here = lax.optimization_barrier((own_left, peer_right, here))
    own_far, peer_far = move(own_left, 1, 0), move(peer_right, -1, 0)
    blocks = (own_left, peer_left, own_right, peer_right)
    near = attend(
        doc_length,
        queries,
        blocks,
        ((3, False), (3, True), (1, False), (1, True)),
        None,
        None,
        "attend_near",
    )
    weights, near = lax.optimization_barrier((weights, near))
    weights_got = move(weights, 0, 1)
    context = attend(
        doc_length,
        queries,
        (own_far, peer_far),
        ((2, False), (2, True)),
        (here, near),
        blocks,
        "attend_far",
    )
    context = lax.all_to_all(context, "head", 0, 0, axis_index_groups=y_groups, tiled=True)
    terms = output(context, move(context, 0, 1), weights, weights_got)
    terms = lax.all_to_all(terms, "head", 0, 0, tiled=True).astype(F32)
    result = (terms[:4] + terms[4:]).astype(BF16)
    return result.reshape(tokens.shape[0], result.shape[-1])


def solution(mesh):
    placed = (
        P(("batch", "seq"), None),
        P(None, "head"),
        P(None, "head"),
        P("head", None),
        P("batch"),
    )
    return jax.shard_map(
        body, mesh=mesh, in_specs=placed, out_specs=P(("batch", "seq"), "head"), check_vma=False
    )
```

```python
import functools
import math

import jax
import jax.numpy as jnp
from jax import lax
from jax.experimental import pallas as pl
from jax.experimental.pallas import tpu as pltpu
from jax.sharding import PartitionSpec as P

HEAD_DIM = 128
LOG2E = 1.4426950408889634
NORM_LIMIT = 60.0
EXTRA = 16
NT = (((1,), (1,)), ((), ()))
VMEM = 30 * 2**20
HBM = pl.BlockSpec(memory_space=pltpu.HBM)
HERE = pl.BlockSpec(memory_space=pltpu.VMEM)
SMEM = pl.BlockSpec(memory_space=pltpu.SMEM)
F32 = jnp.float32
BF16 = jnp.bfloat16


def own_core():
    return lax.rem(lax.axis_index("seq"), 2)


def block_start(by, other, rows):
    seq = lax.axis_index("seq")
    place = lax.rem(lax.div(seq, 2) + by, 4) * 2
    core = lax.rem(seq, 2)
    return (place + (1 - core if other else core)) * rows


def start_all(copies):
    for copy in copies:
        copy.start()
    return copies


def project_kernel(x_ref, ws_ref, wv_ref, own_ref, given_ref, x_scr, ws_scr, wv_scr, sem):
    rows, _ = x_ref.shape
    cuts = x_scr.shape[0]
    step = rows // cuts
    weights = start_all(
        [
            pltpu.make_async_copy(ws_ref, ws_scr, sem.at[0]),
            pltpu.make_async_copy(wv_ref, wv_scr, sem.at[1]),
        ]
    )
    tokens = start_all(
        [
            pltpu.make_async_copy(x_ref.at[pl.ds(i * step, step)], x_scr.at[i], sem.at[2 + i])
            for i in range(cuts)
        ]
    )
    wide = 2 * HEAD_DIM
    row = lax.broadcasted_iota(jnp.int32, (EXTRA, wide), 0)
    extra = [jnp.zeros((EXTRA, wide), F32) for _ in range(2)]
    largest = [jnp.zeros((8, wide), F32) for _ in range(2)]
    ones = jnp.ones((8, HEAD_DIM), BF16)
    mine = own_core() == 0

    def put(here, cols, heads):
        own_ref[here, cols] = jnp.where(mine, heads[0], heads[1])
        given_ref[here, cols] = jnp.where(mine, heads[1], heads[0])

    for copy in weights:
        copy.wait()
    for i in range(cuts):
        tokens[i].wait()
        x = x_scr[i]
        shared = jnp.dot(x, ws_scr[...], preferred_element_type=F32).astype(BF16)
        values = jnp.dot(x, wv_scr[...], preferred_element_type=F32).astype(BF16)
        here = slice(i * step, (i + 1) * step)
        put(here, slice(0, HEAD_DIM), (shared[:, :HEAD_DIM], shared[:, HEAD_DIM:]))
        put(here, slice(HEAD_DIM, wide), (values[:, :HEAD_DIM], values[:, HEAD_DIM:]))
        for h in range(2):
            keys = shared[:, h * HEAD_DIM : (h + 1) * HEAD_DIM].astype(F32)
            square = keys * keys
            high = square.astype(BF16)
            low = (square - high.astype(F32)).astype(BF16)
            total = lax.dot_general(ones, high, NT, preferred_element_type=F32)
            total += lax.dot_general(ones, low, NT, preferred_element_type=F32)
            largest[h] = jnp.maximum(largest[h], total)
            factor = lax.rsqrt(total / HEAD_DIM + 1e-06) * (LOG2E / math.sqrt(HEAD_DIM))
            first = factor.astype(BF16).astype(F32)
            extra[h] = jnp.where(row == i, jnp.concatenate([first] * 2), extra[h])
            extra[h] = jnp.where(row == 4 + i, jnp.concatenate([factor - first] * 2), extra[h])
    for h in range(2):
        top = jnp.broadcast_to(jnp.max(largest[h]), (EXTRA, wide))
        extra[h] = jnp.where(row >= 8, top, extra[h])
    last = slice(rows, rows + EXTRA)
    put(last, slice(0, wide), [e.astype(BF16) for e in extra])


def project(tokens, w_shared, w_value):
    rows, width = tokens.shape
    cuts = 4
    out = jax.ShapeDtypeStruct((rows + EXTRA, 2 * HEAD_DIM), BF16)
    return pl.pallas_call(
        project_kernel,
        in_specs=[HBM] * 3,
        out_specs=(HERE, HERE),
        out_shape=(out, out),
        scratch_shapes=[
            pltpu.VMEM((cuts, rows // cuts, width), BF16),
            pltpu.VMEM(w_shared.shape, BF16),
            pltpu.VMEM(w_value.shape, BF16),
            pltpu.SemaphoreType.DMA((2 + cuts,)),
        ],
        compiler_params=pltpu.CompilerParams(vmem_limit_bytes=56 * 2**20),
        cost_estimate=pl.CostEstimate(
            flops=2 * rows * width * 512, bytes_accessed=7 * 2**20, transcendentals=0
        ),
        name="project",
    )(tokens, w_shared, w_value)


def spread_kernel(w_ref, after_ref, out_ref):
    del after_ref
    mine = w_ref[pl.ds(pl.multiple_of(own_core() * HEAD_DIM, HEAD_DIM), HEAD_DIM), :]
    for i in range(4):
        out_ref[i] = mine


def spread(w_output, after):
    return pl.pallas_call(
        spread_kernel,
        in_specs=[HERE] * 2,
        out_specs=HERE,
        out_shape=jax.ShapeDtypeStruct((4, HEAD_DIM, w_output.shape[1]), BF16),
        compiler_params=pltpu.CompilerParams(vmem_limit_bytes=VMEM),
        name="spread",
    )(w_output, after)


def attend_kernel(places, first, last, doc_ref, *refs):
    count = len(places)
    if first:
        kv_refs, out_ref = refs[:count], refs[count]
        q_refs = kv_refs
        acc = out_ref
    else:
        q_refs, kv_refs, refs = refs[:2], refs[2 : 2 + count], refs[2 + count :]
        if last:
            sums, rest, refs = refs[:2], refs[2:6], refs[6:]
            out_ref, acc, peak, weight_sum = refs
        else:
            (out_ref,) = refs
            acc = out_ref
    rows = kv_refs[0].shape[0] - EXTRA
    tile = 512
    acc[...] = jnp.zeros_like(acc)
    doc_len = doc_ref[0]
    q_starts = [block_start(0, other, rows) for other in (False, True)]
    active = jnp.minimum(q_starts[0], q_starts[1]) < doc_len
    for i in range(count):
        kv_ref = kv_refs[i]
        start = block_start(*places[i], rows)

        @pl.when(active & (start < doc_len))
        def _(i=i, kv_ref=kv_ref, start=start):
            extra = kv_ref[rows : rows + 8, :].astype(F32)
            factor = extra[0:4] + extra[4:8]
            for q in range(2):
                queries = q_refs[q][:rows, :HEAD_DIM]
                total = acc[q]
                for cut in range(rows // tile):
                    keys = slice(cut * tile, (cut + 1) * tile)
                    each = tile // 256
                    scale = jnp.concatenate(
                        [factor[cut * each + j : cut * each + j + 1] for j in range(each)], axis=1
                    )
                    place = lax.broadcasted_iota(jnp.int32, (1, tile), 1) + (start + cut * tile)
                    bias = jnp.where(place < doc_len, 0.0, -1e30)
                    scores = lax.dot_general(
                        queries, kv_ref[keys, :HEAD_DIM], NT, preferred_element_type=F32
                    )
                    weights = jnp.exp2(scores * scale + bias)
                    if first and i == q:
                        weights = jnp.where(
                            lax.broadcasted_iota(jnp.int32, weights.shape, 0)
                            == lax.broadcasted_iota(jnp.int32, weights.shape, 1) + cut * tile,
                            0.0,
                            weights,
                        )
                    values = jnp.concatenate(
                        [kv_ref[keys, HEAD_DIM:], jnp.ones((tile, HEAD_DIM), BF16)], axis=1
                    )
                    total += jnp.dot(weights.astype(BF16), values, preferred_element_type=F32)
                acc[q] = total

    if not last:
        return

    for at in range(2):
        acc[...] += sums[at][...]
    norm = jnp.maximum(
        jnp.max(q_refs[0][rows + 8 :, :].astype(F32)), jnp.max(q_refs[1][rows + 8 :, :].astype(F32))
    )

    @pl.when(norm > NORM_LIMIT**2)
    def _():
        peak[...] = jnp.full_like(peak, -1e30)
        weight_sum[...] = jnp.zeros_like(weight_sum)
        acc[...] = jnp.zeros_like(acc)
        near = ((3, False), (3, True), (1, False), (1, True))
        everything = [
            (q_refs[0], (0, False)),
            (q_refs[1], (0, True)),
            *zip(rest, near),
            *zip(kv_refs, places),
        ]
        small = 256
        for block_ref, place in everything:
            key_start = block_start(*place, rows)
            extra = block_ref[rows : rows + 8, :].astype(F32)
            factor = extra[0:4] + extra[4:8]

            def absorb(at, carry, q, block_ref=block_ref, key_start=key_start, factor=factor):
                low = pl.multiple_of(at * small, small)
                here = pl.ds(low, small)
                query_start = q_starts[q] + low
                for cut in range(rows // small):
                    keys = slice(cut * small, (cut + 1) * small)
                    scores = lax.dot_general(
                        q_refs[q][here, :HEAD_DIM],
                        block_ref[keys, :HEAD_DIM],
                        NT,
                        preferred_element_type=F32,
                    )
                    key_pos = lax.broadcasted_iota(jnp.int32, scores.shape, 1) + (
                        key_start + cut * small
                    )
                    query_pos = lax.broadcasted_iota(jnp.int32, scores.shape, 0) + query_start
                    allowed = (key_pos < doc_len) & (key_pos != query_pos)
                    scores = jnp.where(allowed, scores * factor[cut : cut + 1], -1e30)
                    old = peak[q, here, :]
                    new = jnp.maximum(old, jnp.max(scores, axis=1, keepdims=True))
                    weights = jnp.where(allowed, jnp.exp2(scores - new[:, :1]), 0.0)
                    rescale = jnp.exp2(old - new)
                    peak[q, here, :] = new
                    weight_sum[q, here, :] = weight_sum[q, here, :] * rescale + jnp.sum(
                        weights, axis=1, keepdims=True
                    )
                    acc[q, here, :HEAD_DIM] = acc[q, here, :HEAD_DIM] * rescale + jnp.dot(
                        weights.astype(BF16), block_ref[keys, HEAD_DIM:], preferred_element_type=F32
                    )
                return carry

            for q in range(2):
                lax.fori_loop(0, rows // small, functools.partial(absorb, q=q), 0)
        for q in range(2):
            acc[q, :, HEAD_DIM:] = weight_sum[q]

    core = own_core()
    for q in range(2):
        total = acc[q]
        inside = lax.broadcasted_iota(jnp.int32, (rows, HEAD_DIM), 0) + q_starts[q] < doc_len
        mixed = jnp.where(inside, total[:, :HEAD_DIM] / total[:, HEAD_DIM:], 0.0)
        block = core if q == 0 else 1 - core
        out_ref[:, block] = mixed.astype(BF16).reshape(4, rows // 4, HEAD_DIM)


def attend(doc_length, queries, blocks, places, states, rest, name):
    rows = blocks[0].shape[0] - EXTRA
    count = len(blocks)
    first, last = queries is None, rest is not None
    out_shape = jax.ShapeDtypeStruct((2, rows, 2 * HEAD_DIM), F32)
    args = list(blocks)
    scratch = []
    if not first:
        args = [*queries, *blocks]
    if last:
        args += [*states, *rest]
        scratch = [
            pltpu.VMEM(out_shape.shape, F32),
            pltpu.VMEM((2, rows, HEAD_DIM), F32),
            pltpu.VMEM((2, rows, HEAD_DIM), F32),
        ]
        out_shape = jax.ShapeDtypeStruct((4, 2, rows // 4, HEAD_DIM), BF16)
    return pl.pallas_call(
        functools.partial(attend_kernel, places, first, last),
        in_specs=[SMEM] + [HERE] * len(args),
        out_specs=HERE,
        out_shape=out_shape,
        scratch_shapes=scratch,
        compiler_params=pltpu.CompilerParams(vmem_limit_bytes=VMEM),
        cost_estimate=pl.CostEstimate(
            flops=16 * rows * rows * count * HEAD_DIM,
            bytes_accessed=4 * 2**20,
            transcendentals=0,
        ),
        name=name,
    )(doc_length, *args)


def output_kernel(ctx_ref, got_ref, w_ref, w_got_ref, out_ref):
    core = own_core()
    lefts = [
        jnp.concatenate([ref[y, core] for y in range(4)], axis=1) for ref in (ctx_ref, got_ref)
    ]
    width = w_ref.shape[2]
    step = width // 8
    for i in range(8):
        cols = slice(i * step, (i + 1) * step)
        part = None
        for left, ref in zip(lefts, (w_ref, w_got_ref)):
            right = ref[:, :, cols].reshape(4 * HEAD_DIM, step)
            term = jnp.dot(left, right, preferred_element_type=F32)
            part = term if part is None else part + term
        out_ref[i] = part.astype(BF16)


def output(context, got, weights, weights_got):
    rows = context.shape[2]
    width = weights.shape[2]
    return pl.pallas_call(
        output_kernel,
        in_specs=[HERE] * 4,
        out_specs=HERE,
        out_shape=jax.ShapeDtypeStruct((8, rows, width // 8), BF16),
        compiler_params=pltpu.CompilerParams(vmem_limit_bytes=VMEM),
        cost_estimate=pl.CostEstimate(
            flops=2 * rows * width * 1024, bytes_accessed=6 * 2**20, transcendentals=0
        ),
        name="output",
    )(context, got, weights, weights_got)


def body(tokens, w_shared, w_value, w_output, doc_length):
    def move(array, by, cross):
        return lax.ppermute(
            array, "seq", [(i, (i // 2 + by) % 4 * 2 + (i % 2 ^ cross)) for i in range(8)]
        )

    own, given = project(tokens, w_shared, w_value)
    peer = move(given, 0, 1)
    own_left, peer_right = move(own, 1, 0), move(given, -1, 1)
    peer_left, own_right = move(given, 1, 1), move(own, -1, 0)

    y_groups = [[0, 1, 2, 3], [4, 5, 6, 7]]
    queries = (own, peer)
    here = attend(doc_length, None, queries, ((0, False), (0, True)), None, None, "attend_here")
    weights = lax.all_to_all(
        spread(w_output, here), "head", 0, 0, axis_index_groups=y_groups, tiled=True
    )
    weights_got = move(weights, 0, 1)
    own_left, peer_right, here = lax.optimization_barrier((own_left, peer_right, here))
    own_far, peer_far = move(own_left, 1, 0), move(peer_right, -1, 0)
    blocks = (own_left, peer_left, own_right, peer_right)
    near = attend(
        doc_length,
        queries,
        blocks,
        ((3, False), (3, True), (1, False), (1, True)),
        None,
        None,
        "attend_near",
    )
    context = attend(
        doc_length,
        queries,
        (own_far, peer_far),
        ((2, False), (2, True)),
        (here, near),
        blocks,
        "attend_far",
    )
    context = lax.all_to_all(context, "head", 0, 0, axis_index_groups=y_groups, tiled=True)
    terms = output(context, move(context, 0, 1), weights, weights_got)
    terms = lax.all_to_all(terms, "head", 0, 0, tiled=True).astype(F32)
    result = (terms[:4] + terms[4:]).astype(BF16)
    return result.reshape(tokens.shape[0], result.shape[-1])


def solution(mesh):
    placed = (
        P(("batch", "seq"), None),
        P(None, "head"),
        P(None, "head"),
        P("head", None),
        P("batch"),
    )
    return jax.shard_map(
        body, mesh=mesh, in_specs=placed, out_specs=P(("batch", "seq"), "head"), check_vma=False
    )
```

```python
import functools
import math

import jax
import jax.numpy as jnp
from jax import lax
from jax.experimental import pallas as pl
from jax.experimental.pallas import tpu as pltpu
from jax.sharding import PartitionSpec as P

HEAD_DIM = 128
LOG2E = 1.4426950408889634
NORM_LIMIT = 60.0
EXTRA = 16
NT = (((1,), (1,)), ((), ()))
VMEM = 30 * 2**20
ANY = pl.BlockSpec(memory_space=pl.ANY)
HERE = pl.BlockSpec(memory_space=pltpu.VMEM)
SMEM = pl.BlockSpec(memory_space=pltpu.SMEM)
F32 = jnp.float32
BF16 = jnp.bfloat16


def own_core():
    return lax.rem(lax.axis_index("seq"), 2)


def block_start(by, other, rows):
    seq = lax.axis_index("seq")
    place = lax.rem(lax.div(seq, 2) + by, 4) * 2
    core = lax.rem(seq, 2)
    return (place + (1 - core if other else core)) * rows


def start_all(copies):
    for copy in copies:
        copy.start()
    return copies


def project_kernel(x_ref, ws_ref, wv_ref, own_ref, given_ref, x_scr, ws_scr, wv_scr, sem):
    rows, _ = x_ref.shape
    cuts = x_scr.shape[0]
    step = rows // cuts
    weights = start_all(
        [
            pltpu.make_async_copy(ws_ref, ws_scr, sem.at[0]),
            pltpu.make_async_copy(wv_ref, wv_scr, sem.at[1]),
        ]
    )
    tokens = start_all(
        [
            pltpu.make_async_copy(x_ref.at[pl.ds(i * step, step)], x_scr.at[i], sem.at[2 + i])
            for i in range(cuts)
        ]
    )
    wide = 2 * HEAD_DIM
    row = lax.broadcasted_iota(jnp.int32, (EXTRA, wide), 0)
    extra = [jnp.zeros((EXTRA, wide), F32) for _ in range(2)]
    largest = [jnp.zeros((8, wide), F32) for _ in range(2)]
    ones = jnp.ones((8, HEAD_DIM), BF16)
    mine = own_core() == 0

    def put(here, cols, heads):
        own_ref[here, cols] = jnp.where(mine, heads[0], heads[1])
        given_ref[here, cols] = jnp.where(mine, heads[1], heads[0])

    for copy in weights:
        copy.wait()
    for i in range(cuts):
        tokens[i].wait()
        x = x_scr[i]
        shared = jnp.dot(x, ws_scr[...], preferred_element_type=F32).astype(BF16)
        values = jnp.dot(x, wv_scr[...], preferred_element_type=F32).astype(BF16)
        here = slice(i * step, (i + 1) * step)
        put(here, slice(0, HEAD_DIM), (shared[:, :HEAD_DIM], shared[:, HEAD_DIM:]))
        put(here, slice(HEAD_DIM, wide), (values[:, :HEAD_DIM], values[:, HEAD_DIM:]))
        for h in range(2):
            keys = shared[:, h * HEAD_DIM : (h + 1) * HEAD_DIM].astype(F32)
            square = keys * keys
            high = square.astype(BF16)
            low = (square - high.astype(F32)).astype(BF16)
            total = lax.dot_general(ones, high, NT, preferred_element_type=F32)
            total += lax.dot_general(ones, low, NT, preferred_element_type=F32)
            largest[h] = jnp.maximum(largest[h], total)
            factor = lax.rsqrt(total / HEAD_DIM + 1e-06) * (LOG2E / math.sqrt(HEAD_DIM))
            first = factor.astype(BF16).astype(F32)
            extra[h] = jnp.where(row == i, jnp.concatenate([first] * 2), extra[h])
            extra[h] = jnp.where(row == 4 + i, jnp.concatenate([factor - first] * 2), extra[h])
    for h in range(2):
        top = jnp.broadcast_to(jnp.max(largest[h]), (EXTRA, wide))
        extra[h] = jnp.where(row >= 8, top, extra[h])
    last = slice(rows, rows + EXTRA)
    put(last, slice(0, wide), [e.astype(BF16) for e in extra])


def project(tokens, w_shared, w_value):
    rows, width = tokens.shape
    cuts = 4
    out = jax.ShapeDtypeStruct((rows + EXTRA, 2 * HEAD_DIM), BF16)
    return pl.pallas_call(
        project_kernel,
        in_specs=[ANY] * 3,
        out_specs=(HERE, HERE),
        out_shape=(out, out),
        scratch_shapes=[
            pltpu.VMEM((cuts, rows // cuts, width), BF16),
            pltpu.VMEM(w_shared.shape, BF16),
            pltpu.VMEM(w_value.shape, BF16),
            pltpu.SemaphoreType.DMA((2 + cuts,)),
        ],
        compiler_params=pltpu.CompilerParams(vmem_limit_bytes=63 * 2**20),
        cost_estimate=pl.CostEstimate(
            flops=2 * rows * width * 512, bytes_accessed=7 * 2**20, transcendentals=0
        ),
        name="project",
    )(tokens, w_shared, w_value)


def spread_kernel(w_ref, after_ref, out_ref, scr, sem):
    del after_ref
    mine = w_ref.at[pl.ds(pl.multiple_of(own_core() * HEAD_DIM, HEAD_DIM), HEAD_DIM)]
    pltpu.sync_copy(mine, scr)
    for copy in start_all(
        [pltpu.make_async_copy(scr, out_ref.at[i], sem.at[i]) for i in range(4)]
    ):
        copy.wait()


def spread(w_output, after):
    piece = (HEAD_DIM, w_output.shape[1])
    return pl.pallas_call(
        spread_kernel,
        in_specs=[ANY] * 2,
        out_specs=ANY,
        out_shape=jax.ShapeDtypeStruct((4, *piece), BF16),
        scratch_shapes=[pltpu.VMEM(piece, BF16), pltpu.SemaphoreType.DMA((4,))],
        compiler_params=pltpu.CompilerParams(vmem_limit_bytes=63 * 2**20),
        name="spread",
    )(w_output, after)


def attend_kernel(places, first, last, doc_ref, *refs):
    count = len(places)
    if first:
        kv_refs, refs = refs[:count], refs[count:]
        out_ref, kv_scr, acc, sem, acc_sem = refs
        q_of = lambda q: kv_scr[q, :-EXTRA, :HEAD_DIM]
        copies = []
    else:
        q_refs, kv_refs, refs = refs[:2], refs[2 : 2 + count], refs[2 + count :]
        if last:
            states, rest, refs = refs[:2], refs[2:6], refs[6:]
            out_ref, kv_scr, acc, sem, acc_sem, q_scr, sums, sums_sem, peak, weight_sum = refs
        else:
            out_ref, kv_scr, acc, sem, acc_sem, q_scr = refs
        q_of = lambda q: q_scr[q, :-EXTRA, :]
        copies = start_all(
            [
                pltpu.make_async_copy(q_refs[q].at[:, pl.ds(0, HEAD_DIM)], q_scr.at[q], acc_sem.at[2 + q])
                for q in range(2)
            ]
        )
    rows = kv_scr.shape[1] - EXTRA
    tile = 512
    blocks = start_all(
        [pltpu.make_async_copy(kv_refs[i], kv_scr.at[i], sem.at[i]) for i in range(count)]
    )
    if last:
        added = start_all(
            [pltpu.make_async_copy(states[i], sums.at[i], sums_sem.at[i]) for i in range(2)]
        )
    acc[...] = jnp.zeros_like(acc)
    for copy in copies:
        copy.wait()
    doc_len = doc_ref[0]
    q_starts = [block_start(0, other, rows) for other in (False, True)]
    active = jnp.minimum(q_starts[0], q_starts[1]) < doc_len
    if first:
        for copy in blocks:
            copy.wait()
    for i in range(count):
        if not first:
            blocks[i].wait()
        start = block_start(*places[i], rows)

        @pl.when(active & (start < doc_len))
        def _(i=i, start=start):
            extra = kv_scr[i, rows : rows + 8, :].astype(F32)
            factor = extra[0:4] + extra[4:8]
            for q in range(2):
                queries = q_of(q)
                total = acc[q]
                for cut in range(rows // tile):
                    keys = slice(cut * tile, (cut + 1) * tile)
                    each = tile // 256
                    scale = jnp.concatenate(
                        [factor[cut * each + j : cut * each + j + 1] for j in range(each)], axis=1
                    )
                    place = lax.broadcasted_iota(jnp.int32, (1, tile), 1) + (start + cut * tile)
                    bias = jnp.where(place < doc_len, 0.0, -1e30)
                    scores = lax.dot_general(
                        queries, kv_scr[i, keys, :HEAD_DIM], NT, preferred_element_type=F32
                    )
                    weights = jnp.exp2(scores * scale + bias)
                    if first and i == q:
                        weights = jnp.where(
                            lax.broadcasted_iota(jnp.int32, weights.shape, 0)
                            == lax.broadcasted_iota(jnp.int32, weights.shape, 1) + cut * tile,
                            0.0,
                            weights,
                        )
                    values = jnp.concatenate(
                        [kv_scr[i, keys, HEAD_DIM:], jnp.ones((tile, HEAD_DIM), BF16)], axis=1
                    )
                    total += jnp.dot(weights.astype(BF16), values, preferred_element_type=F32)
                acc[q] = total

    if not last:
        for copy in start_all(
            [pltpu.make_async_copy(acc.at[q], out_ref.at[q], acc_sem.at[q]) for q in range(2)]
        ):
            copy.wait()
        return

    for copy in added:
        copy.wait()
    norm = jnp.maximum(
        jnp.max(q_scr[0, rows + 8 :, :].astype(F32)), jnp.max(q_scr[1, rows + 8 :, :].astype(F32))
    )

    @pl.when(norm > NORM_LIMIT**2)
    def _():
        peak[...] = jnp.full_like(peak, -1e30)
        weight_sum[...] = jnp.zeros_like(weight_sum)
        acc[...] = jnp.zeros_like(acc)
        sums[...] = jnp.zeros_like(sums)
        near = ((3, False), (3, True), (1, False), (1, True))
        everything = [
            (q_refs[0], (0, False)),
            (q_refs[1], (0, True)),
            *zip(rest, near),
            *zip(kv_refs, places),
        ]
        small = 256
        for block_ref, place in everything:
            pltpu.sync_copy(block_ref, kv_scr.at[0])
            key_start = block_start(*place, rows)
            extra = kv_scr[0, rows : rows + 8, :].astype(F32)
            factor = extra[0:4] + extra[4:8]

            def absorb(at, carry, key_start=key_start, factor=factor):
                q = lax.div(at, rows // small)
                low = pl.multiple_of(lax.rem(at, rows // small) * small, small)
                here = pl.ds(low, small)
                query_start = jnp.where(q == 0, q_starts[0], q_starts[1]) + low
                for cut in range(rows // small):
                    keys = slice(cut * small, (cut + 1) * small)
                    scores = lax.dot_general(
                        q_scr[q, here, :], kv_scr[0, keys, :HEAD_DIM], NT, preferred_element_type=F32
                    )
                    key_pos = lax.broadcasted_iota(jnp.int32, scores.shape, 1) + (
                        key_start + cut * small
                    )
                    query_pos = lax.broadcasted_iota(jnp.int32, scores.shape, 0) + query_start
                    allowed = (key_pos < doc_len) & (key_pos != query_pos)
                    scores = jnp.where(allowed, scores * factor[cut : cut + 1], -1e30)
                    old = peak[q, here, :]
                    new = jnp.maximum(old, jnp.max(scores, axis=1, keepdims=True))
                    weights = jnp.where(allowed, jnp.exp2(scores - new[:, :1]), 0.0)
                    rescale = jnp.exp2(old - new)
                    peak[q, here, :] = new
                    weight_sum[q, here, :] = weight_sum[q, here, :] * rescale + jnp.sum(
                        weights, axis=1, keepdims=True
                    )
                    acc[q, here, :HEAD_DIM] = acc[q, here, :HEAD_DIM] * rescale + jnp.dot(
                        weights.astype(BF16), kv_scr[0, keys, HEAD_DIM:], preferred_element_type=F32
                    )
                return carry

            lax.fori_loop(0, 2 * rows // small, absorb, 0)
        for q in range(2):
            acc[q, :, HEAD_DIM:] = weight_sum[q]

    core = own_core()
    for q in range(2):
        total = acc[q] + (sums[0, q] + sums[1, q])
        inside = lax.broadcasted_iota(jnp.int32, (rows, HEAD_DIM), 0) + q_starts[q] < doc_len
        mixed = jnp.where(inside, total[:, :HEAD_DIM] / total[:, HEAD_DIM:], 0.0)
        block = core if q == 0 else 1 - core
        out_ref[:, block] = mixed.astype(BF16).reshape(4, rows // 4, HEAD_DIM)


def attend(doc_length, queries, blocks, places, states, rest, name):
    rows = blocks[0].shape[0] - EXTRA
    count = len(blocks)
    first, last = queries is None, rest is not None
    out_shape = jax.ShapeDtypeStruct((2, rows, 2 * HEAD_DIM), F32)
    scratch = [
        pltpu.VMEM((count, rows + EXTRA, 2 * HEAD_DIM), BF16),
        pltpu.VMEM(out_shape.shape, F32),
        pltpu.SemaphoreType.DMA((count,)),
        pltpu.SemaphoreType.DMA((4,)),
    ]
    args = list(blocks)
    if not first:
        args = [*queries, *blocks]
        scratch.append(pltpu.VMEM((2, rows + EXTRA, HEAD_DIM), BF16))
    if last:
        args += [*states, *rest]
        scratch += [
            pltpu.VMEM((2, *out_shape.shape), F32),
            pltpu.SemaphoreType.DMA((2,)),
        ]
        out_shape = jax.ShapeDtypeStruct((4, 2, rows // 4, HEAD_DIM), BF16)
        scratch += [
            pltpu.VMEM((2, rows, HEAD_DIM), F32),
            pltpu.VMEM((2, rows, HEAD_DIM), F32),
        ]
    return pl.pallas_call(
        functools.partial(attend_kernel, places, first, last),
        in_specs=[SMEM] + [ANY] * len(args),
        out_specs=HERE if last else ANY,
        out_shape=out_shape,
        scratch_shapes=scratch,
        compiler_params=pltpu.CompilerParams(vmem_limit_bytes=63 * 2**20),
        cost_estimate=pl.CostEstimate(
            flops=16 * rows * rows * count * HEAD_DIM,
            bytes_accessed=4 * 2**20,
            transcendentals=0,
        ),
        name=name,
    )(doc_length, *args)


def output_kernel(ctx_ref, got_ref, w_ref, w_got_ref, out_ref):
    core = own_core()
    lefts = [
        jnp.concatenate([ref[y, core] for y in range(4)], axis=1) for ref in (ctx_ref, got_ref)
    ]
    width = w_ref.shape[2]
    step = width // 8
    for i in range(8):
        cols = slice(i * step, (i + 1) * step)
        part = None
        for left, ref in zip(lefts, (w_ref, w_got_ref)):
            right = ref[:, :, cols].reshape(4 * HEAD_DIM, step)
            term = jnp.dot(left, right, preferred_element_type=F32)
            part = term if part is None else part + term
        out_ref[i] = part.astype(BF16)


def output(context, got, weights, weights_got):
    rows = context.shape[2]
    width = weights.shape[2]
    return pl.pallas_call(
        output_kernel,
        in_specs=[HERE] * 4,
        out_specs=HERE,
        out_shape=jax.ShapeDtypeStruct((8, rows, width // 8), BF16),
        compiler_params=pltpu.CompilerParams(vmem_limit_bytes=VMEM),
        cost_estimate=pl.CostEstimate(
            flops=2 * rows * width * 1024, bytes_accessed=6 * 2**20, transcendentals=0
        ),
        name="output",
    )(context, got, weights, weights_got)


def body(tokens, w_shared, w_value, w_output, doc_length):
    def move(array, by, cross):
        return lax.ppermute(
            array, "seq", [(i, (i // 2 + by) % 4 * 2 + (i % 2 ^ cross)) for i in range(8)]
        )

    own, given = project(tokens, w_shared, w_value)
    peer = move(given, 0, 1)
    own_left, peer_right = move(own, 1, 0), move(given, -1, 1)
    peer_left, own_right = move(given, 1, 1), move(own, -1, 0)

    y_groups = [[0, 1, 2, 3], [4, 5, 6, 7]]
    queries = (own, peer)
    here = attend(doc_length, None, queries, ((0, False), (0, True)), None, None, "attend_here")
    weights = lax.all_to_all(
        spread(w_output, here), "head", 0, 0, axis_index_groups=y_groups, tiled=True
    )
    own_left, peer_right, here = lax.optimization_barrier((own_left, peer_right, here))
    own_far, peer_far = move(own_left, 1, 0), move(peer_right, -1, 0)
    blocks = (own_left, peer_left, own_right, peer_right)
    near = attend(
        doc_length,
        queries,
        blocks,
        ((3, False), (3, True), (1, False), (1, True)),
        None,
        None,
        "attend_near",
    )
    context = attend(
        doc_length,
        queries,
        (own_far, peer_far),
        ((2, False), (2, True)),
        (here, near),
        blocks,
        "attend_far",
    )
    weights, context = lax.optimization_barrier((weights, context))
    weights_got = move(weights, 0, 1)
    context = lax.all_to_all(context, "head", 0, 0, axis_index_groups=y_groups, tiled=True)
    terms = output(context, move(context, 0, 1), weights, weights_got)
    terms = lax.all_to_all(terms, "head", 0, 0, tiled=True).astype(F32)
    result = (terms[:4] + terms[4:]).astype(BF16)
    return result.reshape(tokens.shape[0], result.shape[-1])


def solution(mesh):
    placed = (
        P(("batch", "seq"), None),
        P(None, "head"),
        P(None, "head"),
        P("head", None),
        P("batch"),
    )
    return jax.shard_map(
        body, mesh=mesh, in_specs=placed, out_specs=P(("batch", "seq"), "head"), check_vma=False
    )
```

```python
import functools
import math

import jax
import jax.numpy as jnp
from jax import lax
from jax.experimental import pallas as pl
from jax.experimental.pallas import tpu as pltpu
from jax.sharding import PartitionSpec as P

HEAD_DIM = 128
LOG2E = 1.4426950408889634
NORM_LIMIT = 60.0
EXTRA = 16
NT = (((1,), (1,)), ((), ()))
VMEM = 30 * 2**20
ANY = pl.BlockSpec(memory_space=pl.ANY)
HERE = pl.BlockSpec(memory_space=pltpu.VMEM)
SMEM = pl.BlockSpec(memory_space=pltpu.SMEM)
F32 = jnp.float32
BF16 = jnp.bfloat16


def own_core():
    return lax.rem(lax.axis_index("seq"), 2)


def block_start(by, other, rows):
    seq = lax.axis_index("seq")
    place = lax.rem(lax.div(seq, 2) + by, 4) * 2
    core = lax.rem(seq, 2)
    return (place + (1 - core if other else core)) * rows


def start_all(copies):
    for copy in copies:
        copy.start()
    return copies


def project_kernel(x_ref, ws_ref, wv_ref, own_ref, given_ref, x_scr, ws_scr, wv_scr, sem):
    rows, _ = x_ref.shape
    cuts = x_scr.shape[0]
    step = rows // cuts
    weights = start_all(
        [
            pltpu.make_async_copy(ws_ref, ws_scr, sem.at[0]),
            pltpu.make_async_copy(wv_ref, wv_scr, sem.at[1]),
        ]
    )
    tokens = start_all(
        [
            pltpu.make_async_copy(x_ref.at[pl.ds(i * step, step)], x_scr.at[i], sem.at[2 + i])
            for i in range(cuts)
        ]
    )
    wide = 2 * HEAD_DIM
    row = lax.broadcasted_iota(jnp.int32, (EXTRA, wide), 0)
    extra = [jnp.zeros((EXTRA, wide), F32) for _ in range(2)]
    largest = [jnp.zeros((8, wide), F32) for _ in range(2)]
    ones = jnp.ones((8, HEAD_DIM), BF16)
    mine = own_core() == 0

    def put(here, cols, heads):
        own_ref[here, cols] = jnp.where(mine, heads[0], heads[1])
        given_ref[here, cols] = jnp.where(mine, heads[1], heads[0])

    for copy in weights:
        copy.wait()
    for i in range(cuts):
        tokens[i].wait()
        x = x_scr[i]
        shared = jnp.dot(x, ws_scr[...], preferred_element_type=F32).astype(BF16)
        values = jnp.dot(x, wv_scr[...], preferred_element_type=F32).astype(BF16)
        here = slice(i * step, (i + 1) * step)
        put(here, slice(0, HEAD_DIM), (shared[:, :HEAD_DIM], shared[:, HEAD_DIM:]))
        put(here, slice(HEAD_DIM, wide), (values[:, :HEAD_DIM], values[:, HEAD_DIM:]))
        for h in range(2):
            keys = shared[:, h * HEAD_DIM : (h + 1) * HEAD_DIM].astype(F32)
            square = keys * keys
            high = square.astype(BF16)
            low = (square - high.astype(F32)).astype(BF16)
            total = lax.dot_general(ones, high, NT, preferred_element_type=F32)
            total += lax.dot_general(ones, low, NT, preferred_element_type=F32)
            largest[h] = jnp.maximum(largest[h], total)
            factor = lax.rsqrt(total / HEAD_DIM + 1e-06) * (LOG2E / math.sqrt(HEAD_DIM))
            first = factor.astype(BF16).astype(F32)
            extra[h] = jnp.where(row == i, jnp.concatenate([first] * 2), extra[h])
            extra[h] = jnp.where(row == 4 + i, jnp.concatenate([factor - first] * 2), extra[h])
    for h in range(2):
        top = jnp.broadcast_to(jnp.max(largest[h]), (EXTRA, wide))
        extra[h] = jnp.where(row >= 8, top, extra[h])
    last = slice(rows, rows + EXTRA)
    put(last, slice(0, wide), [e.astype(BF16) for e in extra])


def project(tokens, w_shared, w_value):
    rows, width = tokens.shape
    cuts = 4
    out = jax.ShapeDtypeStruct((rows + EXTRA, 2 * HEAD_DIM), BF16)
    return pl.pallas_call(
        project_kernel,
        in_specs=[ANY] * 3,
        out_specs=(HERE, HERE),
        out_shape=(out, out),
        scratch_shapes=[
            pltpu.VMEM((cuts, rows // cuts, width), BF16),
            pltpu.VMEM(w_shared.shape, BF16),
            pltpu.VMEM(w_value.shape, BF16),
            pltpu.SemaphoreType.DMA((2 + cuts,)),
        ],
        compiler_params=pltpu.CompilerParams(vmem_limit_bytes=63 * 2**20),
        cost_estimate=pl.CostEstimate(
            flops=2 * rows * width * 512, bytes_accessed=7 * 2**20, transcendentals=0
        ),
        name="project",
    )(tokens, w_shared, w_value)


def pick_kernel(w_ref, after_ref, out_ref, scr):
    del after_ref
    mine = w_ref.at[pl.ds(pl.multiple_of(own_core() * HEAD_DIM, HEAD_DIM), HEAD_DIM)]
    pltpu.sync_copy(mine, scr)
    pltpu.sync_copy(scr, out_ref)


def pick(w_output, after):
    piece = (HEAD_DIM, w_output.shape[1])
    return pl.pallas_call(
        pick_kernel,
        in_specs=[ANY] * 2,
        out_specs=ANY,
        out_shape=jax.ShapeDtypeStruct(piece, BF16),
        scratch_shapes=[pltpu.VMEM(piece, BF16)],
        compiler_params=pltpu.CompilerParams(vmem_limit_bytes=63 * 2**20),
        name="pick",
    )(w_output, after)


def attend_kernel(places, first, last, doc_ref, *refs):
    count = len(places)
    if first:
        kv_refs, refs = refs[:count], refs[count:]
        out_ref, kv_scr, acc, sem, acc_sem = refs
        q_of = lambda q: kv_scr[q, :-EXTRA, :HEAD_DIM]
        copies = []
    else:
        q_refs, kv_refs, refs = refs[:2], refs[2 : 2 + count], refs[2 + count :]
        if last:
            states, rest, refs = refs[:2], refs[2:6], refs[6:]
            out_ref, kv_scr, acc, sem, acc_sem, q_scr, sums, sums_sem, peak, weight_sum = refs
        else:
            out_ref, kv_scr, acc, sem, acc_sem, q_scr = refs
        q_of = lambda q: q_scr[q, :-EXTRA, :]
        copies = start_all(
            [
                pltpu.make_async_copy(q_refs[q].at[:, pl.ds(0, HEAD_DIM)], q_scr.at[q], acc_sem.at[2 + q])
                for q in range(2)
            ]
        )
    rows = kv_scr.shape[1] - EXTRA
    tile = 512
    blocks = start_all(
        [pltpu.make_async_copy(kv_refs[i], kv_scr.at[i], sem.at[i]) for i in range(count)]
    )
    if last:
        added = start_all(
            [pltpu.make_async_copy(states[i], sums.at[i], sums_sem.at[i]) for i in range(2)]
        )
    acc[...] = jnp.zeros_like(acc)
    for copy in copies:
        copy.wait()
    doc_len = doc_ref[0]
    q_starts = [block_start(0, other, rows) for other in (False, True)]
    active = jnp.minimum(q_starts[0], q_starts[1]) < doc_len
    if first:
        for copy in blocks:
            copy.wait()
    for i in range(count):
        if not first:
            blocks[i].wait()
        start = block_start(*places[i], rows)

        @pl.when(active & (start < doc_len))
        def _(i=i, start=start):
            extra = kv_scr[i, rows : rows + 8, :].astype(F32)
            factor = extra[0:4] + extra[4:8]
            for q in range(2):
                queries = q_of(q)
                total = acc[q]
                for cut in range(rows // tile):
                    keys = slice(cut * tile, (cut + 1) * tile)
                    each = tile // 256
                    scale = jnp.concatenate(
                        [factor[cut * each + j : cut * each + j + 1] for j in range(each)], axis=1
                    )
                    place = lax.broadcasted_iota(jnp.int32, (1, tile), 1) + (start + cut * tile)
                    bias = jnp.where(place < doc_len, 0.0, -1e30)
                    scores = lax.dot_general(
                        queries, kv_scr[i, keys, :HEAD_DIM], NT, preferred_element_type=F32
                    )
                    weights = jnp.exp2(scores * scale + bias)
                    if first and i == q:
                        weights = jnp.where(
                            lax.broadcasted_iota(jnp.int32, weights.shape, 0)
                            == lax.broadcasted_iota(jnp.int32, weights.shape, 1) + cut * tile,
                            0.0,
                            weights,
                        )
                    values = jnp.concatenate(
                        [kv_scr[i, keys, HEAD_DIM:], jnp.ones((tile, HEAD_DIM), BF16)], axis=1
                    )
                    total += jnp.dot(weights.astype(BF16), values, preferred_element_type=F32)
                acc[q] = total

    if not last:
        for copy in start_all(
            [pltpu.make_async_copy(acc.at[q], out_ref.at[q], acc_sem.at[q]) for q in range(2)]
        ):
            copy.wait()
        return

    for copy in added:
        copy.wait()
    norm = jnp.maximum(
        jnp.max(q_scr[0, rows + 8 :, :].astype(F32)), jnp.max(q_scr[1, rows + 8 :, :].astype(F32))
    )

    @pl.when(norm > NORM_LIMIT**2)
    def _():
        peak[...] = jnp.full_like(peak, -1e30)
        weight_sum[...] = jnp.zeros_like(weight_sum)
        acc[...] = jnp.zeros_like(acc)
        sums[...] = jnp.zeros_like(sums)
        near = ((3, False), (3, True), (1, False), (1, True))
        everything = [
            (q_refs[0], (0, False)),
            (q_refs[1], (0, True)),
            *zip(rest, near),
            *zip(kv_refs, places),
        ]
        small = 256
        for block_ref, place in everything:
            pltpu.sync_copy(block_ref, kv_scr.at[0])
            key_start = block_start(*place, rows)
            extra = kv_scr[0, rows : rows + 8, :].astype(F32)
            factor = extra[0:4] + extra[4:8]

            def absorb(at, carry, key_start=key_start, factor=factor):
                q = lax.div(at, rows // small)
                low = pl.multiple_of(lax.rem(at, rows // small) * small, small)
                here = pl.ds(low, small)
                query_start = jnp.where(q == 0, q_starts[0], q_starts[1]) + low
                for cut in range(rows // small):
                    keys = slice(cut * small, (cut + 1) * small)
                    scores = lax.dot_general(
                        q_scr[q, here, :], kv_scr[0, keys, :HEAD_DIM], NT, preferred_element_type=F32
                    )
                    key_pos = lax.broadcasted_iota(jnp.int32, scores.shape, 1) + (
                        key_start + cut * small
                    )
                    query_pos = lax.broadcasted_iota(jnp.int32, scores.shape, 0) + query_start
                    allowed = (key_pos < doc_len) & (key_pos != query_pos)
                    scores = jnp.where(allowed, scores * factor[cut : cut + 1], -1e30)
                    old = peak[q, here, :]
                    new = jnp.maximum(old, jnp.max(scores, axis=1, keepdims=True))
                    weights = jnp.where(allowed, jnp.exp2(scores - new[:, :1]), 0.0)
                    rescale = jnp.exp2(old - new)
                    peak[q, here, :] = new
                    weight_sum[q, here, :] = weight_sum[q, here, :] * rescale + jnp.sum(
                        weights, axis=1, keepdims=True
                    )
                    acc[q, here, :HEAD_DIM] = acc[q, here, :HEAD_DIM] * rescale + jnp.dot(
                        weights.astype(BF16), kv_scr[0, keys, HEAD_DIM:], preferred_element_type=F32
                    )
                return carry

            lax.fori_loop(0, 2 * rows // small, absorb, 0)
        for q in range(2):
            acc[q, :, HEAD_DIM:] = weight_sum[q]

    core = own_core()
    for q in range(2):
        total = acc[q] + (sums[0, q] + sums[1, q])
        inside = lax.broadcasted_iota(jnp.int32, (rows, HEAD_DIM), 0) + q_starts[q] < doc_len
        mixed = jnp.where(inside, total[:, :HEAD_DIM] / total[:, HEAD_DIM:], 0.0)
        block = core if q == 0 else 1 - core
        out_ref[:, block] = mixed.astype(BF16).reshape(4, rows // 4, HEAD_DIM)


def attend(doc_length, queries, blocks, places, states, rest, name):
    rows = blocks[0].shape[0] - EXTRA
    count = len(blocks)
    first, last = queries is None, rest is not None
    out_shape = jax.ShapeDtypeStruct((2, rows, 2 * HEAD_DIM), F32)
    scratch = [
        pltpu.VMEM((count, rows + EXTRA, 2 * HEAD_DIM), BF16),
        pltpu.VMEM(out_shape.shape, F32),
        pltpu.SemaphoreType.DMA((count,)),
        pltpu.SemaphoreType.DMA((4,)),
    ]
    args = list(blocks)
    if not first:
        args = [*queries, *blocks]
        scratch.append(pltpu.VMEM((2, rows + EXTRA, HEAD_DIM), BF16))
    if last:
        args += [*states, *rest]
        scratch += [
            pltpu.VMEM((2, *out_shape.shape), F32),
            pltpu.SemaphoreType.DMA((2,)),
        ]
        out_shape = jax.ShapeDtypeStruct((4, 2, rows // 4, HEAD_DIM), BF16)
        scratch += [
            pltpu.VMEM((2, rows, HEAD_DIM), F32),
            pltpu.VMEM((2, rows, HEAD_DIM), F32),
        ]
    return pl.pallas_call(
        functools.partial(attend_kernel, places, first, last),
        in_specs=[SMEM] + [ANY] * len(args),
        out_specs=HERE if last else ANY,
        out_shape=out_shape,
        scratch_shapes=scratch,
        compiler_params=pltpu.CompilerParams(vmem_limit_bytes=63 * 2**20),
        cost_estimate=pl.CostEstimate(
            flops=0 if last else 16 * rows * rows * count * HEAD_DIM,
            bytes_accessed=0 if last else 4 * 2**20,
            transcendentals=0,
        ),
        name=name,
    )(doc_length, *args)


def output_kernel(ctx_ref, got_ref, w_ref, *refs):
    piece_refs, got_refs = refs[:3], refs[3:6]
    out_ref, w_scr, sem = refs[6:]
    core = own_core()
    y = lax.rem(lax.axis_index("head"), 4)
    width = w_ref.shape[1]
    cuts = sem.shape[0]
    step = width // cuts

    def head(h):
        return w_ref.at[pl.ds(pl.multiple_of(h * HEAD_DIM, HEAD_DIM), HEAD_DIM)]

    sources = [head(core), head(1 - core)]
    for piece, got in zip(piece_refs, got_refs):
        sources += [piece, got]
    copies = []
    for i in range(cuts):
        cols = pl.ds(i * step, step)
        copies.append(
            start_all(
                [
                    pltpu.make_async_copy(
                        ref.at[:, cols],
                        w_scr.at[pl.ds(at * HEAD_DIM, HEAD_DIM), cols],
                        sem.at[i, at],
                    )
                    for at, ref in enumerate(sources)
                ]
            )
        )
    places = [lax.rem(y + by, 4) for by in (0, 3, 1, 2)]
    left = jnp.concatenate(
        [ref[place, core] for place in places for ref in (ctx_ref, got_ref)], axis=1
    )
    for i in range(cuts):
        for copy in copies[i]:
            copy.wait()
        part = jnp.dot(left, w_scr[:, i * step : (i + 1) * step], preferred_element_type=F32)
        part = part.astype(BF16)
        each = step // 256
        for j in range(each):
            out_ref[i * each + j] = part[:, j * 256 : (j + 1) * 256]


def output(context, got, w_output, pieces, pieces_got):
    rows = context.shape[2]
    width = w_output.shape[1]
    cuts = 2
    return pl.pallas_call(
        output_kernel,
        in_specs=[HERE] * 2 + [ANY] * 7,
        out_specs=HERE,
        out_shape=jax.ShapeDtypeStruct((8, rows, width // 8), BF16),
        scratch_shapes=[
            pltpu.VMEM((8 * HEAD_DIM, width), BF16),
            pltpu.SemaphoreType.DMA((cuts, 8)),
        ],
        compiler_params=pltpu.CompilerParams(vmem_limit_bytes=VMEM),
        cost_estimate=pl.CostEstimate(
            flops=2 * rows * width * 1024, bytes_accessed=6 * 2**20, transcendentals=0
        ),
        name="output",
    )(context, got, w_output, *pieces, *pieces_got)


def body(tokens, w_shared, w_value, w_output, doc_length):
    def move(array, by, cross):
        return lax.ppermute(
            array, "seq", [(i, (i // 2 + by) % 4 * 2 + (i % 2 ^ cross)) for i in range(8)]
        )

    own, given = project(tokens, w_shared, w_value)
    peer = move(given, 0, 1)
    own_left, peer_right = move(own, 1, 0), move(given, -1, 1)
    peer_left, own_right = move(given, 1, 1), move(own, -1, 0)

    def along_y(array, by):
        return lax.ppermute(array, "head", [(i, i // 4 * 4 + (i + by) % 4) for i in range(8)])

    picked = pick(w_output, peer)
    w_left = along_y(picked, 1)

    queries = (own, peer)
    here = attend(doc_length, None, queries, ((0, False), (0, True)), None, None, "attend_here")
    own_left, peer_right, here, w_left = lax.optimization_barrier(
        (own_left, peer_right, here, w_left)
    )
    own_far, peer_far = move(own_left, 1, 0), move(peer_right, -1, 0)
    picked, peer_left, own_right, here = lax.optimization_barrier(
        (picked, peer_left, own_right, here)
    )
    w_right, w_far = along_y(picked, -1), along_y(picked, 2)
    blocks = (own_left, peer_left, own_right, peer_right)
    near = attend(
        doc_length,
        queries,
        blocks,
        ((3, False), (3, True), (1, False), (1, True)),
        None,
        None,
        "attend_near",
    )
    context = attend(
        doc_length,
        queries,
        (own_far, peer_far),
        ((2, False), (2, True)),
        (here, near),
        blocks,
        "attend_far",
    )
    y_groups = [[0, 1, 2, 3], [4, 5, 6, 7]]
    context = lax.all_to_all(context, "head", 0, 0, axis_index_groups=y_groups, tiled=True)
    context, *pieces = lax.optimization_barrier((context, w_left, w_right, w_far))
    pieces_got = [move(piece, 0, 1) for piece in pieces]
    terms = output(context, move(context, 0, 1), w_output, pieces, pieces_got)
    terms = lax.all_to_all(terms, "head", 0, 0, tiled=True).astype(F32)
    result = (terms[:4] + terms[4:]).astype(BF16)
    return result.reshape(tokens.shape[0], result.shape[-1])


def solution(mesh):
    placed = (
        P(("batch", "seq"), None),
        P(None, "head"),
        P(None, "head"),
        P("head", None),
        P("batch"),
    )
    return jax.shard_map(
        body, mesh=mesh, in_specs=placed, out_specs=P(("batch", "seq"), "head"), check_vma=False
    )
```

```python
import functools
import math

import jax
import jax.numpy as jnp
from jax import lax
from jax.experimental import pallas as pl
from jax.experimental.pallas import tpu as pltpu
from jax.sharding import PartitionSpec as P

HEAD_DIM = 128
LOG2E = 1.4426950408889634
NORM_LIMIT = 60.0
EXTRA = 16
NT = (((1,), (1,)), ((), ()))
VMEM = 30 * 2**20
ANY = pl.BlockSpec(memory_space=pl.ANY)
HERE = pl.BlockSpec(memory_space=pltpu.VMEM)
SMEM = pl.BlockSpec(memory_space=pltpu.SMEM)
F32 = jnp.float32
BF16 = jnp.bfloat16


def own_core():
    return lax.rem(lax.axis_index("seq"), 2)


def block_start(by, other, rows):
    seq = lax.axis_index("seq")
    place = lax.rem(lax.div(seq, 2) + by, 4) * 2
    core = lax.rem(seq, 2)
    return (place + (1 - core if other else core)) * rows


def start_all(copies):
    for copy in copies:
        copy.start()
    return copies


def project_kernel(x_ref, ws_ref, wv_ref, own_ref, given_ref, x_scr, w_scr, out_scr, sem, out_sem):
    rows, _ = x_ref.shape
    cuts = x_scr.shape[0]
    step = rows // cuts
    wide = 2 * HEAD_DIM
    weights = start_all(
        [
            pltpu.make_async_copy(ws_ref, w_scr.at[:, pl.ds(0, wide)], sem.at[0]),
            pltpu.make_async_copy(wv_ref, w_scr.at[:, pl.ds(wide, wide)], sem.at[1]),
        ]
    )
    tokens = start_all(
        [
            pltpu.make_async_copy(x_ref.at[pl.ds(i * step, step)], x_scr.at[i], sem.at[2 + i])
            for i in range(cuts)
        ]
    )
    core = own_core()
    outs = []

    def send(low, size):
        here = pl.ds(low, size)
        for h, ref in ((core, own_ref), (1 - core, given_ref)):
            outs.extend(
                start_all(
                    [
                        pltpu.make_async_copy(
                            out_scr.at[h, here], ref.at[here], out_sem.at[len(outs)]
                        )
                    ]
                )
            )

    row = lax.broadcasted_iota(jnp.int32, (EXTRA, wide), 0)
    extra = [jnp.zeros((EXTRA, wide), F32) for _ in range(2)]
    largest = [jnp.zeros((8, wide), F32) for _ in range(2)]
    ones = jnp.ones((8, HEAD_DIM), BF16)
    for copy in weights:
        copy.wait()
    for i in range(cuts):
        tokens[i].wait()
        both = jnp.dot(x_scr[i], w_scr[...], preferred_element_type=F32).astype(BF16)
        here = slice(i * step, (i + 1) * step)
        for h in range(2):
            at = h * HEAD_DIM
            out_scr[h, here, :HEAD_DIM] = both[:, at : at + HEAD_DIM]
            out_scr[h, here, HEAD_DIM:] = both[:, wide + at : wide + at + HEAD_DIM]
        send(i * step, step)
        for h in range(2):
            keys = both[:, h * HEAD_DIM : (h + 1) * HEAD_DIM].astype(F32)
            square = keys * keys
            high = square.astype(BF16)
            low = (square - high.astype(F32)).astype(BF16)
            total = lax.dot_general(ones, high, NT, preferred_element_type=F32)
            total += lax.dot_general(ones, low, NT, preferred_element_type=F32)
            largest[h] = jnp.maximum(largest[h], total)
            factor = lax.rsqrt(total / HEAD_DIM + 1e-06) * (LOG2E / math.sqrt(HEAD_DIM))
            first = factor.astype(BF16).astype(F32)
            extra[h] = jnp.where(row == i, jnp.concatenate([first] * 2), extra[h])
            extra[h] = jnp.where(row == 4 + i, jnp.concatenate([factor - first] * 2), extra[h])
    for h in range(2):
        top = jnp.broadcast_to(jnp.max(largest[h]), (EXTRA, wide))
        out_scr[h, rows:, :] = jnp.where(row >= 8, top, extra[h]).astype(BF16)
    send(rows, EXTRA)
    for copy in outs:
        copy.wait()


def project(tokens, w_shared, w_value):
    rows, width = tokens.shape
    cuts = 4
    out = jax.ShapeDtypeStruct((rows + EXTRA, 2 * HEAD_DIM), BF16)
    return pl.pallas_call(
        project_kernel,
        in_specs=[ANY] * 3,
        out_specs=(ANY, ANY),
        out_shape=(out, out),
        scratch_shapes=[
            pltpu.VMEM((cuts, rows // cuts, width), BF16),
            pltpu.VMEM((width, 4 * HEAD_DIM), BF16),
            pltpu.VMEM((2, rows + EXTRA, 2 * HEAD_DIM), BF16),
            pltpu.SemaphoreType.DMA((2 + cuts,)),
            pltpu.SemaphoreType.DMA((2 * cuts + 2,)),
        ],
        compiler_params=pltpu.CompilerParams(vmem_limit_bytes=63 * 2**20),
        cost_estimate=pl.CostEstimate(
            flops=2 * rows * width * 512, bytes_accessed=7 * 2**20, transcendentals=0
        ),
        name="project",
    )(tokens, w_shared, w_value)


def pick_kernel(w_ref, after_ref, out_ref, scr):
    del after_ref
    mine = w_ref.at[pl.ds(pl.multiple_of(own_core() * HEAD_DIM, HEAD_DIM), HEAD_DIM)]
    pltpu.sync_copy(mine, scr)
    pltpu.sync_copy(scr, out_ref)


def pick(w_output, after):
    piece = (HEAD_DIM, w_output.shape[1])
    return pl.pallas_call(
        pick_kernel,
        in_specs=[ANY] * 2,
        out_specs=ANY,
        out_shape=jax.ShapeDtypeStruct(piece, BF16),
        scratch_shapes=[pltpu.VMEM(piece, BF16)],
        compiler_params=pltpu.CompilerParams(vmem_limit_bytes=63 * 2**20),
        name="pick",
    )(w_output, after)


def attend_kernel(places, first, last, doc_ref, *refs):
    count = len(places)
    if first:
        kv_refs, refs = refs[:count], refs[count:]
        out_ref, kv_scr, acc, sem, acc_sem = refs
        q_of = lambda q: kv_scr[q, :-EXTRA, :HEAD_DIM]
        copies = []
    else:
        q_refs, kv_refs, refs = refs[:2], refs[2 : 2 + count], refs[2 + count :]
        if last:
            states, rest, refs = refs[:2], refs[2:6], refs[6:]
            out_ref, kv_scr, acc, sem, acc_sem, q_scr, sums, sums_sem, peak, weight_sum = refs
        else:
            out_ref, kv_scr, acc, sem, acc_sem, q_scr = refs
        q_of = lambda q: q_scr[q, :-EXTRA, :HEAD_DIM]
        copies = start_all(
            [
                pltpu.make_async_copy(q_refs[q], q_scr.at[q], acc_sem.at[2 + q])
                for q in range(2)
            ]
        )
    rows = kv_scr.shape[1] - EXTRA
    tile = 512
    blocks = start_all(
        [pltpu.make_async_copy(kv_refs[i], kv_scr.at[i], sem.at[i]) for i in range(count)]
    )
    if last:
        added = start_all(
            [pltpu.make_async_copy(states[i], sums.at[i], sums_sem.at[i]) for i in range(2)]
        )
    acc[...] = jnp.zeros_like(acc)
    for copy in copies:
        copy.wait()
    doc_len = doc_ref[0]
    q_starts = [block_start(0, other, rows) for other in (False, True)]
    active = jnp.minimum(q_starts[0], q_starts[1]) < doc_len
    if first:
        for copy in blocks:
            copy.wait()
    for i in range(count):
        if not first:
            blocks[i].wait()
        start = block_start(*places[i], rows)

        @pl.when(active & (start < doc_len))
        def _(i=i, start=start):
            extra = kv_scr[i, rows : rows + 8, :].astype(F32)
            factor = extra[0:4] + extra[4:8]
            for q in range(2):
                queries = q_of(q)
                total = acc[q]
                for cut in range(rows // tile):
                    keys = slice(cut * tile, (cut + 1) * tile)
                    each = tile // 256
                    scale = jnp.concatenate(
                        [factor[cut * each + j : cut * each + j + 1] for j in range(each)], axis=1
                    )
                    place = lax.broadcasted_iota(jnp.int32, (1, tile), 1) + (start + cut * tile)
                    bias = jnp.where(place < doc_len, 0.0, -1e30)
                    scores = lax.dot_general(
                        queries, kv_scr[i, keys, :HEAD_DIM], NT, preferred_element_type=F32
                    )
                    weights = jnp.exp2(scores * scale + bias)
                    if first and i == q:
                        weights = jnp.where(
                            lax.broadcasted_iota(jnp.int32, weights.shape, 0)
                            == lax.broadcasted_iota(jnp.int32, weights.shape, 1) + cut * tile,
                            0.0,
                            weights,
                        )
                    values = jnp.concatenate(
                        [kv_scr[i, keys, HEAD_DIM:], jnp.ones((tile, HEAD_DIM), BF16)], axis=1
                    )
                    total += jnp.dot(weights.astype(BF16), values, preferred_element_type=F32)
                acc[q] = total

    if not last:
        for copy in start_all(
            [pltpu.make_async_copy(acc.at[q], out_ref.at[q], acc_sem.at[q]) for q in range(2)]
        ):
            copy.wait()
        return

    for copy in added:
        copy.wait()
    norm = jnp.maximum(
        jnp.max(q_scr[0, rows + 8 :, :].astype(F32)), jnp.max(q_scr[1, rows + 8 :, :].astype(F32))
    )

    @pl.when(norm > NORM_LIMIT**2)
    def _():
        peak[...] = jnp.full_like(peak, -1e30)
        weight_sum[...] = jnp.zeros_like(weight_sum)
        acc[...] = jnp.zeros_like(acc)
        sums[...] = jnp.zeros_like(sums)
        near = ((3, False), (3, True), (1, False), (1, True))
        everything = [
            (q_refs[0], (0, False)),
            (q_refs[1], (0, True)),
            *zip(rest, near),
            *zip(kv_refs, places),
        ]
        small = 256
        for block_ref, place in everything:
            pltpu.sync_copy(block_ref, kv_scr.at[0])
            key_start = block_start(*place, rows)
            extra = kv_scr[0, rows : rows + 8, :].astype(F32)
            factor = extra[0:4] + extra[4:8]

            def absorb(at, carry, key_start=key_start, factor=factor):
                q = lax.div(at, rows // small)
                low = pl.multiple_of(lax.rem(at, rows // small) * small, small)
                here = pl.ds(low, small)
                query_start = jnp.where(q == 0, q_starts[0], q_starts[1]) + low
                for cut in range(rows // small):
                    keys = slice(cut * small, (cut + 1) * small)
                    scores = lax.dot_general(
                        q_scr[q, here, :HEAD_DIM], kv_scr[0, keys, :HEAD_DIM], NT, preferred_element_type=F32
                    )
                    key_pos = lax.broadcasted_iota(jnp.int32, scores.shape, 1) + (
                        key_start + cut * small
                    )
                    query_pos = lax.broadcasted_iota(jnp.int32, scores.shape, 0) + query_start
                    allowed = (key_pos < doc_len) & (key_pos != query_pos)
                    scores = jnp.where(allowed, scores * factor[cut : cut + 1], -1e30)
                    old = peak[q, here, :]
                    new = jnp.maximum(old, jnp.max(scores, axis=1, keepdims=True))
                    weights = jnp.where(allowed, jnp.exp2(scores - new[:, :1]), 0.0)
                    rescale = jnp.exp2(old - new)
                    peak[q, here, :] = new
                    weight_sum[q, here, :] = weight_sum[q, here, :] * rescale + jnp.sum(
                        weights, axis=1, keepdims=True
                    )
                    acc[q, here, :HEAD_DIM] = acc[q, here, :HEAD_DIM] * rescale + jnp.dot(
                        weights.astype(BF16), kv_scr[0, keys, HEAD_DIM:], preferred_element_type=F32
                    )
                return carry

            lax.fori_loop(0, 2 * rows // small, absorb, 0)
        for q in range(2):
            acc[q, :, HEAD_DIM:] = weight_sum[q]

    core = own_core()
    for q in range(2):
        total = acc[q] + (sums[0, q] + sums[1, q])
        inside = lax.broadcasted_iota(jnp.int32, (rows, HEAD_DIM), 0) + q_starts[q] < doc_len
        mixed = jnp.where(inside, total[:, :HEAD_DIM] / total[:, HEAD_DIM:], 0.0)
        block = core if q == 0 else 1 - core
        out_ref[:, block] = mixed.astype(BF16).reshape(4, rows // 4, HEAD_DIM)


def attend(doc_length, queries, blocks, places, states, rest, name):
    rows = blocks[0].shape[0] - EXTRA
    count = len(blocks)
    first, last = queries is None, rest is not None
    out_shape = jax.ShapeDtypeStruct((2, rows, 2 * HEAD_DIM), F32)
    scratch = [
        pltpu.VMEM((count, rows + EXTRA, 2 * HEAD_DIM), BF16),
        pltpu.VMEM(out_shape.shape, F32),
        pltpu.SemaphoreType.DMA((count,)),
        pltpu.SemaphoreType.DMA((4,)),
    ]
    args = list(blocks)
    if not first:
        args = [*queries, *blocks]
        scratch.append(pltpu.VMEM((2, rows + EXTRA, 2 * HEAD_DIM), BF16))
    if last:
        args += [*states, *rest]
        scratch += [
            pltpu.VMEM((2, *out_shape.shape), F32),
            pltpu.SemaphoreType.DMA((2,)),
        ]
        out_shape = jax.ShapeDtypeStruct((4, 2, rows // 4, HEAD_DIM), BF16)
        scratch += [
            pltpu.VMEM((2, rows, HEAD_DIM), F32),
            pltpu.VMEM((2, rows, HEAD_DIM), F32),
        ]
    return pl.pallas_call(
        functools.partial(attend_kernel, places, first, last),
        in_specs=[SMEM] + [ANY] * len(args),
        out_specs=HERE if last else ANY,
        out_shape=out_shape,
        scratch_shapes=scratch,
        compiler_params=pltpu.CompilerParams(vmem_limit_bytes=63 * 2**20),
        cost_estimate=pl.CostEstimate(
            flops=0 if last else 16 * rows * rows * count * HEAD_DIM,
            bytes_accessed=0 if last else 4 * 2**20,
            transcendentals=0,
        ),
        name=name,
    )(doc_length, *args)


def output_kernel(ctx_ref, got_ref, w_ref, *refs):
    piece_refs, got_refs = refs[:3], refs[3:6]
    out_ref, w_scr, sem = refs[6:]
    core = own_core()
    y = lax.rem(lax.axis_index("head"), 4)
    width = w_ref.shape[1]
    cuts = sem.shape[0]
    step = width // cuts

    def head(h):
        return w_ref.at[pl.ds(pl.multiple_of(h * HEAD_DIM, HEAD_DIM), HEAD_DIM)]

    sources = [head(core), head(1 - core)]
    for piece, got in zip(piece_refs, got_refs):
        sources += [piece, got]
    copies = []
    for i in range(cuts):
        cols = pl.ds(i * step, step)
        copies.append(
            start_all(
                [
                    pltpu.make_async_copy(
                        ref.at[:, cols],
                        w_scr.at[pl.ds(at * HEAD_DIM, HEAD_DIM), cols],
                        sem.at[i, at],
                    )
                    for at, ref in enumerate(sources)
                ]
            )
        )
    places = [lax.rem(y + by, 4) for by in (0, 3, 1, 2)]
    left = jnp.concatenate(
        [ref[place, core] for place in places for ref in (ctx_ref, got_ref)], axis=1
    )
    for i in range(cuts):
        for copy in copies[i]:
            copy.wait()
        part = jnp.dot(left, w_scr[:, i * step : (i + 1) * step], preferred_element_type=F32)
        part = part.astype(BF16)
        each = step // 256
        for j in range(each):
            out_ref[i * each + j] = part[:, j * 256 : (j + 1) * 256]


def output(context, got, w_output, pieces, pieces_got):
    rows = context.shape[2]
    width = w_output.shape[1]
    cuts = 2
    return pl.pallas_call(
        output_kernel,
        in_specs=[HERE] * 2 + [ANY] * 7,
        out_specs=HERE,
        out_shape=jax.ShapeDtypeStruct((8, rows, width // 8), BF16),
        scratch_shapes=[
            pltpu.VMEM((8 * HEAD_DIM, width), BF16),
            pltpu.SemaphoreType.DMA((cuts, 8)),
        ],
        compiler_params=pltpu.CompilerParams(vmem_limit_bytes=VMEM),
        cost_estimate=pl.CostEstimate(
            flops=2 * rows * width * 1024, bytes_accessed=6 * 2**20, transcendentals=0
        ),
        name="output",
    )(context, got, w_output, *pieces, *pieces_got)


def body(tokens, w_shared, w_value, w_output, doc_length):
    def move(array, by, cross):
        return lax.ppermute(
            array, "seq", [(i, (i // 2 + by) % 4 * 2 + (i % 2 ^ cross)) for i in range(8)]
        )

    own, given = project(tokens, w_shared, w_value)
    peer = move(given, 0, 1)
    own_left, peer_right = move(own, 1, 0), move(given, -1, 1)
    peer_left, own_right = move(given, 1, 1), move(own, -1, 0)

    def along_y(array, by):
        return lax.ppermute(array, "head", [(i, i // 4 * 4 + (i + by) % 4) for i in range(8)])

    picked = pick(w_output, peer)
    w_left = along_y(picked, 1)

    queries = (own, peer)
    here = attend(doc_length, None, queries, ((0, False), (0, True)), None, None, "attend_here")
    own_left, peer_right, here, w_left = lax.optimization_barrier(
        (own_left, peer_right, here, w_left)
    )
    own_far, peer_far = move(own_left, 1, 0), move(peer_right, -1, 0)
    picked, peer_left, own_right, here = lax.optimization_barrier(
        (picked, peer_left, own_right, here)
    )
    w_right, w_far = along_y(picked, -1), along_y(picked, 2)
    blocks = (own_left, peer_left, own_right, peer_right)
    near = attend(
        doc_length,
        queries,
        blocks,
        ((3, False), (3, True), (1, False), (1, True)),
        None,
        None,
        "attend_near",
    )
    context = attend(
        doc_length,
        queries,
        (own_far, peer_far),
        ((2, False), (2, True)),
        (here, near),
        blocks,
        "attend_far",
    )
    y_groups = [[0, 1, 2, 3], [4, 5, 6, 7]]
    context, *pieces = lax.optimization_barrier((context, w_left, w_right, w_far))
    context = lax.all_to_all(context, "head", 0, 0, axis_index_groups=y_groups, tiled=True)
    pieces_got = [move(piece, 0, 1) for piece in pieces]
    terms = output(context, move(context, 0, 1), w_output, pieces, pieces_got)
    terms = lax.all_to_all(terms, "head", 0, 0, tiled=True).astype(F32)
    result = (terms[:4] + terms[4:]).astype(BF16)
    return result.reshape(tokens.shape[0], result.shape[-1])


def solution(mesh):
    placed = (
        P(("batch", "seq"), None),
        P(None, "head"),
        P(None, "head"),
        P("head", None),
        P("batch"),
    )
    return jax.shard_map(
        body, mesh=mesh, in_specs=placed, out_specs=P(("batch", "seq"), "head"), check_vma=False
    )
```

```python
import functools
import math

import jax
import jax.numpy as jnp
from jax import lax
from jax.experimental import pallas as pl
from jax.experimental.pallas import tpu as pltpu
from jax.sharding import PartitionSpec as P

HEAD_DIM = 128
LOG2E = 1.4426950408889634
NORM_LIMIT = 60.0
EXTRA = 16
VMEM = 65280 * 2**10
NT = (((1,), (1,)), ((), ()))
ANY = pl.BlockSpec(memory_space=pl.ANY)
HERE = pl.BlockSpec(memory_space=pltpu.VMEM)
SMEM = pl.BlockSpec(memory_space=pltpu.SMEM)
F32 = jnp.float32
BF16 = jnp.bfloat16


def own_core():
    return lax.rem(lax.axis_index("seq"), 2)


def block_start(by, other, rows):
    seq = lax.axis_index("seq")
    place = lax.rem(lax.div(seq, 2) + by, 4) * 2
    core = lax.rem(seq, 2)
    return (place + (1 - core if other else core)) * rows


def start_all(copies):
    for copy in copies:
        copy.start()
    return copies


def project_kernel(x_ref, ws_ref, wv_ref, own_ref, given_ref, x_scr, w_scr, out_scr, sem, out_sem):
    rows, _ = x_ref.shape
    cuts = x_scr.shape[0]
    step = rows // cuts
    wide = 2 * HEAD_DIM
    weights = start_all(
        [
            pltpu.make_async_copy(ws_ref, w_scr.at[:, pl.ds(0, wide)], sem.at[0]),
            pltpu.make_async_copy(wv_ref, w_scr.at[:, pl.ds(wide, wide)], sem.at[1]),
        ]
    )
    tokens = start_all(
        [
            pltpu.make_async_copy(x_ref.at[pl.ds(i * step, step)], x_scr.at[i], sem.at[2 + i])
            for i in range(cuts)
        ]
    )
    core = own_core()
    outs = []

    def send(low, size):
        here = pl.ds(low, size)
        for h, ref in ((core, own_ref), (1 - core, given_ref)):
            outs.extend(
                start_all(
                    [
                        pltpu.make_async_copy(
                            out_scr.at[h, here], ref.at[here], out_sem.at[len(outs)]
                        )
                    ]
                )
            )

    row = lax.broadcasted_iota(jnp.int32, (EXTRA, wide), 0)
    extra = [jnp.zeros((EXTRA, wide), F32) for _ in range(2)]
    largest = [jnp.zeros((8, wide), F32) for _ in range(2)]
    ones = jnp.ones((8, HEAD_DIM), BF16)
    for copy in weights:
        copy.wait()
    for i in range(cuts):
        tokens[i].wait()
        both = jnp.dot(x_scr[i], w_scr[...], preferred_element_type=F32).astype(BF16)
        here = slice(i * step, (i + 1) * step)
        for h in range(2):
            at = h * HEAD_DIM
            out_scr[h, here, :HEAD_DIM] = both[:, at : at + HEAD_DIM]
            out_scr[h, here, HEAD_DIM:] = both[:, wide + at : wide + at + HEAD_DIM]
        send(i * step, step)
        for h in range(2):
            keys = both[:, h * HEAD_DIM : (h + 1) * HEAD_DIM].astype(F32)
            square = keys * keys
            total = lax.dot_general(ones, square.astype(BF16), NT, preferred_element_type=F32)
            largest[h] = jnp.maximum(largest[h], total)
            factor = lax.rsqrt(total / HEAD_DIM + 1e-06) * (LOG2E / math.sqrt(HEAD_DIM))
            first = factor.astype(BF16).astype(F32)
            extra[h] = jnp.where(row == i, jnp.concatenate([first] * 2), extra[h])
            extra[h] = jnp.where(row == 4 + i, jnp.concatenate([factor - first] * 2), extra[h])
    for h in range(2):
        top = jnp.broadcast_to(jnp.max(largest[h]), (EXTRA, wide))
        out_scr[h, rows:, :] = jnp.where(row >= 8, top, extra[h]).astype(BF16)
    send(rows, EXTRA)
    for copy in outs:
        copy.wait()


def project(tokens, w_shared, w_value):
    rows, width = tokens.shape
    cuts = 4
    out = jax.ShapeDtypeStruct((rows + EXTRA, 2 * HEAD_DIM), BF16)
    return pl.pallas_call(
        project_kernel,
        in_specs=[ANY] * 3,
        out_specs=(ANY, ANY),
        out_shape=(out, out),
        scratch_shapes=[
            pltpu.VMEM((cuts, rows // cuts, width), BF16),
            pltpu.VMEM((width, 4 * HEAD_DIM), BF16),
            pltpu.VMEM((2, rows + EXTRA, 2 * HEAD_DIM), BF16),
            pltpu.SemaphoreType.DMA((2 + cuts,)),
            pltpu.SemaphoreType.DMA((2 * cuts + 2,)),
        ],
        compiler_params=pltpu.CompilerParams(vmem_limit_bytes=VMEM),
        cost_estimate=pl.CostEstimate(
            flops=2 * rows * width * 512, bytes_accessed=7 * 2**20, transcendentals=0
        ),
        name="project",
    )(tokens, w_shared, w_value)


def spread_kernel(w_ref, after_ref, out_ref, scr, sem):
    del after_ref
    mine = w_ref.at[pl.ds(pl.multiple_of(own_core() * HEAD_DIM, HEAD_DIM), HEAD_DIM)]
    pltpu.sync_copy(mine, scr)
    for copy in start_all(
        [pltpu.make_async_copy(scr, out_ref.at[i], sem.at[i]) for i in range(4)]
    ):
        copy.wait()


def spread(w_output, after):
    piece = (HEAD_DIM, w_output.shape[1])
    return pl.pallas_call(
        spread_kernel,
        in_specs=[ANY] * 2,
        out_specs=ANY,
        out_shape=jax.ShapeDtypeStruct((4, *piece), BF16),
        scratch_shapes=[pltpu.VMEM(piece, BF16), pltpu.SemaphoreType.DMA((4,))],
        compiler_params=pltpu.CompilerParams(vmem_limit_bytes=VMEM),
        name="spread",
    )(w_output, after)


def attend_kernel(places, first, last, doc_ref, *refs):
    count = len(places)
    if first:
        kv_refs, refs = refs[:count], refs[count:]
        out_ref, kv_scr, acc, sem, acc_sem = refs
        copies = []
    else:
        q_refs, kv_refs, refs = refs[:2], refs[2 : 2 + count], refs[2 + count :]
        if last:
            states, rest, refs = refs[:2], refs[2:6], refs[6:]
            out_ref, kv_scr, acc, sem, acc_sem, q_scr, sums, sums_sem, peak, weight_sum = refs
        else:
            out_ref, kv_scr, acc, sem, acc_sem, q_scr = refs
        copies = start_all(
            [
                pltpu.make_async_copy(q_refs[q], q_scr.at[q], acc_sem.at[2 + q])
                for q in range(2)
            ]
        )
    rows = kv_scr.shape[1] - EXTRA
    tile = 512
    blocks = start_all(
        [pltpu.make_async_copy(kv_refs[i], kv_scr.at[i], sem.at[i]) for i in range(count)]
    )
    if last:
        added = start_all(
            [pltpu.make_async_copy(states[i], sums.at[i], sums_sem.at[i]) for i in range(2)]
        )
    acc[...] = jnp.zeros_like(acc)
    for copy in copies:
        copy.wait()
    doc_len = doc_ref[0]
    q_starts = [block_start(0, other, rows) for other in (False, True)]
    active = jnp.minimum(q_starts[0], q_starts[1]) < doc_len
    starts = [block_start(*place, rows) for place in places]
    q_all = kv_scr if first else q_scr
    for copy in blocks if first else blocks[:1]:
        copy.wait()

    def absorb_block(at, carry):
        q, i = lax.div(at, count), lax.rem(at, count)
        start = starts[0]
        for j in range(1, count):
            start = jnp.where(i == j, starts[j], start)
        if not first:

            @pl.when((q == 0) & (i > 0))
            def _():
                pltpu.make_async_copy(kv_refs[0], kv_scr.at[i], sem.at[i]).wait()

        @pl.when(active & (start < doc_len))
        def _():
            extra = kv_scr[i, rows : rows + 8, :].astype(F32)
            factor = extra[0:4] + extra[4:8]
            queries = q_all[q, :rows, :HEAD_DIM]
            total = acc[q]
            for cut in range(rows // tile):
                keys = slice(cut * tile, (cut + 1) * tile)
                each = tile // 256
                scale = jnp.concatenate(
                    [factor[cut * each + j : cut * each + j + 1] for j in range(each)], axis=1
                )
                place = lax.broadcasted_iota(jnp.int32, (1, tile), 1) + (start + cut * tile)
                bias = jnp.where(place < doc_len, 0.0, -1e30)
                scores = lax.dot_general(
                    queries, kv_scr[i, keys, :HEAD_DIM], NT, preferred_element_type=F32
                )
                weights = jnp.exp2(scores * scale + bias)
                if first:
                    apart = jnp.where(i == q, cut * tile, 4 * rows)
                    weights = jnp.where(
                        lax.broadcasted_iota(jnp.int32, weights.shape, 0)
                        == lax.broadcasted_iota(jnp.int32, weights.shape, 1) + apart,
                        0.0,
                        weights,
                    )
                values = jnp.concatenate(
                    [kv_scr[i, keys, HEAD_DIM:], jnp.ones((tile, HEAD_DIM), BF16)], axis=1
                )
                total += jnp.dot(weights.astype(BF16), values, preferred_element_type=F32)
            acc[q] = total

        return carry

    def leave(q):
        return pltpu.make_async_copy(acc.at[q], out_ref.at[q], acc_sem.at[q])

    lax.fori_loop(0, count, absorb_block, 0)
    if not last:
        leave(0).start()
    lax.fori_loop(count, 2 * count, absorb_block, 0)
    if not last:
        leave(1).start()
        leave(0).wait()
        leave(1).wait()
        return

    for copy in added:
        copy.wait()
    norm = jnp.maximum(
        jnp.max(q_scr[0, rows + 8 :, :].astype(F32)), jnp.max(q_scr[1, rows + 8 :, :].astype(F32))
    )

    @pl.when(norm > NORM_LIMIT**2)
    def _():
        peak[...] = jnp.full_like(peak, -1e30)
        weight_sum[...] = jnp.zeros_like(weight_sum)
        acc[...] = jnp.zeros_like(acc)
        sums[...] = jnp.zeros_like(sums)
        near = ((3, False), (3, True), (1, False), (1, True))
        everything = [
            (q_refs[0], (0, False)),
            (q_refs[1], (0, True)),
            *zip(rest, near),
            *zip(kv_refs, places),
        ]
        small = 256
        for block_ref, place in everything:
            pltpu.sync_copy(block_ref, kv_scr.at[0])
            key_start = block_start(*place, rows)
            extra = kv_scr[0, rows : rows + 8, :].astype(F32)
            factor = extra[0:4] + extra[4:8]

            def absorb(at, carry, key_start=key_start, factor=factor):
                q = lax.div(at, rows // small)
                low = pl.multiple_of(lax.rem(at, rows // small) * small, small)
                here = pl.ds(low, small)
                query_start = jnp.where(q == 0, q_starts[0], q_starts[1]) + low
                for cut in range(rows // small):
                    keys = slice(cut * small, (cut + 1) * small)
                    scores = lax.dot_general(
                        q_scr[q, here, :HEAD_DIM], kv_scr[0, keys, :HEAD_DIM], NT, preferred_element_type=F32
                    )
                    key_pos = lax.broadcasted_iota(jnp.int32, scores.shape, 1) + (
                        key_start + cut * small
                    )
                    query_pos = lax.broadcasted_iota(jnp.int32, scores.shape, 0) + query_start
                    allowed = (key_pos < doc_len) & (key_pos != query_pos)
                    scores = jnp.where(allowed, scores * factor[cut : cut + 1], -1e30)
                    old = peak[q, here, :]
                    new = jnp.maximum(old, jnp.max(scores, axis=1, keepdims=True))
                    weights = jnp.where(allowed, jnp.exp2(scores - new[:, :1]), 0.0)
                    rescale = jnp.exp2(old - new)
                    peak[q, here, :] = new
                    weight_sum[q, here, :] = weight_sum[q, here, :] * rescale + jnp.sum(
                        weights, axis=1, keepdims=True
                    )
                    acc[q, here, :HEAD_DIM] = acc[q, here, :HEAD_DIM] * rescale + jnp.dot(
                        weights.astype(BF16), kv_scr[0, keys, HEAD_DIM:], preferred_element_type=F32
                    )
                return carry

            lax.fori_loop(0, 2 * rows // small, absorb, 0)
        for q in range(2):
            acc[q, :, HEAD_DIM:] = weight_sum[q]

    core = own_core()
    for q in range(2):
        total = acc[q] + (sums[0, q] + sums[1, q])
        inside = lax.broadcasted_iota(jnp.int32, (rows, HEAD_DIM), 0) + q_starts[q] < doc_len
        mixed = jnp.where(inside, total[:, :HEAD_DIM] / total[:, HEAD_DIM:], 0.0)
        block = core if q == 0 else 1 - core
        out_ref[:, block] = mixed.astype(BF16).reshape(4, rows // 4, HEAD_DIM)


def attend(doc_length, queries, blocks, places, states, rest, name):
    rows = blocks[0].shape[0] - EXTRA
    count = len(blocks)
    first, last = queries is None, rest is not None
    out_shape = jax.ShapeDtypeStruct((2, rows, 2 * HEAD_DIM), F32)
    scratch = [
        pltpu.VMEM((count, rows + EXTRA, 2 * HEAD_DIM), BF16),
        pltpu.VMEM(out_shape.shape, F32),
        pltpu.SemaphoreType.DMA((count,)),
        pltpu.SemaphoreType.DMA((4,)),
    ]
    args = list(blocks)
    if not first:
        args = [*queries, *blocks]
        scratch.append(pltpu.VMEM((2, rows + EXTRA, 2 * HEAD_DIM), BF16))
    if last:
        args += [*states, *rest]
        scratch += [
            pltpu.VMEM((2, *out_shape.shape), F32),
            pltpu.SemaphoreType.DMA((2,)),
        ]
        out_shape = jax.ShapeDtypeStruct((4, 2, rows // 4, HEAD_DIM), BF16)
        scratch += [
            pltpu.VMEM((2, rows, HEAD_DIM), F32),
            pltpu.VMEM((2, rows, HEAD_DIM), F32),
        ]
    return pl.pallas_call(
        functools.partial(attend_kernel, places, first, last),
        in_specs=[SMEM] + [ANY] * len(args),
        out_specs=HERE if last else ANY,
        out_shape=out_shape,
        scratch_shapes=scratch,
        compiler_params=pltpu.CompilerParams(vmem_limit_bytes=VMEM),
        cost_estimate=pl.CostEstimate(
            flops=16 * rows * rows * count * HEAD_DIM,
            bytes_accessed=4 * 2**20,
            transcendentals=0,
        ),
        name=name,
    )(doc_length, *args)


def output_kernel(ctx_ref, got_ref, w_ref, w_got_ref, out_ref):
    core = own_core()
    lefts = [
        jnp.concatenate([ref[y, core] for y in range(4)], axis=1) for ref in (ctx_ref, got_ref)
    ]
    width = w_ref.shape[2]
    step = width // 8
    for i in range(8):
        cols = slice(i * step, (i + 1) * step)
        part = None
        for left, ref in zip(lefts, (w_ref, w_got_ref)):
            right = ref[:, :, cols].reshape(4 * HEAD_DIM, step)
            term = jnp.dot(left, right, preferred_element_type=F32)
            part = term if part is None else part + term
        out_ref[i] = part.astype(BF16)


def output(context, got, weights, weights_got):
    rows = context.shape[2]
    width = weights.shape[2]
    return pl.pallas_call(
        output_kernel,
        in_specs=[HERE] * 4,
        out_specs=HERE,
        out_shape=jax.ShapeDtypeStruct((8, rows, width // 8), BF16),
        compiler_params=pltpu.CompilerParams(vmem_limit_bytes=30 * 2**20),
        cost_estimate=pl.CostEstimate(
            flops=2 * rows * width * 1024, bytes_accessed=6 * 2**20, transcendentals=0
        ),
        name="output",
    )(context, got, weights, weights_got)


def body(tokens, w_shared, w_value, w_output, doc_length):
    def move(array, by, cross):
        return lax.ppermute(
            array, "seq", [(i, (i // 2 + by) % 4 * 2 + (i % 2 ^ cross)) for i in range(8)]
        )

    own, given = project(tokens, w_shared, w_value)
    peer = move(given, 0, 1)
    own_left, peer_right = move(own, 1, 0), move(given, -1, 1)
    peer_left, own_right = move(given, 1, 1), move(own, -1, 0)

    queries = (own, peer)
    here = attend(doc_length, None, queries, ((0, False), (0, True)), None, None, "attend_here")
    y_groups = [[0, 1, 2, 3], [4, 5, 6, 7]]
    weights = lax.all_to_all(
        spread(w_output, here), "head", 0, 0, axis_index_groups=y_groups, tiled=True
    )
    own_left, peer_right, here = lax.optimization_barrier((own_left, peer_right, here))
    own_far, peer_far = move(own_left, 1, 0), move(peer_right, -1, 0)
    blocks = (own_left, peer_left, own_right, peer_right)
    near = attend(
        doc_length,
        queries,
        blocks,
        ((3, False), (3, True), (1, False), (1, True)),
        None,
        None,
        "attend_near",
    )
    context = attend(
        doc_length,
        queries,
        (own_far, peer_far),
        ((2, False), (2, True)),
        (here, near),
        blocks,
        "attend_far",
    )
    weights, context = lax.optimization_barrier((weights, context))
    weights_got = move(weights, 0, 1)
    context = lax.all_to_all(context, "head", 0, 0, axis_index_groups=y_groups, tiled=True)
    terms = output(context, move(context, 0, 1), weights, weights_got)
    terms = lax.all_to_all(terms, "head", 0, 0, tiled=True).astype(F32)
    result = (terms[:4] + terms[4:]).astype(BF16)
    return result.reshape(tokens.shape[0], result.shape[-1])


def solution(mesh):
    placed = (
        P(("batch", "seq"), None),
        P(None, "head"),
        P(None, "head"),
        P("head", None),
        P("batch"),
    )
    return jax.shard_map(
        body, mesh=mesh, in_specs=placed, out_specs=P(("batch", "seq"), "head"), check_vma=False
    )
```

```python
import functools
import math

import jax
import jax.numpy as jnp
from jax import lax
from jax.experimental import pallas as pl
from jax.experimental.pallas import tpu as pltpu
from jax.sharding import PartitionSpec as P

HEAD_DIM = 128
LOG2E = 1.4426950408889634
NORM_LIMIT = 60.0
EXTRA = 16
VMEM = 65280 * 2**10
NT = (((1,), (1,)), ((), ()))
ANY = pl.BlockSpec(memory_space=pl.ANY)
HERE = pl.BlockSpec(memory_space=pltpu.VMEM)
SMEM = pl.BlockSpec(memory_space=pltpu.SMEM)
F32 = jnp.float32
BF16 = jnp.bfloat16


def own_core():
    return lax.rem(lax.axis_index("seq"), 2)


def block_start(by, other, rows):
    seq = lax.axis_index("seq")
    place = lax.rem(lax.div(seq, 2) + by, 4) * 2
    core = lax.rem(seq, 2)
    return (place + (1 - core if other else core)) * rows


def start_all(copies):
    for copy in copies:
        copy.start()
    return copies


def project_kernel(x_ref, ws_ref, wv_ref, own_ref, given_ref, x_scr, w_scr, out_scr, sem, out_sem):
    rows, _ = x_ref.shape
    cuts = x_scr.shape[0]
    step = rows // cuts
    wide = 2 * HEAD_DIM
    weights = start_all(
        [
            pltpu.make_async_copy(ws_ref, w_scr.at[:, pl.ds(0, wide)], sem.at[0]),
            pltpu.make_async_copy(wv_ref, w_scr.at[:, pl.ds(wide, wide)], sem.at[1]),
        ]
    )
    tokens = start_all(
        [
            pltpu.make_async_copy(x_ref.at[pl.ds(i * step, step)], x_scr.at[i], sem.at[2 + i])
            for i in range(cuts)
        ]
    )
    core = own_core()
    outs = []

    def send(low, size):
        here = pl.ds(low, size)
        for h, ref in ((core, own_ref), (1 - core, given_ref)):
            outs.extend(
                start_all(
                    [
                        pltpu.make_async_copy(
                            out_scr.at[h, here], ref.at[here], out_sem.at[len(outs)]
                        )
                    ]
                )
            )

    row = lax.broadcasted_iota(jnp.int32, (EXTRA, wide), 0)
    extra = [jnp.zeros((EXTRA, wide), F32) for _ in range(2)]
    largest = [jnp.zeros((8, wide), F32) for _ in range(2)]
    ones = jnp.ones((8, HEAD_DIM), BF16)
    for copy in weights:
        copy.wait()
    for i in range(cuts):
        tokens[i].wait()
        both = jnp.dot(x_scr[i], w_scr[...], preferred_element_type=F32).astype(BF16)
        here = slice(i * step, (i + 1) * step)
        for h in range(2):
            at = h * HEAD_DIM
            out_scr[h, here, :HEAD_DIM] = both[:, at : at + HEAD_DIM]
            out_scr[h, here, HEAD_DIM:] = both[:, wide + at : wide + at + HEAD_DIM]
        send(i * step, step)
        for h in range(2):
            keys = both[:, h * HEAD_DIM : (h + 1) * HEAD_DIM].astype(F32)
            square = keys * keys
            total = lax.dot_general(ones, square.astype(BF16), NT, preferred_element_type=F32)
            largest[h] = jnp.maximum(largest[h], total)
            factor = lax.rsqrt(total / HEAD_DIM + 1e-06) * (LOG2E / math.sqrt(HEAD_DIM))
            first = factor.astype(BF16).astype(F32)
            extra[h] = jnp.where(row == i, jnp.concatenate([first] * 2), extra[h])
            extra[h] = jnp.where(row == 4 + i, jnp.concatenate([factor - first] * 2), extra[h])
    for h in range(2):
        top = jnp.broadcast_to(jnp.max(largest[h]), (EXTRA, wide))
        out_scr[h, rows:, :] = jnp.where(row >= 8, top, extra[h]).astype(BF16)
    send(rows, EXTRA)
    for copy in outs:
        copy.wait()


def project(tokens, w_shared, w_value):
    rows, width = tokens.shape
    cuts = 4
    out = jax.ShapeDtypeStruct((rows + EXTRA, 2 * HEAD_DIM), BF16)
    return pl.pallas_call(
        project_kernel,
        in_specs=[ANY] * 3,
        out_specs=(ANY, ANY),
        out_shape=(out, out),
        scratch_shapes=[
            pltpu.VMEM((cuts, rows // cuts, width), BF16),
            pltpu.VMEM((width, 4 * HEAD_DIM), BF16),
            pltpu.VMEM((2, rows + EXTRA, 2 * HEAD_DIM), BF16),
            pltpu.SemaphoreType.DMA((2 + cuts,)),
            pltpu.SemaphoreType.DMA((2 * cuts + 2,)),
        ],
        compiler_params=pltpu.CompilerParams(vmem_limit_bytes=VMEM),
        cost_estimate=pl.CostEstimate(
            flops=2 * rows * width * 512, bytes_accessed=7 * 2**20, transcendentals=0
        ),
        name="project",
    )(tokens, w_shared, w_value)


def spread_kernel(w_ref, after_ref, out_ref, scr, sem):
    del after_ref
    mine = w_ref.at[pl.ds(pl.multiple_of(own_core() * HEAD_DIM, HEAD_DIM), HEAD_DIM)]
    pltpu.sync_copy(mine, scr)
    for copy in start_all(
        [pltpu.make_async_copy(scr, out_ref.at[i], sem.at[i]) for i in range(4)]
    ):
        copy.wait()


def spread(w_output, after):
    piece = (HEAD_DIM, w_output.shape[1])
    return pl.pallas_call(
        spread_kernel,
        in_specs=[ANY] * 2,
        out_specs=ANY,
        out_shape=jax.ShapeDtypeStruct((4, *piece), BF16),
        scratch_shapes=[pltpu.VMEM(piece, BF16), pltpu.SemaphoreType.DMA((4,))],
        compiler_params=pltpu.CompilerParams(vmem_limit_bytes=VMEM),
        name="spread",
    )(w_output, after)


def attend_kernel(places, first, last, doc_ref, *refs):
    count = len(places)
    if first:
        kv_refs, refs = refs[:count], refs[count:]
        out_ref, kv_scr, acc, sem, acc_sem = refs
        copies = []
    else:
        q_refs, kv_refs, refs = refs[:2], refs[2 : 2 + count], refs[2 + count :]
        if last:
            states, rest, refs = refs[:2], refs[2:6], refs[6:]
            out_ref, kv_scr, acc, sem, acc_sem, q_scr, sums, sums_sem, peak, weight_sum = refs
        else:
            out_ref, kv_scr, acc, sem, acc_sem, q_scr = refs
        copies = start_all(
            [
                pltpu.make_async_copy(q_refs[q], q_scr.at[q], acc_sem.at[2 + q])
                for q in range(2)
            ]
        )
    rows = kv_scr.shape[1] - EXTRA
    tile = 512
    blocks = start_all(
        [pltpu.make_async_copy(kv_refs[i], kv_scr.at[i], sem.at[i]) for i in range(count)]
    )
    if last:
        added = start_all(
            [pltpu.make_async_copy(states[i], sums.at[i], sums_sem.at[i]) for i in range(2)]
        )
    acc[...] = jnp.zeros_like(acc)
    for copy in copies:
        copy.wait()
    doc_len = doc_ref[0]
    q_starts = [block_start(0, other, rows) for other in (False, True)]
    active = jnp.minimum(q_starts[0], q_starts[1]) < doc_len
    starts = [block_start(*place, rows) for place in places]
    q_all = kv_scr if first else q_scr
    for copy in blocks if first else blocks[:1]:
        copy.wait()

    def absorb_block(i, carry):
        start = starts[0]
        for j in range(1, count):
            start = jnp.where(i == j, starts[j], start)
        if not first:

            @pl.when(i > 0)
            def _():
                pltpu.make_async_copy(kv_refs[0], kv_scr.at[i], sem.at[i]).wait()

        @pl.when(active & (start < doc_len))
        def _():
            extra = kv_scr[i, rows : rows + 8, :].astype(F32)
            factor = extra[0:4] + extra[4:8]
            for q in range(2):
                queries = q_all[q, :rows, :HEAD_DIM]
                total = acc[q]
                for cut in range(rows // tile):
                    keys = slice(cut * tile, (cut + 1) * tile)
                    each = tile // 256
                    scale = jnp.concatenate(
                        [factor[cut * each + j : cut * each + j + 1] for j in range(each)], axis=1
                    )
                    place = lax.broadcasted_iota(jnp.int32, (1, tile), 1) + (start + cut * tile)
                    bias = jnp.where(place < doc_len, 0.0, -1e30)
                    scores = lax.dot_general(
                        queries, kv_scr[i, keys, :HEAD_DIM], NT, preferred_element_type=F32
                    )
                    weights = jnp.exp2(scores * scale + bias)
                    if first:
                        apart = jnp.where(i == q, cut * tile, 4 * rows)
                        weights = jnp.where(
                            lax.broadcasted_iota(jnp.int32, weights.shape, 0)
                            == lax.broadcasted_iota(jnp.int32, weights.shape, 1) + apart,
                            0.0,
                            weights,
                        )
                    values = jnp.concatenate(
                        [kv_scr[i, keys, HEAD_DIM:], jnp.ones((tile, HEAD_DIM), BF16)], axis=1
                    )
                    total += jnp.dot(weights.astype(BF16), values, preferred_element_type=F32)
                acc[q] = total

        return carry

    lax.fori_loop(0, count, absorb_block, 0)
    if not last:
        outs = start_all(
            [pltpu.make_async_copy(acc.at[q], out_ref.at[q], acc_sem.at[q]) for q in range(2)]
        )
        for copy in outs:
            copy.wait()
        return

    for copy in added:
        copy.wait()
    norm = jnp.maximum(
        jnp.max(q_scr[0, rows + 8 :, :].astype(F32)), jnp.max(q_scr[1, rows + 8 :, :].astype(F32))
    )

    @pl.when(norm > NORM_LIMIT**2)
    def _():
        peak[...] = jnp.full_like(peak, -1e30)
        weight_sum[...] = jnp.zeros_like(weight_sum)
        acc[...] = jnp.zeros_like(acc)
        sums[...] = jnp.zeros_like(sums)
        near = ((3, False), (3, True), (1, False), (1, True))
        everything = [
            (q_refs[0], (0, False)),
            (q_refs[1], (0, True)),
            *zip(rest, near),
            *zip(kv_refs, places),
        ]
        small = 256
        for block_ref, place in everything:
            pltpu.sync_copy(block_ref, kv_scr.at[0])
            key_start = block_start(*place, rows)
            extra = kv_scr[0, rows : rows + 8, :].astype(F32)
            factor = extra[0:4] + extra[4:8]

            def absorb(at, carry, key_start=key_start, factor=factor):
                q = lax.div(at, rows // small)
                low = pl.multiple_of(lax.rem(at, rows // small) * small, small)
                here = pl.ds(low, small)
                query_start = jnp.where(q == 0, q_starts[0], q_starts[1]) + low
                for cut in range(rows // small):
                    keys = slice(cut * small, (cut + 1) * small)
                    scores = lax.dot_general(
                        q_scr[q, here, :HEAD_DIM], kv_scr[0, keys, :HEAD_DIM], NT, preferred_element_type=F32
                    )
                    key_pos = lax.broadcasted_iota(jnp.int32, scores.shape, 1) + (
                        key_start + cut * small
                    )
                    query_pos = lax.broadcasted_iota(jnp.int32, scores.shape, 0) + query_start
                    allowed = (key_pos < doc_len) & (key_pos != query_pos)
                    scores = jnp.where(allowed, scores * factor[cut : cut + 1], -1e30)
                    old = peak[q, here, :]
                    new = jnp.maximum(old, jnp.max(scores, axis=1, keepdims=True))
                    weights = jnp.where(allowed, jnp.exp2(scores - new[:, :1]), 0.0)
                    rescale = jnp.exp2(old - new)
                    peak[q, here, :] = new
                    weight_sum[q, here, :] = weight_sum[q, here, :] * rescale + jnp.sum(
                        weights, axis=1, keepdims=True
                    )
                    acc[q, here, :HEAD_DIM] = acc[q, here, :HEAD_DIM] * rescale + jnp.dot(
                        weights.astype(BF16), kv_scr[0, keys, HEAD_DIM:], preferred_element_type=F32
                    )
                return carry

            lax.fori_loop(0, 2 * rows // small, absorb, 0)
        for q in range(2):
            acc[q, :, HEAD_DIM:] = weight_sum[q]

    core = own_core()
    for q in range(2):
        total = acc[q] + (sums[0, q] + sums[1, q])
        inside = lax.broadcasted_iota(jnp.int32, (rows, HEAD_DIM), 0) + q_starts[q] < doc_len
        mixed = jnp.where(inside, total[:, :HEAD_DIM] / total[:, HEAD_DIM:], 0.0)
        block = core if q == 0 else 1 - core
        out_ref[:, block] = mixed.astype(BF16).reshape(4, rows // 4, HEAD_DIM)


def attend(doc_length, queries, blocks, places, states, rest, name):
    rows = blocks[0].shape[0] - EXTRA
    count = len(blocks)
    first, last = queries is None, rest is not None
    out_shape = jax.ShapeDtypeStruct((2, rows, 2 * HEAD_DIM), F32)
    scratch = [
        pltpu.VMEM((count, rows + EXTRA, 2 * HEAD_DIM), BF16),
        pltpu.VMEM(out_shape.shape, F32),
        pltpu.SemaphoreType.DMA((count,)),
        pltpu.SemaphoreType.DMA((4,)),
    ]
    args = list(blocks)
    if not first:
        args = [*queries, *blocks]
        scratch.append(pltpu.VMEM((2, rows + EXTRA, 2 * HEAD_DIM), BF16))
    if last:
        args += [*states, *rest]
        scratch += [
            pltpu.VMEM((2, *out_shape.shape), F32),
            pltpu.SemaphoreType.DMA((2,)),
        ]
        out_shape = jax.ShapeDtypeStruct((4, 2, rows // 4, HEAD_DIM), BF16)
        scratch += [
            pltpu.VMEM((2, rows, HEAD_DIM), F32),
            pltpu.VMEM((2, rows, HEAD_DIM), F32),
        ]
    return pl.pallas_call(
        functools.partial(attend_kernel, places, first, last),
        in_specs=[SMEM] + [ANY] * len(args),
        out_specs=HERE if last else ANY,
        out_shape=out_shape,
        scratch_shapes=scratch,
        compiler_params=pltpu.CompilerParams(vmem_limit_bytes=VMEM),
        cost_estimate=pl.CostEstimate(
            flops=16 * rows * rows * count * HEAD_DIM,
            bytes_accessed=4 * 2**20,
            transcendentals=0,
        ),
        name=name,
    )(doc_length, *args)


def output_kernel(ctx_ref, got_ref, w_ref, w_got_ref, out_ref):
    core = own_core()
    lefts = [
        jnp.concatenate([ref[y, core] for y in range(4)], axis=1) for ref in (ctx_ref, got_ref)
    ]
    width = w_ref.shape[2]
    step = width // 8
    for i in range(8):
        cols = slice(i * step, (i + 1) * step)
        part = None
        for left, ref in zip(lefts, (w_ref, w_got_ref)):
            right = ref[:, :, cols].reshape(4 * HEAD_DIM, step)
            term = jnp.dot(left, right, preferred_element_type=F32)
            part = term if part is None else part + term
        out_ref[i] = part.astype(BF16)


def output(context, got, weights, weights_got):
    rows = context.shape[2]
    width = weights.shape[2]
    return pl.pallas_call(
        output_kernel,
        in_specs=[HERE] * 4,
        out_specs=HERE,
        out_shape=jax.ShapeDtypeStruct((8, rows, width // 8), BF16),
        compiler_params=pltpu.CompilerParams(vmem_limit_bytes=30 * 2**20),
        cost_estimate=pl.CostEstimate(
            flops=2 * rows * width * 1024, bytes_accessed=6 * 2**20, transcendentals=0
        ),
        name="output",
    )(context, got, weights, weights_got)


def body(tokens, w_shared, w_value, w_output, doc_length):
    def move(array, by, cross):
        return lax.ppermute(
            array, "seq", [(i, (i // 2 + by) % 4 * 2 + (i % 2 ^ cross)) for i in range(8)]
        )

    own, given = project(tokens, w_shared, w_value)
    peer = move(given, 0, 1)
    own_left, peer_right = move(own, 1, 0), move(given, -1, 1)
    peer_left, own_right = move(given, 1, 1), move(own, -1, 0)

    repeated = spread(w_output, peer)
    peer, repeated = lax.optimization_barrier((peer, repeated))
    queries = (own, peer)
    here = attend(doc_length, None, queries, ((0, False), (0, True)), None, None, "attend_here")
    y_groups = [[0, 1, 2, 3], [4, 5, 6, 7]]
    weights = lax.all_to_all(
        repeated, "head", 0, 0, axis_index_groups=y_groups, tiled=True
    )
    own_left, peer_right, here = lax.optimization_barrier((own_left, peer_right, here))
    own_far, peer_far = move(own_left, 1, 0), move(peer_right, -1, 0)
    blocks = (own_left, peer_left, own_right, peer_right)
    near = attend(
        doc_length,
        queries,
        blocks,
        ((3, False), (3, True), (1, False), (1, True)),
        None,
        None,
        "attend_near",
    )
    context = attend(
        doc_length,
        queries,
        (own_far, peer_far),
        ((2, False), (2, True)),
        (here, near),
        blocks,
        "attend_far",
    )
    weights, context = lax.optimization_barrier((weights, context))
    weights_got = move(weights, 0, 1)
    context = lax.all_to_all(context, "head", 0, 0, axis_index_groups=y_groups, tiled=True)
    terms = output(context, move(context, 0, 1), weights, weights_got)
    terms = lax.all_to_all(terms, "head", 0, 0, tiled=True).astype(F32)
    result = (terms[:4] + terms[4:]).astype(BF16)
    return result.reshape(tokens.shape[0], result.shape[-1])


def solution(mesh):
    placed = (
        P(("batch", "seq"), None),
        P(None, "head"),
        P(None, "head"),
        P("head", None),
        P("batch"),
    )
    return jax.shard_map(
        body, mesh=mesh, in_specs=placed, out_specs=P(("batch", "seq"), "head"), check_vma=False
    )
```

```python
import functools
import math

import jax
import jax.numpy as jnp
from jax import lax
from jax.experimental import pallas as pl
from jax.experimental.pallas import tpu as pltpu
from jax.sharding import PartitionSpec as P

HEAD_DIM = 128
LOG2E = 1.4426950408889634
NORM_LIMIT = 60.0
EXTRA = 16
VMEM = 65280 * 2**10
NT = (((1,), (1,)), ((), ()))
ANY = pl.BlockSpec(memory_space=pl.ANY)
HERE = pl.BlockSpec(memory_space=pltpu.VMEM)
SMEM = pl.BlockSpec(memory_space=pltpu.SMEM)
F32 = jnp.float32
BF16 = jnp.bfloat16


def own_core():
    return lax.rem(lax.axis_index("seq"), 2)


def block_start(by, other, rows):
    seq = lax.axis_index("seq")
    place = lax.rem(lax.div(seq, 2) + by, 4) * 2
    core = lax.rem(seq, 2)
    return (place + (1 - core if other else core)) * rows


def start_all(copies):
    for copy in copies:
        copy.start()
    return copies


def project_kernel(x_ref, ws_ref, wv_ref, own_ref, given_ref, x_scr, w_scr, out_scr, sem, out_sem):
    rows, _ = x_ref.shape
    cuts = x_scr.shape[0]
    step = rows // cuts
    wide = 2 * HEAD_DIM
    weights = start_all(
        [
            pltpu.make_async_copy(ws_ref, w_scr.at[:, pl.ds(0, wide)], sem.at[0]),
            pltpu.make_async_copy(wv_ref, w_scr.at[:, pl.ds(wide, wide)], sem.at[1]),
        ]
    )
    tokens = start_all(
        [
            pltpu.make_async_copy(x_ref.at[pl.ds(i * step, step)], x_scr.at[i], sem.at[2 + i])
            for i in range(cuts)
        ]
    )
    core = own_core()
    outs = []

    def send(low, size):
        here = pl.ds(low, size)
        for h, ref in ((core, own_ref), (1 - core, given_ref)):
            outs.extend(
                start_all(
                    [
                        pltpu.make_async_copy(
                            out_scr.at[h, here], ref.at[here], out_sem.at[len(outs)]
                        )
                    ]
                )
            )

    row = lax.broadcasted_iota(jnp.int32, (EXTRA, wide), 0)
    extra = [jnp.zeros((EXTRA, wide), F32) for _ in range(2)]
    largest = [jnp.zeros((8, wide), F32) for _ in range(2)]
    ones = jnp.ones((8, HEAD_DIM), BF16)
    for copy in weights:
        copy.wait()
    for i in range(cuts):
        tokens[i].wait()
        both = jnp.dot(x_scr[i], w_scr[...], preferred_element_type=F32).astype(BF16)
        here = slice(i * step, (i + 1) * step)
        for h in range(2):
            at = h * HEAD_DIM
            out_scr[h, here, :HEAD_DIM] = both[:, at : at + HEAD_DIM]
            out_scr[h, here, HEAD_DIM:] = both[:, wide + at : wide + at + HEAD_DIM]
        send(i * step, step)
        for h in range(2):
            keys = both[:, h * HEAD_DIM : (h + 1) * HEAD_DIM].astype(F32)
            square = keys * keys
            total = lax.dot_general(ones, square.astype(BF16), NT, preferred_element_type=F32)
            largest[h] = jnp.maximum(largest[h], total)
            factor = lax.rsqrt(total / HEAD_DIM + 1e-06) * (LOG2E / math.sqrt(HEAD_DIM))
            first = factor.astype(BF16).astype(F32)
            extra[h] = jnp.where(row == i, jnp.concatenate([first] * 2), extra[h])
            extra[h] = jnp.where(row == 4 + i, jnp.concatenate([factor - first] * 2), extra[h])
    for h in range(2):
        top = jnp.broadcast_to(jnp.max(largest[h]), (EXTRA, wide))
        out_scr[h, rows:, :] = jnp.where(row >= 8, top, extra[h]).astype(BF16)
    send(rows, EXTRA)
    for copy in outs:
        copy.wait()


def project(tokens, w_shared, w_value):
    rows, width = tokens.shape
    cuts = 4
    out = jax.ShapeDtypeStruct((rows + EXTRA, 2 * HEAD_DIM), BF16)
    return pl.pallas_call(
        project_kernel,
        in_specs=[ANY] * 3,
        out_specs=(ANY, ANY),
        out_shape=(out, out),
        scratch_shapes=[
            pltpu.VMEM((cuts, rows // cuts, width), BF16),
            pltpu.VMEM((width, 4 * HEAD_DIM), BF16),
            pltpu.VMEM((2, rows + EXTRA, 2 * HEAD_DIM), BF16),
            pltpu.SemaphoreType.DMA((2 + cuts,)),
            pltpu.SemaphoreType.DMA((2 * cuts + 2,)),
        ],
        compiler_params=pltpu.CompilerParams(vmem_limit_bytes=VMEM),
        cost_estimate=pl.CostEstimate(
            flops=2 * rows * width * 512, bytes_accessed=7 * 2**20, transcendentals=0
        ),
        name="project",
    )(tokens, w_shared, w_value)


def spread_kernel(w_ref, after_ref, out_ref, scr, sem):
    del after_ref
    mine = w_ref.at[pl.ds(pl.multiple_of(own_core() * HEAD_DIM, HEAD_DIM), HEAD_DIM)]
    pltpu.sync_copy(mine, scr)
    for copy in start_all(
        [pltpu.make_async_copy(scr, out_ref.at[i], sem.at[i]) for i in range(4)]
    ):
        copy.wait()


def spread(w_output, after):
    piece = (HEAD_DIM, w_output.shape[1])
    return pl.pallas_call(
        spread_kernel,
        in_specs=[ANY] * 2,
        out_specs=ANY,
        out_shape=jax.ShapeDtypeStruct((4, *piece), BF16),
        scratch_shapes=[pltpu.VMEM(piece, BF16), pltpu.SemaphoreType.DMA((4,))],
        compiler_params=pltpu.CompilerParams(vmem_limit_bytes=VMEM),
        name="spread",
    )(w_output, after)


def attend_kernel(places, first, last, doc_ref, *refs):
    count = len(places)
    if first:
        kv_refs, refs = refs[:count], refs[count:]
        out_ref, kv_scr, acc, sem, acc_sem = refs
        copies = []
    else:
        q_refs, kv_refs, refs = refs[:2], refs[2 : 2 + count], refs[2 + count :]
        if last:
            states, rest, refs = refs[:3], refs[3:7], refs[7:]
            out_ref, kv_scr, acc, sem, acc_sem, q_scr, sums, sums_sem, peak, weight_sum = refs
        else:
            out_ref, kv_scr, acc, sem, acc_sem, q_scr = refs
        copies = start_all(
            [
                pltpu.make_async_copy(q_refs[q], q_scr.at[q], acc_sem.at[2 + q])
                for q in range(2)
            ]
        )
    rows = kv_scr.shape[1] - EXTRA
    tile = 512
    blocks = start_all(
        [pltpu.make_async_copy(kv_refs[i], kv_scr.at[i], sem.at[i]) for i in range(count)]
    )
    if last:
        added = start_all(
            [pltpu.make_async_copy(states[i], sums.at[i], sums_sem.at[i]) for i in range(3)]
        )
    acc[...] = jnp.zeros_like(acc)
    for copy in copies:
        copy.wait()
    doc_len = doc_ref[0]
    q_starts = [block_start(0, other, rows) for other in (False, True)]
    active = jnp.minimum(q_starts[0], q_starts[1]) < doc_len
    starts = [block_start(*place, rows) for place in places]
    q_all = kv_scr if first else q_scr
    for copy in blocks if first else blocks[:1]:
        copy.wait()

    def absorb_block(i, carry):
        start = starts[0]
        for j in range(1, count):
            start = jnp.where(i == j, starts[j], start)
        if not first:

            @pl.when(i > 0)
            def _():
                pltpu.make_async_copy(kv_refs[0], kv_scr.at[i], sem.at[i]).wait()

        @pl.when(active & (start < doc_len))
        def _():
            extra = kv_scr[i, rows : rows + 8, :].astype(F32)
            factor = extra[0:4] + extra[4:8]
            for q in range(2):
                queries = q_all[q, :rows, :HEAD_DIM]
                total = acc[q]
                for cut in range(rows // tile):
                    keys = slice(cut * tile, (cut + 1) * tile)
                    each = tile // 256
                    scale = jnp.concatenate(
                        [factor[cut * each + j : cut * each + j + 1] for j in range(each)], axis=1
                    )
                    place = lax.broadcasted_iota(jnp.int32, (1, tile), 1) + (start + cut * tile)
                    bias = jnp.where(place < doc_len, 0.0, -1e30)
                    scores = lax.dot_general(
                        queries, kv_scr[i, keys, :HEAD_DIM], NT, preferred_element_type=F32
                    )
                    weights = jnp.exp2(scores * scale + bias)
                    if first:
                        apart = jnp.where(i == q, cut * tile, 4 * rows)
                        weights = jnp.where(
                            lax.broadcasted_iota(jnp.int32, weights.shape, 0)
                            == lax.broadcasted_iota(jnp.int32, weights.shape, 1) + apart,
                            0.0,
                            weights,
                        )
                    values = jnp.concatenate(
                        [kv_scr[i, keys, HEAD_DIM:], jnp.ones((tile, HEAD_DIM), BF16)], axis=1
                    )
                    total += jnp.dot(weights.astype(BF16), values, preferred_element_type=F32)
                acc[q] = total

        return carry

    lax.fori_loop(0, count, absorb_block, 0)
    if not last:
        outs = start_all(
            [pltpu.make_async_copy(acc.at[q], out_ref.at[q], acc_sem.at[q]) for q in range(2)]
        )
        for copy in outs:
            copy.wait()
        return

    for copy in added:
        copy.wait()
    norm = jnp.maximum(
        jnp.max(q_scr[0, rows + 8 :, :].astype(F32)), jnp.max(q_scr[1, rows + 8 :, :].astype(F32))
    )

    @pl.when(norm > NORM_LIMIT**2)
    def _():
        peak[...] = jnp.full_like(peak, -1e30)
        weight_sum[...] = jnp.zeros_like(weight_sum)
        acc[...] = jnp.zeros_like(acc)
        sums[...] = jnp.zeros_like(sums)
        near = ((3, False), (3, True), (1, False), (1, True))
        everything = [
            (q_refs[0], (0, False)),
            (q_refs[1], (0, True)),
            *zip(rest, near),
            *zip(kv_refs, places),
        ]
        small = 256
        for block_ref, place in everything:
            pltpu.sync_copy(block_ref, kv_scr.at[0])
            key_start = block_start(*place, rows)
            extra = kv_scr[0, rows : rows + 8, :].astype(F32)
            factor = extra[0:4] + extra[4:8]

            def absorb(at, carry, key_start=key_start, factor=factor):
                q = lax.div(at, rows // small)
                low = pl.multiple_of(lax.rem(at, rows // small) * small, small)
                here = pl.ds(low, small)
                query_start = jnp.where(q == 0, q_starts[0], q_starts[1]) + low
                for cut in range(rows // small):
                    keys = slice(cut * small, (cut + 1) * small)
                    scores = lax.dot_general(
                        q_scr[q, here, :HEAD_DIM], kv_scr[0, keys, :HEAD_DIM], NT, preferred_element_type=F32
                    )
                    key_pos = lax.broadcasted_iota(jnp.int32, scores.shape, 1) + (
                        key_start + cut * small
                    )
                    query_pos = lax.broadcasted_iota(jnp.int32, scores.shape, 0) + query_start
                    allowed = (key_pos < doc_len) & (key_pos != query_pos)
                    scores = jnp.where(allowed, scores * factor[cut : cut + 1], -1e30)
                    old = peak[q, here, :]
                    new = jnp.maximum(old, jnp.max(scores, axis=1, keepdims=True))
                    weights = jnp.where(allowed, jnp.exp2(scores - new[:, :1]), 0.0)
                    rescale = jnp.exp2(old - new)
                    peak[q, here, :] = new
                    weight_sum[q, here, :] = weight_sum[q, here, :] * rescale + jnp.sum(
                        weights, axis=1, keepdims=True
                    )
                    acc[q, here, :HEAD_DIM] = acc[q, here, :HEAD_DIM] * rescale + jnp.dot(
                        weights.astype(BF16), kv_scr[0, keys, HEAD_DIM:], preferred_element_type=F32
                    )
                return carry

            lax.fori_loop(0, 2 * rows // small, absorb, 0)
        for q in range(2):
            acc[q, :, HEAD_DIM:] = weight_sum[q]

    core = own_core()
    for q in range(2):
        total = (acc[q] + sums[0, q]) + (sums[1, q] + sums[2, q])
        inside = lax.broadcasted_iota(jnp.int32, (rows, HEAD_DIM), 0) + q_starts[q] < doc_len
        mixed = jnp.where(inside, total[:, :HEAD_DIM] / total[:, HEAD_DIM:], 0.0)
        block = core if q == 0 else 1 - core
        out_ref[:, block] = mixed.astype(BF16).reshape(4, rows // 4, HEAD_DIM)


def attend(doc_length, queries, blocks, places, states, rest, name):
    rows = blocks[0].shape[0] - EXTRA
    count = len(blocks)
    first, last = queries is None, rest is not None
    out_shape = jax.ShapeDtypeStruct((2, rows, 2 * HEAD_DIM), F32)
    scratch = [
        pltpu.VMEM((count, rows + EXTRA, 2 * HEAD_DIM), BF16),
        pltpu.VMEM(out_shape.shape, F32),
        pltpu.SemaphoreType.DMA((count,)),
        pltpu.SemaphoreType.DMA((4,)),
    ]
    args = list(blocks)
    if not first:
        args = [*queries, *blocks]
        scratch.append(pltpu.VMEM((2, rows + EXTRA, 2 * HEAD_DIM), BF16))
    if last:
        args += [*states, *rest]
        scratch += [
            pltpu.VMEM((3, *out_shape.shape), F32),
            pltpu.SemaphoreType.DMA((3,)),
        ]
        out_shape = jax.ShapeDtypeStruct((4, 2, rows // 4, HEAD_DIM), BF16)
        scratch += [
            pltpu.VMEM((2, rows, HEAD_DIM), F32),
            pltpu.VMEM((2, rows, HEAD_DIM), F32),
        ]
    return pl.pallas_call(
        functools.partial(attend_kernel, places, first, last),
        in_specs=[SMEM] + [ANY] * len(args),
        out_specs=HERE if last else ANY,
        out_shape=out_shape,
        scratch_shapes=scratch,
        compiler_params=pltpu.CompilerParams(vmem_limit_bytes=VMEM),
        cost_estimate=pl.CostEstimate(
            flops=16 * rows * rows * count * HEAD_DIM,
            bytes_accessed=4 * 2**20,
            transcendentals=0,
        ),
        name=name,
    )(doc_length, *args)


def output_kernel(ctx_ref, got_ref, w_ref, w_got_ref, out_ref):
    core = own_core()
    lefts = [
        jnp.concatenate([ref[y, core] for y in range(4)], axis=1) for ref in (ctx_ref, got_ref)
    ]
    width = w_ref.shape[2]
    step = width // 8
    for i in range(8):
        cols = slice(i * step, (i + 1) * step)
        part = None
        for left, ref in zip(lefts, (w_ref, w_got_ref)):
            right = ref[:, :, cols].reshape(4 * HEAD_DIM, step)
            term = jnp.dot(left, right, preferred_element_type=F32)
            part = term if part is None else part + term
        out_ref[i] = part.astype(BF16)


def output(context, got, weights, weights_got):
    rows = context.shape[2]
    width = weights.shape[2]
    return pl.pallas_call(
        output_kernel,
        in_specs=[HERE] * 4,
        out_specs=HERE,
        out_shape=jax.ShapeDtypeStruct((8, rows, width // 8), BF16),
        compiler_params=pltpu.CompilerParams(vmem_limit_bytes=30 * 2**20),
        cost_estimate=pl.CostEstimate(
            flops=2 * rows * width * 1024, bytes_accessed=6 * 2**20, transcendentals=0
        ),
        name="output",
    )(context, got, weights, weights_got)


def body(tokens, w_shared, w_value, w_output, doc_length):
    def move(array, by, cross):
        return lax.ppermute(
            array, "seq", [(i, (i // 2 + by) % 4 * 2 + (i % 2 ^ cross)) for i in range(8)]
        )

    own, given = project(tokens, w_shared, w_value)
    peer = move(given, 0, 1)
    own_left, peer_right = move(own, 1, 0), move(given, -1, 1)
    peer_left, own_right = move(given, 1, 1), move(own, -1, 0)

    repeated = spread(w_output, peer)
    peer, repeated = lax.optimization_barrier((peer, repeated))
    queries = (own, peer)
    here = attend(doc_length, None, queries, ((0, False), (0, True)), None, None, "attend_here")
    y_groups = [[0, 1, 2, 3], [4, 5, 6, 7]]
    weights = lax.all_to_all(
        repeated, "head", 0, 0, axis_index_groups=y_groups, tiled=True
    )
    own_left, peer_right, here = lax.optimization_barrier((own_left, peer_right, here))
    own_far, peer_far = move(own_left, 1, 0), move(peer_right, -1, 0)
    near = attend(
        doc_length,
        queries,
        (own_left, peer_right),
        ((3, False), (1, True)),
        None,
        None,
        "attend_near",
    )
    peer_left, own_right, near = lax.optimization_barrier((peer_left, own_right, near))
    next_near = attend(
        doc_length,
        queries,
        (peer_left, own_right),
        ((3, True), (1, False)),
        None,
        None,
        "attend_next",
    )
    blocks = (own_left, peer_left, own_right, peer_right)
    context = attend(
        doc_length,
        queries,
        (own_far, peer_far),
        ((2, False), (2, True)),
        (here, near, next_near),
        blocks,
        "attend_far",
    )
    weights, context = lax.optimization_barrier((weights, context))
    weights_got = move(weights, 0, 1)
    context = lax.all_to_all(context, "head", 0, 0, axis_index_groups=y_groups, tiled=True)
    terms = output(context, move(context, 0, 1), weights, weights_got)
    terms = lax.all_to_all(terms, "head", 0, 0, tiled=True).astype(F32)
    result = (terms[:4] + terms[4:]).astype(BF16)
    return result.reshape(tokens.shape[0], result.shape[-1])


def solution(mesh):
    placed = (
        P(("batch", "seq"), None),
        P(None, "head"),
        P(None, "head"),
        P("head", None),
        P("batch"),
    )
    return jax.shard_map(
        body, mesh=mesh, in_specs=placed, out_specs=P(("batch", "seq"), "head"), check_vma=False
    )
```

```python
import functools
import math

import jax
import jax.numpy as jnp
from jax import lax
from jax.experimental import pallas as pl
from jax.experimental.pallas import tpu as pltpu
from jax.sharding import PartitionSpec as P

HEAD_DIM = 128
LOG2E = 1.4426950408889634
NORM_LIMIT = 60.0
EXTRA = 16
VMEM = 65280 * 2**10
NT = (((1,), (1,)), ((), ()))
ANY = pl.BlockSpec(memory_space=pl.ANY)
HERE = pl.BlockSpec(memory_space=pltpu.VMEM)
SMEM = pl.BlockSpec(memory_space=pltpu.SMEM)
F32 = jnp.float32
BF16 = jnp.bfloat16


def own_core():
    return lax.rem(lax.axis_index("seq"), 2)


def block_start(by, other, rows):
    seq = lax.axis_index("seq")
    place = lax.rem(lax.div(seq, 2) + by, 4) * 2
    core = lax.rem(seq, 2)
    return (place + (1 - core if other else core)) * rows


def start_all(copies):
    for copy in copies:
        copy.start()
    return copies


def project_kernel(x_ref, ws_ref, wv_ref, own_ref, given_ref, x_scr, w_scr, out_scr, sem, out_sem):
    rows, _ = x_ref.shape
    cuts = x_scr.shape[0]
    step = rows // cuts
    wide = 2 * HEAD_DIM
    weights = start_all(
        [
            pltpu.make_async_copy(ws_ref, w_scr.at[:, pl.ds(0, wide)], sem.at[0]),
            pltpu.make_async_copy(wv_ref, w_scr.at[:, pl.ds(wide, wide)], sem.at[1]),
        ]
    )
    tokens = start_all(
        [
            pltpu.make_async_copy(x_ref.at[pl.ds(i * step, step)], x_scr.at[i], sem.at[2 + i])
            for i in range(cuts)
        ]
    )
    core = own_core()
    outs = []

    def send(low, size):
        here = pl.ds(low, size)
        for h, ref in ((core, own_ref), (1 - core, given_ref)):
            outs.extend(
                start_all(
                    [
                        pltpu.make_async_copy(
                            out_scr.at[h, here], ref.at[here], out_sem.at[len(outs)]
                        )
                    ]
                )
            )

    row = lax.broadcasted_iota(jnp.int32, (EXTRA, wide), 0)
    extra = [jnp.zeros((EXTRA, wide), F32) for _ in range(2)]
    largest = [jnp.zeros((8, wide), F32) for _ in range(2)]
    ones = jnp.ones((8, HEAD_DIM), BF16)
    for copy in weights:
        copy.wait()
    for i in range(cuts):
        tokens[i].wait()
        both = jnp.dot(x_scr[i], w_scr[...], preferred_element_type=F32).astype(BF16)
        here = slice(i * step, (i + 1) * step)
        for h in range(2):
            at = h * HEAD_DIM
            out_scr[h, here, :HEAD_DIM] = both[:, at : at + HEAD_DIM]
            out_scr[h, here, HEAD_DIM:] = both[:, wide + at : wide + at + HEAD_DIM]
        send(i * step, step)
        for h in range(2):
            keys = both[:, h * HEAD_DIM : (h + 1) * HEAD_DIM].astype(F32)
            square = keys * keys
            total = lax.dot_general(ones, square.astype(BF16), NT, preferred_element_type=F32)
            largest[h] = jnp.maximum(largest[h], total)
            factor = lax.rsqrt(total / HEAD_DIM + 1e-06) * (LOG2E / math.sqrt(HEAD_DIM))
            first = factor.astype(BF16).astype(F32)
            extra[h] = jnp.where(row == i, jnp.concatenate([first] * 2), extra[h])
            extra[h] = jnp.where(row == 4 + i, jnp.concatenate([factor - first] * 2), extra[h])
    for h in range(2):
        top = jnp.broadcast_to(jnp.max(largest[h]), (EXTRA, wide))
        out_scr[h, rows:, :] = jnp.where(row >= 8, top, extra[h]).astype(BF16)
    send(rows, EXTRA)
    for copy in outs:
        copy.wait()


def project(tokens, w_shared, w_value):
    rows, width = tokens.shape
    cuts = 4
    out = jax.ShapeDtypeStruct((rows + EXTRA, 2 * HEAD_DIM), BF16)
    return pl.pallas_call(
        project_kernel,
        in_specs=[ANY] * 3,
        out_specs=(ANY, ANY),
        out_shape=(out, out),
        scratch_shapes=[
            pltpu.VMEM((cuts, rows // cuts, width), BF16),
            pltpu.VMEM((width, 4 * HEAD_DIM), BF16),
            pltpu.VMEM((2, rows + EXTRA, 2 * HEAD_DIM), BF16),
            pltpu.SemaphoreType.DMA((2 + cuts,)),
            pltpu.SemaphoreType.DMA((2 * cuts + 2,)),
        ],
        compiler_params=pltpu.CompilerParams(vmem_limit_bytes=VMEM),
        cost_estimate=pl.CostEstimate(
            flops=2 * rows * width * 512, bytes_accessed=7 * 2**20, transcendentals=0
        ),
        name="project",
    )(tokens, w_shared, w_value)


def spread_kernel(w_ref, after_ref, out_ref, scr, sem):
    del after_ref
    mine = w_ref.at[pl.ds(pl.multiple_of(own_core() * HEAD_DIM, HEAD_DIM), HEAD_DIM)]
    pltpu.sync_copy(mine, scr)
    for copy in start_all(
        [pltpu.make_async_copy(scr, out_ref.at[i], sem.at[i]) for i in range(4)]
    ):
        copy.wait()


def spread(w_output, after):
    piece = (HEAD_DIM, w_output.shape[1])
    return pl.pallas_call(
        spread_kernel,
        in_specs=[ANY] * 2,
        out_specs=ANY,
        out_shape=jax.ShapeDtypeStruct((4, *piece), BF16),
        scratch_shapes=[pltpu.VMEM(piece, BF16), pltpu.SemaphoreType.DMA((4,))],
        compiler_params=pltpu.CompilerParams(vmem_limit_bytes=VMEM),
        name="spread",
    )(w_output, after)


def attend_kernel(places, first, last, doc_ref, *refs):
    count = len(places)
    if first:
        kv_refs, refs = refs[:count], refs[count:]
        out_ref, kv_scr, acc, sem, acc_sem = refs
        copies = []
    else:
        q_refs, kv_refs, refs = refs[:2], refs[2 : 2 + count], refs[2 + count :]
        if last:
            states, rest, refs = refs[:2], refs[2:6], refs[6:]
            out_ref, kv_scr, acc, sem, acc_sem, q_scr, sums, sums_sem, peak, weight_sum = refs
        else:
            out_ref, kv_scr, acc, sem, acc_sem, q_scr = refs
        copies = start_all(
            [
                pltpu.make_async_copy(q_refs[q], q_scr.at[q], acc_sem.at[2 + q])
                for q in range(2)
            ]
        )
    rows = kv_scr.shape[1] - EXTRA
    tile = 512
    blocks = start_all(
        [pltpu.make_async_copy(kv_refs[i], kv_scr.at[i], sem.at[i]) for i in range(count)]
    )
    if last:
        added = start_all(
            [pltpu.make_async_copy(states[i], sums.at[i], sums_sem.at[i]) for i in range(2)]
        )
    acc[...] = jnp.zeros_like(acc)
    for copy in copies:
        copy.wait()
    doc_len = doc_ref[0]
    q_starts = [block_start(0, other, rows) for other in (False, True)]
    active = jnp.minimum(q_starts[0], q_starts[1]) < doc_len
    starts = [block_start(*place, rows) for place in places]
    q_all = kv_scr if first else q_scr
    for copy in blocks if first else blocks[:1]:
        copy.wait()

    def absorb_block(i, carry):
        start = starts[0]
        for j in range(1, count):
            start = jnp.where(i == j, starts[j], start)
        if not first:

            @pl.when(i > 0)
            def _():
                pltpu.make_async_copy(kv_refs[0], kv_scr.at[i], sem.at[i]).wait()

        @pl.when(active & (start < doc_len))
        def _():
            extra = kv_scr[i, rows : rows + 8, :].astype(F32)
            factor = extra[0:4] + extra[4:8]
            for q in range(2):
                queries = q_all[q, :rows, :HEAD_DIM]
                total = acc[q]
                for cut in range(rows // tile):
                    keys = slice(cut * tile, (cut + 1) * tile)
                    each = tile // 256
                    scale = jnp.concatenate(
                        [factor[cut * each + j : cut * each + j + 1] for j in range(each)], axis=1
                    )
                    place = lax.broadcasted_iota(jnp.int32, (1, tile), 1) + (start + cut * tile)
                    bias = jnp.where(place < doc_len, 0.0, -1e30)
                    scores = lax.dot_general(
                        queries, kv_scr[i, keys, :HEAD_DIM], NT, preferred_element_type=F32
                    )
                    weights = jnp.exp2(scores * scale + bias)
                    if first:
                        apart = jnp.where(i == q, cut * tile, 4 * rows)
                        weights = jnp.where(
                            lax.broadcasted_iota(jnp.int32, weights.shape, 0)
                            == lax.broadcasted_iota(jnp.int32, weights.shape, 1) + apart,
                            0.0,
                            weights,
                        )
                    values = jnp.concatenate(
                        [kv_scr[i, keys, HEAD_DIM:], jnp.ones((tile, HEAD_DIM), BF16)], axis=1
                    )
                    total += jnp.dot(weights.astype(BF16), values, preferred_element_type=F32)
                acc[q] = total

        return carry

    lax.fori_loop(0, count, absorb_block, 0)
    if not last:
        outs = start_all(
            [pltpu.make_async_copy(acc.at[q], out_ref.at[q], acc_sem.at[q]) for q in range(2)]
        )
        for copy in outs:
            copy.wait()
        return

    for copy in added:
        copy.wait()
    norm = jnp.maximum(
        jnp.max(q_scr[0, rows + 8 :, :].astype(F32)), jnp.max(q_scr[1, rows + 8 :, :].astype(F32))
    )

    @pl.when(norm > NORM_LIMIT**2)
    def _():
        peak[...] = jnp.full_like(peak, -1e30)
        weight_sum[...] = jnp.zeros_like(weight_sum)
        acc[...] = jnp.zeros_like(acc)
        sums[...] = jnp.zeros_like(sums)
        near = ((3, False), (3, True), (1, False), (1, True))
        everything = [
            (q_refs[0], (0, False)),
            (q_refs[1], (0, True)),
            *zip(rest, near),
            *zip(kv_refs, places),
        ]
        small = 256
        for block_ref, place in everything:
            pltpu.sync_copy(block_ref, kv_scr.at[0])
            key_start = block_start(*place, rows)
            extra = kv_scr[0, rows : rows + 8, :].astype(F32)
            factor = extra[0:4] + extra[4:8]

            def absorb(at, carry, key_start=key_start, factor=factor):
                q = lax.div(at, rows // small)
                low = pl.multiple_of(lax.rem(at, rows // small) * small, small)
                here = pl.ds(low, small)
                query_start = jnp.where(q == 0, q_starts[0], q_starts[1]) + low
                for cut in range(rows // small):
                    keys = slice(cut * small, (cut + 1) * small)
                    scores = lax.dot_general(
                        q_scr[q, here, :HEAD_DIM], kv_scr[0, keys, :HEAD_DIM], NT, preferred_element_type=F32
                    )
                    key_pos = lax.broadcasted_iota(jnp.int32, scores.shape, 1) + (
                        key_start + cut * small
                    )
                    query_pos = lax.broadcasted_iota(jnp.int32, scores.shape, 0) + query_start
                    allowed = (key_pos < doc_len) & (key_pos != query_pos)
                    scores = jnp.where(allowed, scores * factor[cut : cut + 1], -1e30)
                    old = peak[q, here, :]
                    new = jnp.maximum(old, jnp.max(scores, axis=1, keepdims=True))
                    weights = jnp.where(allowed, jnp.exp2(scores - new[:, :1]), 0.0)
                    rescale = jnp.exp2(old - new)
                    peak[q, here, :] = new
                    weight_sum[q, here, :] = weight_sum[q, here, :] * rescale + jnp.sum(
                        weights, axis=1, keepdims=True
                    )
                    acc[q, here, :HEAD_DIM] = acc[q, here, :HEAD_DIM] * rescale + jnp.dot(
                        weights.astype(BF16), kv_scr[0, keys, HEAD_DIM:], preferred_element_type=F32
                    )
                return carry

            lax.fori_loop(0, 2 * rows // small, absorb, 0)
        for q in range(2):
            acc[q, :, HEAD_DIM:] = weight_sum[q]

    core = own_core()
    for q in range(2):
        total = acc[q] + (sums[0, q] + sums[1, q])
        inside = lax.broadcasted_iota(jnp.int32, (rows, HEAD_DIM), 0) + q_starts[q] < doc_len
        mixed = jnp.where(inside, total[:, :HEAD_DIM] / total[:, HEAD_DIM:], 0.0)
        block = core if q == 0 else 1 - core
        out_ref[:, block] = mixed.astype(BF16).reshape(4, rows // 4, HEAD_DIM)


def attend(doc_length, queries, blocks, places, states, rest, name):
    rows = blocks[0].shape[0] - EXTRA
    count = len(blocks)
    first, last = queries is None, rest is not None
    out_shape = jax.ShapeDtypeStruct((2, rows, 2 * HEAD_DIM), F32)
    scratch = [
        pltpu.VMEM((count, rows + EXTRA, 2 * HEAD_DIM), BF16),
        pltpu.VMEM(out_shape.shape, F32),
        pltpu.SemaphoreType.DMA((count,)),
        pltpu.SemaphoreType.DMA((4,)),
    ]
    args = list(blocks)
    if not first:
        args = [*queries, *blocks]
        scratch.append(pltpu.VMEM((2, rows + EXTRA, 2 * HEAD_DIM), BF16))
    if last:
        args += [*states, *rest]
        scratch += [
            pltpu.VMEM((2, *out_shape.shape), F32),
            pltpu.SemaphoreType.DMA((2,)),
        ]
        out_shape = jax.ShapeDtypeStruct((4, 2, rows // 4, HEAD_DIM), BF16)
        scratch += [
            pltpu.VMEM((2, rows, HEAD_DIM), F32),
            pltpu.VMEM((2, rows, HEAD_DIM), F32),
        ]
    return pl.pallas_call(
        functools.partial(attend_kernel, places, first, last),
        in_specs=[SMEM] + [ANY] * len(args),
        out_specs=HERE if last else ANY,
        out_shape=out_shape,
        scratch_shapes=scratch,
        compiler_params=pltpu.CompilerParams(vmem_limit_bytes=VMEM),
        cost_estimate=pl.CostEstimate(
            flops=16 * rows * rows * count * HEAD_DIM,
            bytes_accessed=4 * 2**20,
            transcendentals=0,
        ),
        name=name,
    )(doc_length, *args)


def output_kernel(ctx_ref, got_ref, w_ref, w_got_ref, out_ref):
    core = own_core()
    lefts = [
        jnp.concatenate([ref[y, core] for y in range(4)], axis=1) for ref in (ctx_ref, got_ref)
    ]
    width = w_ref.shape[2]
    step = width // 8
    for i in range(8):
        cols = slice(i * step, (i + 1) * step)
        part = None
        for left, ref in zip(lefts, (w_ref, w_got_ref)):
            right = ref[:, :, cols].reshape(4 * HEAD_DIM, step)
            term = jnp.dot(left, right, preferred_element_type=F32)
            part = term if part is None else part + term
        out_ref[i] = part.astype(BF16)


def output(context, got, weights, weights_got):
    rows = context.shape[2]
    width = weights.shape[2]
    return pl.pallas_call(
        output_kernel,
        in_specs=[HERE] * 4,
        out_specs=HERE,
        out_shape=jax.ShapeDtypeStruct((8, rows, width // 8), BF16),
        compiler_params=pltpu.CompilerParams(vmem_limit_bytes=30 * 2**20),
        cost_estimate=pl.CostEstimate(
            flops=2 * rows * width * 1024, bytes_accessed=6 * 2**20, transcendentals=0
        ),
        name="output",
    )(context, got, weights, weights_got)


def body(tokens, w_shared, w_value, w_output, doc_length):
    def move(array, by, cross):
        return lax.ppermute(
            array, "seq", [(i, (i // 2 + by) % 4 * 2 + (i % 2 ^ cross)) for i in range(8)]
        )

    own, given = project(tokens, w_shared, w_value)
    peer = move(given, 0, 1)
    own_left, peer_right = move(own, 1, 0), move(given, -1, 1)
    peer_left, own_right = move(given, 1, 1), move(own, -1, 0)

    repeated = spread(w_output, peer)
    peer, repeated = lax.optimization_barrier((peer, repeated))
    queries = (own, peer)
    here = attend(doc_length, None, queries, ((0, False), (0, True)), None, None, "attend_here")
    y_groups = [[0, 1, 2, 3], [4, 5, 6, 7]]
    weights = lax.all_to_all(
        repeated, "head", 0, 0, axis_index_groups=y_groups, tiled=True
    )
    own_left, peer_right, here = lax.optimization_barrier((own_left, peer_right, here))
    own_far, peer_far = move(own_left, 1, 0), move(peer_right, -1, 0)
    blocks = (own_left, peer_left, own_right, peer_right)
    near = attend(
        doc_length,
        queries,
        blocks,
        ((3, False), (3, True), (1, False), (1, True)),
        None,
        None,
        "attend_near",
    )
    context = attend(
        doc_length,
        queries,
        (own_far, peer_far),
        ((2, False), (2, True)),
        (here, near),
        blocks,
        "attend_far",
    )
    weights, context = lax.optimization_barrier((weights, context))
    weights_got = move(weights, 0, 1)
    context = lax.all_to_all(context, "head", 0, 0, axis_index_groups=y_groups, tiled=True)
    terms = output(context, move(context, 0, 1), weights, weights_got)
    terms = lax.all_to_all(terms, "head", 0, 0, tiled=True)
    result = (terms[:4].astype(F32) + terms[4:].astype(F32)).astype(BF16)
    return result.reshape(tokens.shape[0], result.shape[-1])


def solution(mesh):
    placed = (
        P(("batch", "seq"), None),
        P(None, "head"),
        P(None, "head"),
        P("head", None),
        P("batch"),
    )
    return jax.shard_map(
        body, mesh=mesh, in_specs=placed, out_specs=P(("batch", "seq"), "head"), check_vma=False
    )
```
